32 devices in a mesh: groups: 2 (over y), tile: 4 (over x, core), head: 4 (over z).
Axes of the slice: x: 2, y: 2, z: 4, core: 2. Of those that a mesh axis runs over, the one named last changes fastest.
Arguments:
- features: bfloat16 [24, 192, 7680], P('groups', 'tile'), parts along dimension 0, may hold values from -6 to 6
- proj_weight: bfloat16 [7680, 8192], P('tile', 'head'), may hold values from -0.0625 to 0.0625
- proj_bias: bfloat16 [8192], P('head'), may hold values from -3 to 3
- kv_weight: bfloat16 [8192, 2048], P('tile', 'head'), may hold values from -0.0625 to 0.0625
- key_gain: float32 [1, 128], replicated, may hold values from 0.1 to 1.9
- tile_map: int32 [8, 4], P('groups'), parts along dimension 0, may hold values from 0 to 11, as said below
- tile_count: int32 [8], P('groups'), parts along dimension 0, may hold values from 1 to 4, as said below
- decode_owner: int32 [8], P('groups'), parts along dimension 0, may hold values from 0 to 15, as said below
Outputs:
- cache: bfloat16 [8, 4, 768, 4, 128], P(('groups', 'tile'), 'head'), parts along dimension 0
The draws below stay inside these ranges and needn't reach their ends.
There are 2 independent parts, one for each index of `groups`. The reference program is written for one: setup_inputs(seed, part) draws one part's arguments, and reference() takes and returns one part's arrays. A program takes and returns all parts, laid end to end along the dimension named above; an argument that names none is the same for every part. Nothing has to cross between parts.
Inputs may be any that keep to these rules, and one draw needn't show every extreme that they name: For each request r the entries tile_map[r, j] with j < tile_count[r] are its packed tiles in order, and every packed tile appears exactly once among all such entries; entries with j >= tile_count[r] repeat entry 0. `tile_count`: the counts sum to 12. The tile indices decode_owner[r] // 4 are distinct over the requests.
All inputs are finite; a program needn't handle non-finite values.
Results may differ from the reference program's by a relative error of at most 0.0049.
Values may be sent and summed in bfloat16 or wider, within the bound.
No kernel may reach another device: no remote copies, remote signals or barrier semaphores. Data moves between devices by JAX's collectives and lax.ppermute only.
A program may use at most 128 MiB of HBM per device.

```python
import jax
import jax.numpy as jnp
from jax import lax

D = 8192
VIS = 7680
KVH = 8
HD = 128
LAYERS = 1
MAXT = 4
TOK_TILE = 192
REQUESTS = 4
TILES = 12
HEAD_GROUPS = 4


def tile_layout(key, part):
    first, second, third = jax.random.split(jax.random.fold_in(key, 101), 3)
    pick_full, pick_single = jax.random.split(second)
    slot_owner = jnp.arange(3 * REQUESTS) // 3
    within = jnp.arange(3 * REQUESTS) % 3
    scores = jax.random.permutation(first, 3 * REQUESTS)
    full_request = jax.random.randint(pick_full, (), 0, REQUESTS)
    single_request = (full_request + 1 + jax.random.randint(pick_single, (), 0, REQUESTS - 1)) % REQUESTS
    scores = jnp.where(slot_owner == full_request, -1 - within, scores)
    scores = jnp.where(slot_owner == single_request, 3 * REQUESTS + within, scores)
    ordering = jnp.argsort(scores)
    chosen = slot_owner[ordering[:2 * REQUESTS]]
    counts = 1 + jnp.sum((chosen[:, None] == jnp.arange(REQUESTS)[None, :]).astype(jnp.int32), axis=0)
    starts = jnp.cumsum(counts) - counts
    packing = jax.random.permutation(third, TILES)
    column = jnp.arange(MAXT)[None, :]
    places = starts[:, None] + jnp.where(column < counts[:, None], column, 0)
    return (packing[places].astype(jnp.int32), counts.astype(jnp.int32))


def draw_tile_map(key, part):
    table, counts = tile_layout(key, part)
    return table


def draw_tile_count(key, part):
    table, counts = tile_layout(key, part)
    return counts


def draw_decode_owner(key, part):
    key = jax.random.fold_in(key, 7)
    first, second = jax.random.split(key)
    tile_order = jax.random.permutation(first, REQUESTS)
    turns = jax.random.randint(second, (REQUESTS,), 0, HEAD_GROUPS)
    turns = jnp.where(tile_order == 0, 0, turns)
    turns = jnp.where(tile_order == REQUESTS - 1, HEAD_GROUPS - 1, turns)
    return (tile_order * HEAD_GROUPS + turns).astype(jnp.int32)


def levels(stream_key, dims, cuts, least, largest):
    gain, own = 1.0, jax.random.fold_in(stream_key, 6)
    for dim, parts in cuts:
        draws = jnp.exp(jax.random.uniform(jax.random.fold_in(own, dim), (parts,), jnp.float32, least / len(cuts), largest / len(cuts)))
        gain = gain * jnp.repeat(draws, dims[dim] // parts).reshape([-1 if axis == dim else 1 for axis in range(len(dims))])
    return gain


def gaussian(stream_key, dims, deviation, bound, cuts=(), held_as=jnp.bfloat16):
    values = jax.random.normal(stream_key, dims, jnp.float32) * deviation
    if len(cuts) > 0:
        values = levels(stream_key, dims, cuts, -0.22, 0.18) * values
    return jnp.clip(values, min=-bound, max=bound).astype(held_as)


def setup_inputs(seed: int = 0, part: int = 0) -> dict:
    seeds = jax.random.split(jax.random.key(seed), 9)
    part_keys = jax.random.split(jax.random.fold_in(seeds[8], part), 9)
    features = gaussian(part_keys[0], (TILES, TOK_TILE, VIS), 1.0, 6.0, ((1, 4),))
    proj_weight = gaussian(seeds[1], (VIS, D), VIS ** -0.5, 0.0625, ((0, 4), (1, 4)))
    proj_bias = gaussian(seeds[2], (D,), 0.5, 3.0, ((0, 4),))
    kv_weight = gaussian(seeds[3], (D, KVH * LAYERS * 2 * HD), D ** -0.5, 0.0625, ((0, 4), (1, 4)))
    key_gain = jnp.clip(1.0 + 0.18 * jax.random.normal(seeds[4], (LAYERS, HD), jnp.float32), 0.1, 1.9)
    tile_map = draw_tile_map(jax.random.fold_in(jax.random.fold_in(seeds[8], part), 71), part)
    tile_count = draw_tile_count(jax.random.fold_in(jax.random.fold_in(seeds[8], part), 71), part)
    decode_owner = draw_decode_owner(jax.random.fold_in(jax.random.fold_in(seeds[8], part), 71), part)
    return {"features": features, "proj_weight": proj_weight, "proj_bias": proj_bias, "kv_weight": kv_weight, "key_gain": key_gain, "tile_map": tile_map, "tile_count": tile_count, "decode_owner": decode_owner}


eps_norm = 1e-05

def reference(features, proj_weight, proj_bias, kv_weight, key_gain, tile_map, tile_count, decode_owner):
    tile_slots, tile_tokens, feature_width = features.shape
    feature_rows = features.reshape(tile_slots * tile_tokens, feature_width)
    projected = jnp.dot(feature_rows, proj_weight, preferred_element_type=jnp.float32)
    projected = (projected + proj_bias.astype(jnp.float32)).astype(jnp.bfloat16)
    key_value = jnp.dot(projected, kv_weight, preferred_element_type=jnp.float32)
    layers, head_dim = key_gain.shape
    blocks = key_value.reshape(tile_slots, tile_tokens, KVH, layers, 2, head_dim)
    keys_raw = blocks[:, :, :, :, 0]
    inv_rms = lax.rsqrt(lax.optimization_barrier(jnp.mean(keys_raw * keys_raw, axis=-1, keepdims=True)) + eps_norm)
    keys_normed = keys_raw * inv_rms * key_gain
    stacked = jnp.stack([keys_normed, blocks[:, :, :, :, 1]], axis=4).astype(jnp.bfloat16)
    per_group = KVH // HEAD_GROUPS
    most_tiles = tile_map.shape[1]

    def one_request(request):
        usable = jnp.arange(most_tiles) < tile_count[request]
        picked = stacked[tile_map[request]]
        picked = jnp.where(usable[:, None, None, None, None, None], picked, jnp.zeros_like(picked))
        picked = picked.reshape(most_tiles * tile_tokens, HEAD_GROUPS, per_group * layers * 2, head_dim)
        picked = jnp.transpose(picked, (1, 0, 2, 3))
        return jnp.roll(picked, decode_owner[request] % HEAD_GROUPS, axis=0)
    per_request = lax.map(one_request, jnp.arange(REQUESTS))
    cache = jnp.zeros_like(per_request).at[decode_owner // HEAD_GROUPS].set(per_request)
    return cache
```

```python
import jax
import jax.numpy as jnp
from jax import lax
from jax.sharding import PartitionSpec as P

eps_norm = 1e-05


def shifted_2(shard, axis, by):
    count = lax.axis_size(axis)
    return lax.ppermute(shard, axis, [(i, (i + by) % count) for i in range(count)])


def swapped(shard, axis, bit):
    return lax.ppermute(shard, axis, [(i, i ^ bit) for i in range(lax.axis_size(axis))])


def add_columns(operand, portion):
    return jnp.dot(operand, portion, preferred_element_type=jnp.float32)


def routing(tile_map, tile_count, decode_owner, tile_slots, head_groups):
    most_tiles = tile_map.shape[1]
    owner_tile = decode_owner // head_groups
    owner_turn = decode_owner % head_groups
    usable = jnp.arange(most_tiles)[None, :] < tile_count[:, None]
    matched = (tile_map[:, :, None] == jnp.arange(tile_slots)[None, None, :]) & usable[:, :, None]
    return owner_tile, owner_turn, matched


def gather_plan(
    features, proj_weight, proj_bias, kv_weight, key_gain, tile_map, tile_count, decode_owner
):
    tile_slots, shard_len, feature_width = features.shape
    token_rows = tile_slots * shard_len
    feature_rows = features.reshape(token_rows, feature_width)
    weight_cols = lax.all_gather(proj_weight, "tile", axis=0, tiled=True)
    projected = jnp.dot(feature_rows, weight_cols, preferred_element_type=jnp.float32)
    projected_local = (projected + proj_bias.astype(jnp.float32)).astype(jnp.bfloat16)
    kv_width = kv_weight.shape[1]
    projected_all = lax.all_gather(projected_local, "head", axis=1, tiled=True)
    key_value = add_columns(projected_all, lax.all_gather(kv_weight, "tile", axis=0, tiled=True))
    layers, head_dim = key_gain.shape
    blocks = key_value.reshape(token_rows, -1, layers, 2, head_dim)
    keys_raw = blocks[:, :, :, 0]
    inv_rms = lax.rsqrt(jnp.mean(keys_raw * keys_raw, axis=-1, keepdims=True) + eps_norm)
    keys_normed = keys_raw * inv_rms * key_gain[None, None]
    stacked = jnp.stack([keys_normed, blocks[:, :, :, 1]], axis=3).astype(jnp.bfloat16)
    per_tile = stacked.reshape(tile_slots, shard_len * kv_width)
    tile_ranks = lax.axis_size("tile")
    head_groups = lax.axis_size("head")
    most_tiles = tile_map.shape[1]
    owner_tile, owner_turn, matched = routing(
        tile_map, tile_count, decode_owner, tile_slots, head_groups
    )
    owned_by = (owner_tile[:, None] == jnp.arange(tile_ranks)[None, :]).astype(jnp.float32)
    selector = jnp.einsum("rd,rjs->jds", owned_by, matched.astype(jnp.float32))
    selector = selector.astype(jnp.bfloat16).reshape(most_tiles * tile_ranks, tile_slots)
    outgoing = add_columns(selector, per_tile).astype(jnp.bfloat16)
    outgoing = outgoing.reshape(most_tiles, tile_ranks, shard_len, kv_width)
    arrived = lax.all_to_all(outgoing, "tile", split_axis=1, concat_axis=1, tiled=True)
    gathered_rows = arrived.reshape(
        most_tiles * tile_ranks * shard_len, kv_width // head_dim, head_dim
    )
    my_turn = jnp.sum(jnp.where(owner_tile == lax.axis_index("tile"), owner_turn, 0))
    stride = 1
    while stride < head_groups:
        shifted = shifted_2(gathered_rows, "head", stride)
        gathered_rows = jnp.where(my_turn // stride % 2 == 1, shifted, gathered_rows)
        stride = stride * 2
    return gathered_rows[None, None]


block_order = ((3, 2, 1, 0), (3, 2, 0, 1), (0, 1, 3, 2), (0, 1, 2, 3))
inward = [(0, 1), (3, 2)]
across = [(1, 2), (2, 1)]
outward = [(2, 3), (1, 0)]


def sum_over_planes(block):
    def send(value, pairs):
        return lax.ppermute(value.astype(jnp.bfloat16), "head", pairs).astype(jnp.float32)

    first_in = send(block(0), inward)
    second_in = send(block(1), inward)
    third_in = send(block(2), inward)
    first_across = send(block(0) + first_in, across)
    second_across = send(block(1) + second_in, across)
    first_out = send(block(2) + first_across, outward)
    return (block(3) + third_in + second_across + first_out).astype(jnp.bfloat16)


def product_plan(
    features, proj_weight, proj_bias, kv_weight, key_gain, tile_map, tile_count, decode_owner
):
    tile_slots, shard_len, feature_width = features.shape
    token_rows = tile_slots * shard_len
    depth = proj_weight.shape[0]
    layers, head_dim = key_gain.shape
    most_tiles = tile_map.shape[1]
    group, tile, head = (lax.axis_index(name) for name in ("groups", "tile", "head"))
    feature_rows = features.reshape(token_rows, feature_width)
    feature_parts = [
        lax.dynamic_slice_in_dim(feature_rows, (tile ^ r) * depth, depth, axis=1) for r in range(4)
    ]
    flip = [(t * 4 + h, h * 4 + t) for t in range(4) for h in range(4)]

    def turned(shard):
        return lax.ppermute(shard, ("tile", "head"), flip)

    bias_rows = turned(proj_bias)
    bias_part = add_columns(bias_rows[None], kv_weight)
    bias_part = bias_part + swapped(bias_part, "tile", 1)
    bias_part = bias_part + swapped(bias_part, "tile", 2)
    bias_part = bias_part.reshape(2, layers, 2, head_dim)

    owner_tile, owner_turn, matched = routing(tile_map, tile_count, decode_owner, tile_slots, 4)
    turn_of = jnp.sum(jnp.where(matched, owner_turn[:, None, None], 0), axis=(0, 1))
    owned_by = (owner_tile[:, None] == (tile ^ jnp.arange(4))[None, :]).astype(jnp.float32)
    selector = jnp.einsum("rd,rjs->djs", owned_by, matched.astype(jnp.float32))
    selector = selector.astype(jnp.bfloat16).reshape(4 * most_tiles, tile_slots)

    order = jnp.array(block_order, jnp.int32)[head]
    per_head = kv_weight.reshape(-1, 2, layers, 2, head_dim)
    mine = lax.dynamic_index_in_dim(per_head, group, axis=1, keepdims=False)
    width = layers * head_dim
    routed = []
    for part in range(2):
        block_0 = turned(mine[:, :, part].reshape(-1, width))
        block_2 = swapped(block_0, "tile", 2)
        near = jnp.concatenate([block_0, swapped(block_0, "tile", 1)], axis=1)
        far = jnp.concatenate([block_2, swapped(block_2, "tile", 1)], axis=1)
        near_product = add_columns(proj_weight, near)
        far_product = add_columns(proj_weight, far)

        def block(k):
            which = order[k] ^ tile
            from_near = lax.dynamic_slice_in_dim(near_product, which % 2 * width, width, axis=1)
            from_far = lax.dynamic_slice_in_dim(far_product, which % 2 * width, width, axis=1)
            return jnp.where(which >= 2, from_far, from_near)

        own = sum_over_planes(block)
        across_x, across_y = swapped(own, "tile", 2), swapped(own, "groups", 1)
        diagonal = swapped(across_y, "tile", 2) if part == 0 else swapped(across_x, "groups", 1)
        rows_0 = jnp.concatenate([own, across_y], axis=1)
        rows_2 = jnp.concatenate([across_x, diagonal], axis=1)
        rows = [rows_0, swapped(rows_0, "tile", 1), rows_2, swapped(rows_2, "tile", 1)]
        total = sum(add_columns(feature_parts[r], rows[r]) for r in range(4))
        total = total.reshape(token_rows, 2, layers, head_dim)
        total = jnp.where(group == 0, total, total[:, ::-1]) + bias_part[None, :, :, part]
        if part == 0:
            inv_rms = lax.rsqrt(jnp.mean(total * total, axis=-1, keepdims=True) + eps_norm)
            total = total * inv_rms * key_gain[None, None]
        rolled = total.astype(jnp.bfloat16).reshape(tile_slots, shard_len, 2 * width)
        for stride in (1, 2):
            odd = (turn_of // stride % 2 == 1)[:, None, None]
            rolled = jnp.where(odd, shifted_2(rolled, "head", stride), rolled)
        outgoing = add_columns(selector, rolled.reshape(tile_slots, -1)).astype(jnp.bfloat16)
        outgoing = outgoing.reshape(4, most_tiles, shard_len, 2, layers, head_dim)
        arrived = [outgoing[0]] + [swapped(outgoing[r], "tile", r) for r in (1, 2, 3)]
        even = [jnp.where(tile % 2 == 0, arrived[r], arrived[r ^ 1]) for r in range(4)]
        ranked = [jnp.where(tile < 2, even[r], even[r ^ 2]) for r in range(4)]
        routed.append(jnp.stack(ranked, axis=1))
    cache = jnp.stack(routed, axis=-2)
    return cache.reshape(1, 1, most_tiles * 4 * shard_len, 4 * layers, head_dim)


def solution(mesh):
    placed = (
        P("groups", "tile", None),
        P("tile", "head"),
        P("head"),
        P("tile", "head"),
        P(),
        P("groups", None),
        P("groups"),
        P("groups"),
    )
    sizes = tuple(mesh.shape[name] for name in ("groups", "tile", "head"))
    return jax.shard_map(
        product_plan if sizes == (2, 4, 4) else gather_plan,
        mesh=mesh,
        in_specs=placed,
        out_specs=P(("groups", "tile"), "head", None, None, None),
        check_vma=False,
    )
```

```python
import jax
import jax.numpy as jnp
from jax import lax
from jax.sharding import PartitionSpec as P

eps_norm = 1e-05


def shifted_2(shard, axis, by):
    count = lax.axis_size(axis)
    return lax.ppermute(shard, axis, [(i, (i + by) % count) for i in range(count)])


def swapped(shard, axis, bit):
    return lax.ppermute(shard, axis, [(i, i ^ bit) for i in range(lax.axis_size(axis))])


def add_columns(operand, portion):
    return jnp.dot(operand, portion, preferred_element_type=jnp.float32)


def routing(tile_map, tile_count, decode_owner, tile_slots, head_groups):
    most_tiles = tile_map.shape[1]
    owner_tile = decode_owner // head_groups
    owner_turn = decode_owner % head_groups
    usable = jnp.arange(most_tiles)[None, :] < tile_count[:, None]
    matched = (tile_map[:, :, None] == jnp.arange(tile_slots)[None, None, :]) & usable[:, :, None]
    return owner_tile, owner_turn, matched


def gather_plan(
    features, proj_weight, proj_bias, kv_weight, key_gain, tile_map, tile_count, decode_owner
):
    tile_slots, shard_len, feature_width = features.shape
    token_rows = tile_slots * shard_len
    feature_rows = features.reshape(token_rows, feature_width)
    weight_cols = lax.all_gather(proj_weight, "tile", axis=0, tiled=True)
    projected = jnp.dot(feature_rows, weight_cols, preferred_element_type=jnp.float32)
    projected_local = (projected + proj_bias.astype(jnp.float32)).astype(jnp.bfloat16)
    kv_width = kv_weight.shape[1]
    projected_all = lax.all_gather(projected_local, "head", axis=1, tiled=True)
    key_value = add_columns(projected_all, lax.all_gather(kv_weight, "tile", axis=0, tiled=True))
    layers, head_dim = key_gain.shape
    blocks = key_value.reshape(token_rows, -1, layers, 2, head_dim)
    keys_raw = blocks[:, :, :, 0]
    inv_rms = lax.rsqrt(jnp.mean(keys_raw * keys_raw, axis=-1, keepdims=True) + eps_norm)
    keys_normed = keys_raw * inv_rms * key_gain[None, None]
    stacked = jnp.stack([keys_normed, blocks[:, :, :, 1]], axis=3).astype(jnp.bfloat16)
    per_tile = stacked.reshape(tile_slots, shard_len * kv_width)
    tile_ranks = lax.axis_size("tile")
    head_groups = lax.axis_size("head")
    most_tiles = tile_map.shape[1]
    owner_tile, owner_turn, matched = routing(
        tile_map, tile_count, decode_owner, tile_slots, head_groups
    )
    owned_by = (owner_tile[:, None] == jnp.arange(tile_ranks)[None, :]).astype(jnp.float32)
    selector = jnp.einsum("rd,rjs->jds", owned_by, matched.astype(jnp.float32))
    selector = selector.astype(jnp.bfloat16).reshape(most_tiles * tile_ranks, tile_slots)
    outgoing = add_columns(selector, per_tile).astype(jnp.bfloat16)
    outgoing = outgoing.reshape(most_tiles, tile_ranks, shard_len, kv_width)
    arrived = lax.all_to_all(outgoing, "tile", split_axis=1, concat_axis=1, tiled=True)
    gathered_rows = arrived.reshape(
        most_tiles * tile_ranks * shard_len, kv_width // head_dim, head_dim
    )
    my_turn = jnp.sum(jnp.where(owner_tile == lax.axis_index("tile"), owner_turn, 0))
    stride = 1
    while stride < head_groups:
        shifted = shifted_2(gathered_rows, "head", stride)
        gathered_rows = jnp.where(my_turn // stride % 2 == 1, shifted, gathered_rows)
        stride = stride * 2
    return gathered_rows[None, None]


def product_plan(
    features, proj_weight, proj_bias, kv_weight, key_gain, tile_map, tile_count, decode_owner
):
    tile_slots, shard_len, feature_width = features.shape
    token_rows = tile_slots * shard_len
    depth = proj_weight.shape[0]
    layers, head_dim = key_gain.shape
    width = layers * head_dim
    most_tiles = tile_map.shape[1]
    group, tile, head = (lax.axis_index(name) for name in ("groups", "tile", "head"))
    first_core, first_chip = tile % 2 == 0, tile < 2
    at_end = (head == 0) | (head == 3)
    feature_rows = features.reshape(token_rows, feature_width)
    feature_parts = [
        lax.dynamic_slice_in_dim(feature_rows, (tile ^ r) * depth, depth, axis=1) for r in range(4)
    ]

    flip = [(t * 4 + h, h * 4 + t) for t in range(4) for h in range(4)]
    bias_rows = lax.ppermute(proj_bias, ("tile", "head"), flip)
    bias_part = add_columns(bias_rows[None], kv_weight)
    bias_part = bias_part + swapped(bias_part, "tile", 1)
    bias_part = bias_part + swapped(bias_part, "tile", 2)
    bias_part = bias_part.reshape(2, layers, 2, head_dim)

    owner_tile, owner_turn, matched = routing(tile_map, tile_count, decode_owner, tile_slots, 4)
    turn_of = jnp.sum(jnp.where(matched, owner_turn[:, None, None], 0), axis=(0, 1))
    owned_by = (owner_tile[:, None] == (tile ^ jnp.arange(4))[None, :]).astype(jnp.float32)
    selector = jnp.einsum("rd,rjs->djs", owned_by, matched.astype(jnp.float32))
    selector = selector.astype(jnp.bfloat16).reshape(4 * most_tiles, tile_slots)

    rounds = [
        [
            (t * 4 + h, (t // 2 * 2 + (h ^ h // 2) % 2) * 4 + t % 2 + 2 * ((h // 2) ^ j))
            for t in range(4)
            for h in range(4)
        ]
        for j in range(2)
    ]
    half = kv_weight.shape[0] // 2
    routed = []
    for part in range(2):
        column = (group * 2 + part) * head_dim
        mine = lax.dynamic_slice_in_dim(kv_weight, column, head_dim, axis=1)
        stays = lax.dynamic_slice_in_dim(mine, tile // 2 * half, half, axis=0)
        leaves = lax.dynamic_slice_in_dim(mine, half - tile // 2 * half, half, axis=0)
        comes = swapped(leaves, "tile", 2)
        pieces = []
        for j in range(2):
            own_rows = tile // 2 == (head // 2) ^ j
            pieces.append(
                lax.ppermute(jnp.where(own_rows, stays, comes), ("tile", "head"), rounds[j])
            )
        near_half = jnp.concatenate(pieces, axis=1)
        other_half = swapped(near_half, "tile", 2)
        near = jnp.concatenate(
            [
                jnp.where(first_chip, near_half, other_half),
                jnp.where(first_chip, other_half, near_half),
            ],
            axis=0,
        )
        far = swapped(near, "tile", 1)
        far_leaves = at_end == first_core
        outer = add_columns(proj_weight, jnp.where(far_leaves, far, near)).astype(jnp.bfloat16)
        pair_sum = add_columns(proj_weight, jnp.where(far_leaves, near, far))
        pair_sum = pair_sum + swapped(outer, "head", 1).astype(jnp.float32)
        mirrored = swapped(pair_sum[:, width:].astype(jnp.bfloat16), "head", 3)
        own = (pair_sum[:, :width] + mirrored.astype(jnp.float32)).astype(jnp.bfloat16)

        across_x, across_y = swapped(own, "tile", 2), swapped(own, "groups", 1)
        diagonal = swapped(across_y, "tile", 2) if part == 0 else swapped(across_x, "groups", 1)

        def both_heads(ours, theirs):
            left, right = jnp.where(group == 0, ours, theirs), jnp.where(group == 0, theirs, ours)
            return lax.optimization_barrier(jnp.concatenate([left, right], axis=1))

        rows_0, rows_2 = both_heads(own, across_y), both_heads(across_x, diagonal)
        rows = [rows_0, swapped(rows_0, "tile", 1), rows_2, swapped(rows_2, "tile", 1)]
        total = sum(add_columns(feature_parts[r], rows[r]) for r in range(4))
        finished = []
        for k in range(2):
            entries = total[:, k * width : (k + 1) * width].reshape(token_rows, layers, head_dim)
            entries = entries + bias_part[k, :, part][None]
            if part == 0:
                squares = jnp.mean(entries * entries, axis=-1, keepdims=True)
                entries = entries * lax.rsqrt(squares + eps_norm) * key_gain[None]
            finished.append(entries.reshape(token_rows, width).astype(jnp.bfloat16))
        rolled = jnp.concatenate(finished, axis=1).reshape(tile_slots, shard_len, 2 * width)
        for stride in (1, 2):
            odd = (turn_of // stride % 2 == 1)[:, None, None]
            rolled = jnp.where(odd, shifted_2(rolled, "head", stride), rolled)
        outgoing = add_columns(selector, rolled.reshape(tile_slots, -1)).astype(jnp.bfloat16)
        outgoing = outgoing.reshape(4, most_tiles, shard_len, 2, layers, head_dim)
        arrived = [outgoing[0]] + [swapped(outgoing[r], "tile", r) for r in (1, 2, 3)]
        even = [jnp.where(first_core, arrived[r], arrived[r ^ 1]) for r in range(4)]
        ranked = [jnp.where(first_chip, even[r], even[r ^ 2]) for r in range(4)]
        routed.append(jnp.stack(ranked, axis=1))
    cache = jnp.stack(routed, axis=-2)
    return cache.reshape(1, 1, most_tiles * 4 * shard_len, 4 * layers, head_dim)


def solution(mesh):
    placed = (
        P("groups", "tile", None),
        P("tile", "head"),
        P("head"),
        P("tile", "head"),
        P(),
        P("groups", None),
        P("groups"),
        P("groups"),
    )
    sizes = tuple(mesh.shape[name] for name in ("groups", "tile", "head"))
    return jax.shard_map(
        product_plan if sizes == (2, 4, 4) else gather_plan,
        mesh=mesh,
        in_specs=placed,
        out_specs=P(("groups", "tile"), "head", None, None, None),
        check_vma=False,
    )
```

```python
import jax
import jax.numpy as jnp
from jax import lax
from jax.sharding import PartitionSpec as P

eps_norm = 1e-05


def shifted_2(shard, axis, by):
    count = lax.axis_size(axis)
    return lax.ppermute(shard, axis, [(i, (i + by) % count) for i in range(count)])


def swapped(shard, axis, bit):
    return lax.ppermute(shard, axis, [(i, i ^ bit) for i in range(lax.axis_size(axis))])


def add_columns(operand, portion):
    return jnp.dot(operand, portion, preferred_element_type=jnp.float32)


def routing(tile_map, tile_count, decode_owner, tile_slots, head_groups):
    most_tiles = tile_map.shape[1]
    owner_tile = decode_owner // head_groups
    owner_turn = decode_owner % head_groups
    usable = jnp.arange(most_tiles)[None, :] < tile_count[:, None]
    matched = (tile_map[:, :, None] == jnp.arange(tile_slots)[None, None, :]) & usable[:, :, None]
    return owner_tile, owner_turn, matched


def gather_plan(
    features, proj_weight, proj_bias, kv_weight, key_gain, tile_map, tile_count, decode_owner
):
    tile_slots, shard_len, feature_width = features.shape
    token_rows = tile_slots * shard_len
    feature_rows = features.reshape(token_rows, feature_width)
    weight_cols = lax.all_gather(proj_weight, "tile", axis=0, tiled=True)
    projected = jnp.dot(feature_rows, weight_cols, preferred_element_type=jnp.float32)
    projected_local = (projected + proj_bias.astype(jnp.float32)).astype(jnp.bfloat16)
    kv_width = kv_weight.shape[1]
    projected_all = lax.all_gather(projected_local, "head", axis=1, tiled=True)
    key_value = add_columns(projected_all, lax.all_gather(kv_weight, "tile", axis=0, tiled=True))
    layers, head_dim = key_gain.shape
    blocks = key_value.reshape(token_rows, -1, layers, 2, head_dim)
    keys_raw = blocks[:, :, :, 0]
    inv_rms = lax.rsqrt(jnp.mean(keys_raw * keys_raw, axis=-1, keepdims=True) + eps_norm)
    keys_normed = keys_raw * inv_rms * key_gain[None, None]
    stacked = jnp.stack([keys_normed, blocks[:, :, :, 1]], axis=3).astype(jnp.bfloat16)
    per_tile = stacked.reshape(tile_slots, shard_len * kv_width)
    tile_ranks = lax.axis_size("tile")
    head_groups = lax.axis_size("head")
    most_tiles = tile_map.shape[1]
    owner_tile, owner_turn, matched = routing(
        tile_map, tile_count, decode_owner, tile_slots, head_groups
    )
    owned_by = (owner_tile[:, None] == jnp.arange(tile_ranks)[None, :]).astype(jnp.float32)
    selector = jnp.einsum("rd,rjs->jds", owned_by, matched.astype(jnp.float32))
    selector = selector.astype(jnp.bfloat16).reshape(most_tiles * tile_ranks, tile_slots)
    outgoing = add_columns(selector, per_tile).astype(jnp.bfloat16)
    outgoing = outgoing.reshape(most_tiles, tile_ranks, shard_len, kv_width)
    arrived = lax.all_to_all(outgoing, "tile", split_axis=1, concat_axis=1, tiled=True)
    gathered_rows = arrived.reshape(
        most_tiles * tile_ranks * shard_len, kv_width // head_dim, head_dim
    )
    my_turn = jnp.sum(jnp.where(owner_tile == lax.axis_index("tile"), owner_turn, 0))
    stride = 1
    while stride < head_groups:
        shifted = shifted_2(gathered_rows, "head", stride)
        gathered_rows = jnp.where(my_turn // stride % 2 == 1, shifted, gathered_rows)
        stride = stride * 2
    return gathered_rows[None, None]


def after(value, before):
    return value if before is None else lax.optimization_barrier((value, before))[0]


def product_plan(
    features, proj_weight, proj_bias, kv_weight, key_gain, tile_map, tile_count, decode_owner
):
    tile_slots, shard_len, feature_width = features.shape
    token_rows = tile_slots * shard_len
    depth = proj_weight.shape[0]
    layers, head_dim = key_gain.shape
    width = layers * head_dim
    most_tiles = tile_map.shape[1]
    group, tile, head = (lax.axis_index(name) for name in ("groups", "tile", "head"))
    first_core, first_chip = tile % 2 == 0, tile < 2
    at_end = (head == 0) | (head == 3)
    feature_rows = features.reshape(token_rows, feature_width)
    feature_parts = [
        lax.dynamic_slice_in_dim(feature_rows, (tile ^ r) * depth, depth, axis=1) for r in range(4)
    ]

    flip = [(t * 4 + h, h * 4 + t) for t in range(4) for h in range(4)]
    bias_rows = lax.ppermute(proj_bias, ("tile", "head"), flip)
    bias_part = add_columns(bias_rows[None], kv_weight)
    bias_part = bias_part + swapped(bias_part, "tile", 1)
    bias_part = bias_part + swapped(bias_part, "tile", 2)
    bias_part = bias_part.reshape(2, layers, 2, head_dim)

    owner_tile, owner_turn, matched = routing(tile_map, tile_count, decode_owner, tile_slots, 4)
    turn_of = jnp.sum(jnp.where(matched, owner_turn[:, None, None], 0), axis=(0, 1))
    owned_by = (owner_tile[:, None] == (tile ^ jnp.arange(4))[None, :]).astype(jnp.float32)
    selector = jnp.einsum("rd,rjs->djs", owned_by, matched.astype(jnp.float32))
    selector = selector.astype(jnp.bfloat16).reshape(4 * most_tiles, tile_slots)

    rounds = [
        [
            (t * 4 + h, (t // 2 * 2 + (h ^ h // 2) % 2) * 4 + t % 2 + 2 * ((h // 2) ^ j))
            for t in range(4)
            for h in range(4)
        ]
        for j in range(2)
    ]
    half = kv_weight.shape[0] // 2

    def cross_chips(part, before):
        column = (group * 2 + part) * head_dim
        mine = lax.dynamic_slice_in_dim(kv_weight, column, head_dim, axis=1)
        stays = lax.dynamic_slice_in_dim(mine, tile // 2 * half, half, axis=0)
        leaves = lax.dynamic_slice_in_dim(mine, half - tile // 2 * half, half, axis=0)
        return stays, swapped(after(leaves, before), "tile", 2)

    def cross_planes(stays, comes, before):
        pieces = []
        for j in range(2):
            own_rows = tile // 2 == (head // 2) ^ j
            piece = after(jnp.where(own_rows, stays, comes), before)
            pieces.append(lax.ppermute(piece, ("tile", "head"), rounds[j]))
        return jnp.concatenate(pieces, axis=1)

    def within_plane(near_half):
        other_half = swapped(near_half, "tile", 2)
        top = jnp.where(first_chip, near_half, other_half)
        bottom = jnp.where(first_chip, other_half, near_half)
        near = jnp.concatenate([top, bottom], axis=0)
        return near, swapped(near, "tile", 1)

    def sum_over_planes(near, far, before):
        far_leaves = at_end == first_core
        outer = add_columns(proj_weight, jnp.where(far_leaves, far, near)).astype(jnp.bfloat16)
        pair_sum = add_columns(proj_weight, jnp.where(far_leaves, near, far))
        pair_sum = pair_sum + swapped(after(outer, before), "head", 1).astype(jnp.float32)
        mirrored = swapped(pair_sum[:, width:].astype(jnp.bfloat16), "head", 3)
        return (pair_sum[:, :width] + mirrored.astype(jnp.float32)).astype(jnp.bfloat16)

    def both_heads(ours, theirs):
        left, right = jnp.where(group == 0, ours, theirs), jnp.where(group == 0, theirs, ours)
        return lax.optimization_barrier(jnp.concatenate([left, right], axis=1))

    def times_features(own, part):
        across_x, across_y = swapped(own, "tile", 2), swapped(own, "groups", 1)
        diagonal = swapped(across_y, "tile", 2) if part == 0 else swapped(across_x, "groups", 1)
        rows_0, rows_2 = both_heads(own, across_y), both_heads(across_x, diagonal)
        rows = [rows_0, swapped(rows_0, "tile", 1), rows_2, swapped(rows_2, "tile", 1)]
        return sum(add_columns(feature_parts[r], rows[r]) for r in range(4))

    def finish(total, part):
        finished = []
        for k in range(2):
            entries = total[:, k * width : (k + 1) * width].reshape(token_rows, layers, head_dim)
            entries = entries + bias_part[k, :, part][None]
            if part == 0:
                squares = jnp.mean(entries * entries, axis=-1, keepdims=True)
                entries = entries * lax.rsqrt(squares + eps_norm) * key_gain[None]
            finished.append(entries.reshape(token_rows, width).astype(jnp.bfloat16))
        return jnp.concatenate(finished, axis=1).reshape(tile_slots, shard_len, 2 * width)

    def route(rolled, before):
        rolled = after(rolled, before)
        for stride in (1, 2):
            odd = (turn_of // stride % 2 == 1)[:, None, None]
            rolled = jnp.where(odd, shifted_2(rolled, "head", stride), rolled)
        outgoing = add_columns(selector, rolled.reshape(tile_slots, -1)).astype(jnp.bfloat16)
        outgoing = outgoing.reshape(4, most_tiles, shard_len, 2, layers, head_dim)
        arrived = [outgoing[0]] + [swapped(outgoing[r], "tile", r) for r in (1, 2, 3)]
        even = [jnp.where(first_core, arrived[r], arrived[r ^ 1]) for r in range(4)]
        ranked = [jnp.where(first_chip, even[r], even[r ^ 2]) for r in range(4)]
        return jnp.stack(ranked, axis=1), rolled

    key_stays, key_comes = cross_chips(0, None)
    value_stays, value_comes = cross_chips(1, key_comes)
    key_half = cross_planes(key_stays, key_comes, None)
    value_half = cross_planes(value_stays, value_comes, key_half)
    key_near, key_far = within_plane(key_half)
    value_near, value_far = within_plane(after(value_half, key_near))
    key_own = sum_over_planes(key_near, key_far, None)
    value_own = sum_over_planes(value_near, value_far, key_own)
    keys = finish(times_features(key_own, 0), 0)
    values = finish(times_features(value_own, 1), 1)
    routed_keys, keys = route(keys, value_own)
    routed_values, _ = route(values, keys)
    cache = jnp.stack([routed_keys, routed_values], axis=-2)
    return cache.reshape(1, 1, most_tiles * 4 * shard_len, 4 * layers, head_dim)


def solution(mesh):
    placed = (
        P("groups", "tile", None),
        P("tile", "head"),
        P("head"),
        P("tile", "head"),
        P(),
        P("groups", None),
        P("groups"),
        P("groups"),
    )
    sizes = tuple(mesh.shape[name] for name in ("groups", "tile", "head"))
    return jax.shard_map(
        product_plan if sizes == (2, 4, 4) else gather_plan,
        mesh=mesh,
        in_specs=placed,
        out_specs=P(("groups", "tile"), "head", None, None, None),
        check_vma=False,
    )
```

```python
import jax
import jax.numpy as jnp
from jax import lax
from jax.sharding import PartitionSpec as P

eps_norm = 1e-05


def shifted_2(shard, axis, by):
    count = lax.axis_size(axis)
    return lax.ppermute(shard, axis, [(i, (i + by) % count) for i in range(count)])


def swapped(shard, axis, bit):
    return lax.ppermute(shard, axis, [(i, i ^ bit) for i in range(lax.axis_size(axis))])


def add_columns(operand, portion):
    return jnp.dot(operand, portion, preferred_element_type=jnp.float32)


def routing(tile_map, tile_count, decode_owner, tile_slots, head_groups):
    most_tiles = tile_map.shape[1]
    owner_tile = decode_owner // head_groups
    owner_turn = decode_owner % head_groups
    usable = jnp.arange(most_tiles)[None, :] < tile_count[:, None]
    matched = (tile_map[:, :, None] == jnp.arange(tile_slots)[None, None, :]) & usable[:, :, None]
    return owner_tile, owner_turn, matched


def gather_plan(
    features, proj_weight, proj_bias, kv_weight, key_gain, tile_map, tile_count, decode_owner
):
    tile_slots, shard_len, feature_width = features.shape
    token_rows = tile_slots * shard_len
    feature_rows = features.reshape(token_rows, feature_width)
    weight_cols = lax.all_gather(proj_weight, "tile", axis=0, tiled=True)
    projected = jnp.dot(feature_rows, weight_cols, preferred_element_type=jnp.float32)
    projected_local = (projected + proj_bias.astype(jnp.float32)).astype(jnp.bfloat16)
    kv_width = kv_weight.shape[1]
    projected_all = lax.all_gather(projected_local, "head", axis=1, tiled=True)
    key_value = add_columns(projected_all, lax.all_gather(kv_weight, "tile", axis=0, tiled=True))
    layers, head_dim = key_gain.shape
    blocks = key_value.reshape(token_rows, -1, layers, 2, head_dim)
    keys_raw = blocks[:, :, :, 0]
    inv_rms = lax.rsqrt(jnp.mean(keys_raw * keys_raw, axis=-1, keepdims=True) + eps_norm)
    keys_normed = keys_raw * inv_rms * key_gain[None, None]
    stacked = jnp.stack([keys_normed, blocks[:, :, :, 1]], axis=3).astype(jnp.bfloat16)
    per_tile = stacked.reshape(tile_slots, shard_len * kv_width)
    tile_ranks = lax.axis_size("tile")
    head_groups = lax.axis_size("head")
    most_tiles = tile_map.shape[1]
    owner_tile, owner_turn, matched = routing(
        tile_map, tile_count, decode_owner, tile_slots, head_groups
    )
    owned_by = (owner_tile[:, None] == jnp.arange(tile_ranks)[None, :]).astype(jnp.float32)
    selector = jnp.einsum("rd,rjs->jds", owned_by, matched.astype(jnp.float32))
    selector = selector.astype(jnp.bfloat16).reshape(most_tiles * tile_ranks, tile_slots)
    outgoing = add_columns(selector, per_tile).astype(jnp.bfloat16)
    outgoing = outgoing.reshape(most_tiles, tile_ranks, shard_len, kv_width)
    arrived = lax.all_to_all(outgoing, "tile", split_axis=1, concat_axis=1, tiled=True)
    gathered_rows = arrived.reshape(
        most_tiles * tile_ranks * shard_len, kv_width // head_dim, head_dim
    )
    my_turn = jnp.sum(jnp.where(owner_tile == lax.axis_index("tile"), owner_turn, 0))
    stride = 1
    while stride < head_groups:
        shifted = shifted_2(gathered_rows, "head", stride)
        gathered_rows = jnp.where(my_turn // stride % 2 == 1, shifted, gathered_rows)
        stride = stride * 2
    return gathered_rows[None, None]


def after(value, before):
    return value if before is None else lax.optimization_barrier((value, before))[0]


def product_plan(
    features, proj_weight, proj_bias, kv_weight, key_gain, tile_map, tile_count, decode_owner
):
    tile_slots, shard_len, feature_width = features.shape
    token_rows = tile_slots * shard_len
    depth = proj_weight.shape[0]
    layers, head_dim = key_gain.shape
    width = layers * head_dim
    most_tiles = tile_map.shape[1]
    group, tile, head = (lax.axis_index(name) for name in ("groups", "tile", "head"))
    first_core, first_chip = tile % 2 == 0, tile < 2
    at_end = (head == 0) | (head == 3)
    feature_rows = features.reshape(token_rows, feature_width)
    feature_parts = [
        lax.dynamic_slice_in_dim(feature_rows, (tile ^ r) * depth, depth, axis=1) for r in range(4)
    ]

    flip = [(t * 4 + h, h * 4 + t) for t in range(4) for h in range(4)]
    bias_rows = lax.ppermute(proj_bias, ("tile", "head"), flip)
    bias_part = add_columns(bias_rows[None], kv_weight)
    bias_part = bias_part + swapped(bias_part, "tile", 1)
    bias_part = bias_part + swapped(bias_part, "tile", 2)
    bias_part = bias_part.reshape(2, layers, 2, head_dim)

    owner_tile, owner_turn, matched = routing(tile_map, tile_count, decode_owner, tile_slots, 4)
    turn_of = jnp.sum(jnp.where(matched, owner_turn[:, None, None], 0), axis=(0, 1))
    owned_by = (owner_tile[:, None] == (tile ^ jnp.arange(4))[None, :]).astype(jnp.float32)
    selector = jnp.einsum("rd,rjs->djs", owned_by, matched.astype(jnp.float32))
    selector = selector.astype(jnp.bfloat16).reshape(4 * most_tiles, tile_slots)

    rounds = [
        [
            (t * 4 + h, (t // 2 * 2 + (h ^ h // 2) % 2) * 4 + t % 2 + 2 * ((h // 2) ^ j))
            for t in range(4)
            for h in range(4)
        ]
        for j in range(2)
    ]
    half = kv_weight.shape[0] // 2

    def cross_planes(stays, comes, before):
        pieces = []
        for j in range(2):
            own_rows = tile // 2 == (head // 2) ^ j
            piece = after(jnp.where(own_rows, stays, comes), before)
            pieces.append(lax.ppermute(piece, ("tile", "head"), rounds[j]))
        return jnp.concatenate(pieces, axis=1)

    def whole_rows(near_half, other_half):
        top = jnp.where(first_chip, near_half, other_half)
        bottom = jnp.where(first_chip, other_half, near_half)
        return jnp.concatenate([top, bottom], axis=0)

    far_leaves = at_end == first_core

    def products(near, far):
        leaves = add_columns(proj_weight, jnp.where(far_leaves, far, near)).astype(jnp.bfloat16)
        stays = after(jnp.where(far_leaves, near, far), leaves)
        return leaves, add_columns(proj_weight, stays)

    def mirror_sum(pair_sum):
        mirrored = swapped(pair_sum[:, width:].astype(jnp.bfloat16), "head", 3)
        return (pair_sum[:, :width] + mirrored.astype(jnp.float32)).astype(jnp.bfloat16)

    def other_chips(own):
        diagonal = [
            ((g * 4 + t) * 4 + h, ((1 - g) * 4 + (t ^ 2)) * 4 + h)
            for g in range(2)
            for t in range(4)
            for h in range(4)
        ]
        return (
            swapped(own, "tile", 2),
            swapped(own, "groups", 1),
            lax.ppermute(own, ("groups", "tile", "head"), diagonal),
        )

    def both_heads(ours, theirs):
        left, right = jnp.where(group == 0, ours, theirs), jnp.where(group == 0, theirs, ours)
        return lax.optimization_barrier(jnp.concatenate([left, right], axis=1))

    def times_features(own, others):
        across_x, across_y, diagonal = others
        rows_0, rows_2 = both_heads(own, across_y), both_heads(across_x, diagonal)
        rows = [rows_0, swapped(rows_0, "tile", 1), rows_2, swapped(rows_2, "tile", 1)]
        return sum(add_columns(feature_parts[r], rows[r]) for r in range(4))

    def finish(total, part):
        finished = []
        for k in range(2):
            entries = total[:, k * width : (k + 1) * width].reshape(token_rows, layers, head_dim)
            entries = entries + bias_part[k, :, part][None]
            if part == 0:
                squares = jnp.mean(entries * entries, axis=-1, keepdims=True)
                entries = entries * lax.rsqrt(squares + eps_norm) * key_gain[None]
            finished.append(entries.reshape(token_rows, width).astype(jnp.bfloat16))
        return jnp.concatenate(finished, axis=1).reshape(tile_slots, shard_len, 2 * width)

    def route(rolled, before):
        rolled = after(rolled, before)
        for stride in (1, 2):
            odd = (turn_of // stride % 2 == 1)[:, None, None]
            rolled = jnp.where(odd, shifted_2(rolled, "head", stride), rolled)
        outgoing = add_columns(selector, rolled.reshape(tile_slots, -1)).astype(jnp.bfloat16)
        outgoing = outgoing.reshape(4, most_tiles, shard_len, 2, layers, head_dim)
        arrived = [outgoing[0]] + [swapped(outgoing[r], "tile", r) for r in (1, 2, 3)]
        even = [jnp.where(first_core, arrived[r], arrived[r ^ 1]) for r in range(4)]
        ranked = [jnp.where(first_chip, even[r], even[r ^ 2]) for r in range(4)]
        return jnp.stack(ranked, axis=1), rolled

    mine = lax.dynamic_slice_in_dim(kv_weight, group * 2 * head_dim, 2 * head_dim, axis=1)
    stays = lax.dynamic_slice_in_dim(mine, tile // 2 * half, half, axis=0)
    leaves = lax.dynamic_slice_in_dim(mine, half - tile // 2 * half, half, axis=0)
    comes = swapped(leaves, "tile", 2)
    key_half = cross_planes(stays[:, :width], comes[:, :width], None)
    key_half = after(key_half, bias_part)
    value_half = cross_planes(stays[:, width:], comes[:, width:], key_half)
    key_near = whole_rows(key_half, swapped(key_half, "tile", 2))
    key_near = after(key_near, value_half)
    key_leaves, key_stays = products(key_near, swapped(key_near, "tile", 1))
    value_other = after(swapped(value_half, "tile", 2), key_stays)
    value_near = whole_rows(value_half, value_other)
    value_leaves, value_stays = products(value_near, swapped(value_near, "tile", 1))
    key_comes = after(swapped(key_leaves, "head", 1), value_stays)
    key_own = mirror_sum(key_stays + key_comes.astype(jnp.float32))
    key_others = other_chips(key_own)
    value_comes = after(swapped(after(value_leaves, key_own), "head", 1), key_others)
    value_pair = value_stays + value_comes.astype(jnp.float32)
    value_own = mirror_sum(value_pair)
    keys = finish(times_features(after(key_own, value_pair), key_others), 0)
    routed_keys, keys = route(keys, value_own)
    values = finish(times_features(value_own, other_chips(value_own)), 1)
    routed_values, _ = route(values, keys)
    cache = jnp.stack([routed_keys, routed_values], axis=-2)
    return cache.reshape(1, 1, most_tiles * 4 * shard_len, 4 * layers, head_dim)


def solution(mesh):
    placed = (
        P("groups", "tile", None),
        P("tile", "head"),
        P("head"),
        P("tile", "head"),
        P(),
        P("groups", None),
        P("groups"),
        P("groups"),
    )
    sizes = tuple(mesh.shape[name] for name in ("groups", "tile", "head"))
    return jax.shard_map(
        product_plan if sizes == (2, 4, 4) else gather_plan,
        mesh=mesh,
        in_specs=placed,
        out_specs=P(("groups", "tile"), "head", None, None, None),
        check_vma=False,
    )
```

```python
import jax
import jax.numpy as jnp
from jax import lax
from jax.sharding import PartitionSpec as P

eps_norm = 1e-05


def shifted_2(shard, axis, by):
    count = lax.axis_size(axis)
    return lax.ppermute(shard, axis, [(i, (i + by) % count) for i in range(count)])


def swapped(shard, axis, bit):
    return lax.ppermute(shard, axis, [(i, i ^ bit) for i in range(lax.axis_size(axis))])


def add_columns(operand, portion):
    return jnp.dot(operand, portion, preferred_element_type=jnp.float32)


def routing(tile_map, tile_count, decode_owner, tile_slots, head_groups):
    most_tiles = tile_map.shape[1]
    owner_tile = decode_owner // head_groups
    owner_turn = decode_owner % head_groups
    usable = jnp.arange(most_tiles)[None, :] < tile_count[:, None]
    matched = (tile_map[:, :, None] == jnp.arange(tile_slots)[None, None, :]) & usable[:, :, None]
    return owner_tile, owner_turn, matched


def gather_plan(
    features, proj_weight, proj_bias, kv_weight, key_gain, tile_map, tile_count, decode_owner
):
    tile_slots, shard_len, feature_width = features.shape
    token_rows = tile_slots * shard_len
    feature_rows = features.reshape(token_rows, feature_width)
    weight_cols = lax.all_gather(proj_weight, "tile", axis=0, tiled=True)
    projected = jnp.dot(feature_rows, weight_cols, preferred_element_type=jnp.float32)
    projected_local = (projected + proj_bias.astype(jnp.float32)).astype(jnp.bfloat16)
    kv_width = kv_weight.shape[1]
    projected_all = lax.all_gather(projected_local, "head", axis=1, tiled=True)
    key_value = add_columns(projected_all, lax.all_gather(kv_weight, "tile", axis=0, tiled=True))
    layers, head_dim = key_gain.shape
    blocks = key_value.reshape(token_rows, -1, layers, 2, head_dim)
    keys_raw = blocks[:, :, :, 0]
    inv_rms = lax.rsqrt(jnp.mean(keys_raw * keys_raw, axis=-1, keepdims=True) + eps_norm)
    keys_normed = keys_raw * inv_rms * key_gain[None, None]
    stacked = jnp.stack([keys_normed, blocks[:, :, :, 1]], axis=3).astype(jnp.bfloat16)
    per_tile = stacked.reshape(tile_slots, shard_len * kv_width)
    tile_ranks = lax.axis_size("tile")
    head_groups = lax.axis_size("head")
    most_tiles = tile_map.shape[1]
    owner_tile, owner_turn, matched = routing(
        tile_map, tile_count, decode_owner, tile_slots, head_groups
    )
    owned_by = (owner_tile[:, None] == jnp.arange(tile_ranks)[None, :]).astype(jnp.float32)
    selector = jnp.einsum("rd,rjs->jds", owned_by, matched.astype(jnp.float32))
    selector = selector.astype(jnp.bfloat16).reshape(most_tiles * tile_ranks, tile_slots)
    outgoing = add_columns(selector, per_tile).astype(jnp.bfloat16)
    outgoing = outgoing.reshape(most_tiles, tile_ranks, shard_len, kv_width)
    arrived = lax.all_to_all(outgoing, "tile", split_axis=1, concat_axis=1, tiled=True)
    gathered_rows = arrived.reshape(
        most_tiles * tile_ranks * shard_len, kv_width // head_dim, head_dim
    )
    my_turn = jnp.sum(jnp.where(owner_tile == lax.axis_index("tile"), owner_turn, 0))
    stride = 1
    while stride < head_groups:
        shifted = shifted_2(gathered_rows, "head", stride)
        gathered_rows = jnp.where(my_turn // stride % 2 == 1, shifted, gathered_rows)
        stride = stride * 2
    return gathered_rows[None, None]


def after(value, before):
    return value if before is None else lax.optimization_barrier((value, before))[0]


def product_plan(
    features, proj_weight, proj_bias, kv_weight, key_gain, tile_map, tile_count, decode_owner
):
    tile_slots, shard_len, feature_width = features.shape
    token_rows = tile_slots * shard_len
    depth = proj_weight.shape[0]
    layers, head_dim = key_gain.shape
    width = layers * head_dim
    most_tiles = tile_map.shape[1]
    group, tile, head = (lax.axis_index(name) for name in ("groups", "tile", "head"))
    first_core, first_chip = tile % 2 == 0, tile < 2
    at_end = (head == 0) | (head == 3)
    feature_rows = features.reshape(token_rows, feature_width)
    feature_parts = [
        lax.dynamic_slice_in_dim(feature_rows, (tile ^ r) * depth, depth, axis=1) for r in range(4)
    ]

    flip = [(t * 4 + h, h * 4 + t) for t in range(4) for h in range(4)]
    bias_rows = lax.ppermute(proj_bias, ("tile", "head"), flip)
    bias_part = add_columns(bias_rows[None], kv_weight)
    bias_part = bias_part + swapped(bias_part, "tile", 1)
    bias_part = bias_part + swapped(bias_part, "tile", 2)
    bias_part = bias_part.reshape(2, layers, 2, head_dim)

    owner_tile, owner_turn, matched = routing(tile_map, tile_count, decode_owner, tile_slots, 4)
    turn_of = jnp.sum(jnp.where(matched, owner_turn[:, None, None], 0), axis=(0, 1))
    owned_by = (owner_tile[:, None] == (tile ^ jnp.arange(4))[None, :]).astype(jnp.float32)
    selector = jnp.einsum("rd,rjs->djs", owned_by, matched.astype(jnp.float32))
    selector = selector.astype(jnp.bfloat16).reshape(4 * most_tiles, tile_slots)

    rounds = [
        [
            (t * 4 + h, (t // 2 * 2 + (h ^ h // 2) % 2) * 4 + t % 2 + 2 * ((h // 2) ^ j))
            for t in range(4)
            for h in range(4)
        ]
        for j in range(2)
    ]
    half = kv_weight.shape[0] // 2

    def cross_planes(stays, comes, before):
        pieces = []
        for j in range(2):
            own_rows = tile // 2 == (head // 2) ^ j
            piece = after(jnp.where(own_rows, stays, comes), before)
            pieces.append(lax.ppermute(piece, ("tile", "head"), rounds[j]))
        return jnp.concatenate(pieces, axis=1)

    def whole_rows(near_half, other_half):
        top = jnp.where(first_chip, near_half, other_half)
        bottom = jnp.where(first_chip, other_half, near_half)
        return jnp.concatenate([top, bottom], axis=0)

    far_leaves = at_end == first_core

    def products(near, far):
        leaves = add_columns(proj_weight, jnp.where(far_leaves, far, near)).astype(jnp.bfloat16)
        stays = after(jnp.where(far_leaves, near, far), leaves)
        return leaves, add_columns(proj_weight, stays)

    def mirror_sum(pair_sum):
        mirrored = swapped(pair_sum[:, width:].astype(jnp.bfloat16), "head", 3)
        return (pair_sum[:, :width] + mirrored.astype(jnp.float32)).astype(jnp.bfloat16)

    def other_chips(own):
        diagonal = [
            ((g * 4 + t) * 4 + h, ((1 - g) * 4 + (t ^ 2)) * 4 + h)
            for g in range(2)
            for t in range(4)
            for h in range(4)
        ]
        return (
            swapped(own, "tile", 2),
            swapped(own, "groups", 1),
            lax.ppermute(own, ("groups", "tile", "head"), diagonal),
        )

    def both_heads(ours, theirs):
        left, right = jnp.where(group == 0, ours, theirs), jnp.where(group == 0, theirs, ours)
        return lax.optimization_barrier(jnp.concatenate([left, right], axis=1))

    def times_features(own, others):
        across_x, across_y, diagonal = others
        rows_0, rows_2 = both_heads(own, across_y), both_heads(across_x, diagonal)
        rows = [rows_0, swapped(rows_0, "tile", 1), rows_2, swapped(rows_2, "tile", 1)]
        return sum(add_columns(feature_parts[r], rows[r]) for r in range(4))

    def finish(total, part):
        finished = []
        for k in range(2):
            entries = total[:, k * width : (k + 1) * width].reshape(token_rows, layers, head_dim)
            entries = entries + bias_part[k, :, part][None]
            if part == 0:
                squares = jnp.mean(entries * entries, axis=-1, keepdims=True)
                entries = entries * lax.rsqrt(squares + eps_norm) * key_gain[None]
            finished.append(entries.reshape(token_rows, width).astype(jnp.bfloat16))
        return jnp.concatenate(finished, axis=1).reshape(tile_slots, shard_len, 2 * width)

    def roll(rolled, stride):
        odd = (turn_of // stride % 2 == 1)[:, None, None]
        return jnp.where(odd, shifted_2(rolled, "head", stride), rolled)

    def to_owners(rolled):
        outgoing = add_columns(selector, rolled.reshape(tile_slots, -1)).astype(jnp.bfloat16)
        outgoing = outgoing.reshape(4, most_tiles, shard_len, 2, layers, head_dim)
        arrived = [outgoing[0]] + [swapped(outgoing[r], "tile", r) for r in (1, 2, 3)]
        even = [jnp.where(first_core, arrived[r], arrived[r ^ 1]) for r in range(4)]
        ranked = [jnp.where(first_chip, even[r], even[r ^ 2]) for r in range(4)]
        return jnp.stack(ranked, axis=1)

    column = group * 2 * head_dim
    key_mine = lax.dynamic_slice_in_dim(kv_weight, column, head_dim, axis=1)
    value_mine = lax.dynamic_slice_in_dim(kv_weight, column + head_dim, head_dim, axis=1)
    to_plane = [
        (t * 4 + h, (h // 2 * 2 + (h ^ h // 2) % 2) * 4 + t) for t in range(4) for h in range(4)
    ]
    key_block = after(lax.ppermute(key_mine, ("tile", "head"), to_plane), bias_part)
    stays = lax.dynamic_slice_in_dim(value_mine, tile // 2 * half, half, axis=0)
    leaves = lax.dynamic_slice_in_dim(value_mine, half - tile // 2 * half, half, axis=0)
    value_half = cross_planes(stays, swapped(leaves, "tile", 2), key_block)
    key_other = swapped(key_block, "tile", 2)
    kept_first = tile // 2 == head // 2
    key_near = jnp.concatenate(
        [jnp.where(kept_first, key_block, key_other), jnp.where(kept_first, key_other, key_block)],
        axis=1,
    )
    key_leaves, key_stays = products(key_near, swapped(key_near, "tile", 1))
    value_half = after(value_half, key_leaves)
    value_other = after(swapped(value_half, "tile", 2), key_stays)
    value_near = whole_rows(value_half, value_other)
    value_leaves, value_stays = products(value_near, swapped(value_near, "tile", 1))
    key_comes = after(swapped(key_leaves, "head", 1), value_stays)
    key_own = mirror_sum(key_stays + key_comes.astype(jnp.float32))
    value_comes = swapped(after(value_leaves, key_comes), "head", 1)
    key_others = other_chips(key_own)
    value_comes = after(value_comes, key_others)
    value_pair = value_stays + value_comes.astype(jnp.float32)
    value_own = mirror_sum(value_pair)
    keys = finish(times_features(after(key_own, value_pair), key_others), 0)
    keys = roll(after(keys, value_own), 1)
    value_others = other_chips(value_own)
    values = finish(times_features(after(value_own, keys), value_others), 1)
    keys = roll(keys, 2)
    values = roll(roll(after(values, keys), 1), 2)
    cache = jnp.stack([to_owners(keys), to_owners(values)], axis=-2)
    return cache.reshape(1, 1, most_tiles * 4 * shard_len, 4 * layers, head_dim)


def solution(mesh):
    placed = (
        P("groups", "tile", None),
        P("tile", "head"),
        P("head"),
        P("tile", "head"),
        P(),
        P("groups", None),
        P("groups"),
        P("groups"),
    )
    sizes = tuple(mesh.shape[name] for name in ("groups", "tile", "head"))
    return jax.shard_map(
        product_plan if sizes == (2, 4, 4) else gather_plan,
        mesh=mesh,
        in_specs=placed,
        out_specs=P(("groups", "tile"), "head", None, None, None),
        check_vma=False,
    )
```

```python
import jax
import jax.numpy as jnp
from jax import lax
from jax.sharding import PartitionSpec as P

eps_norm = 1e-05


def shifted_2(shard, axis, by):
    count = lax.axis_size(axis)
    return lax.ppermute(shard, axis, [(i, (i + by) % count) for i in range(count)])


def swapped(shard, axis, bit):
    return lax.ppermute(shard, axis, [(i, i ^ bit) for i in range(lax.axis_size(axis))])


def add_columns(operand, portion):
    return jnp.dot(operand, portion, preferred_element_type=jnp.float32)


def routing(tile_map, tile_count, decode_owner, tile_slots, head_groups):
    most_tiles = tile_map.shape[1]
    owner_tile = decode_owner // head_groups
    owner_turn = decode_owner % head_groups
    usable = jnp.arange(most_tiles)[None, :] < tile_count[:, None]
    matched = (tile_map[:, :, None] == jnp.arange(tile_slots)[None, None, :]) & usable[:, :, None]
    return owner_tile, owner_turn, matched


def gather_plan(
    features, proj_weight, proj_bias, kv_weight, key_gain, tile_map, tile_count, decode_owner
):
    tile_slots, shard_len, feature_width = features.shape
    token_rows = tile_slots * shard_len
    feature_rows = features.reshape(token_rows, feature_width)
    weight_cols = lax.all_gather(proj_weight, "tile", axis=0, tiled=True)
    projected = jnp.dot(feature_rows, weight_cols, preferred_element_type=jnp.float32)
    projected_local = (projected + proj_bias.astype(jnp.float32)).astype(jnp.bfloat16)
    kv_width = kv_weight.shape[1]
    projected_all = lax.all_gather(projected_local, "head", axis=1, tiled=True)
    key_value = add_columns(projected_all, lax.all_gather(kv_weight, "tile", axis=0, tiled=True))
    layers, head_dim = key_gain.shape
    blocks = key_value.reshape(token_rows, -1, layers, 2, head_dim)
    keys_raw = blocks[:, :, :, 0]
    inv_rms = lax.rsqrt(jnp.mean(keys_raw * keys_raw, axis=-1, keepdims=True) + eps_norm)
    keys_normed = keys_raw * inv_rms * key_gain[None, None]
    stacked = jnp.stack([keys_normed, blocks[:, :, :, 1]], axis=3).astype(jnp.bfloat16)
    per_tile = stacked.reshape(tile_slots, shard_len * kv_width)
    tile_ranks = lax.axis_size("tile")
    head_groups = lax.axis_size("head")
    most_tiles = tile_map.shape[1]
    owner_tile, owner_turn, matched = routing(
        tile_map, tile_count, decode_owner, tile_slots, head_groups
    )
    owned_by = (owner_tile[:, None] == jnp.arange(tile_ranks)[None, :]).astype(jnp.float32)
    selector = jnp.einsum("rd,rjs->jds", owned_by, matched.astype(jnp.float32))
    selector = selector.astype(jnp.bfloat16).reshape(most_tiles * tile_ranks, tile_slots)
    outgoing = add_columns(selector, per_tile).astype(jnp.bfloat16)
    outgoing = outgoing.reshape(most_tiles, tile_ranks, shard_len, kv_width)
    arrived = lax.all_to_all(outgoing, "tile", split_axis=1, concat_axis=1, tiled=True)
    gathered_rows = arrived.reshape(
        most_tiles * tile_ranks * shard_len, kv_width // head_dim, head_dim
    )
    my_turn = jnp.sum(jnp.where(owner_tile == lax.axis_index("tile"), owner_turn, 0))
    stride = 1
    while stride < head_groups:
        shifted = shifted_2(gathered_rows, "head", stride)
        gathered_rows = jnp.where(my_turn // stride % 2 == 1, shifted, gathered_rows)
        stride = stride * 2
    return gathered_rows[None, None]


def product_plan(
    features, proj_weight, proj_bias, kv_weight, key_gain, tile_map, tile_count, decode_owner
):
    tile_slots, shard_len, feature_width = features.shape
    token_rows = tile_slots * shard_len
    depth = proj_weight.shape[0]
    layers, head_dim = key_gain.shape
    width = layers * head_dim
    most_tiles = tile_map.shape[1]
    group, tile, head = (lax.axis_index(name) for name in ("groups", "tile", "head"))
    first_core, first_chip = tile % 2 == 0, tile < 2
    at_end = (head == 0) | (head == 3)
    feature_rows = features.reshape(token_rows, feature_width)
    step = lax.optimization_barrier

    def moved(shard, target):
        pairs = []
        for t in range(4):
            for h in range(4):
                to_tile, to_head = target(t, h)
                pairs.append((t * 4 + h, to_tile * 4 + to_head))
        return lax.ppermute(shard, ("tile", "head"), pairs)

    def outer_core(h):
        return (h ^ h // 2) % 2

    def times_features(rows, r):
        columns = lax.dynamic_slice_in_dim(feature_rows, (tile ^ r) * depth, depth, axis=1)
        return add_columns(columns, rows)

    def put_first(condition, one, other, axis):
        return jnp.concatenate(
            [jnp.where(condition, one, other), jnp.where(condition, other, one)], axis=axis
        )

    def both_heads(ours, theirs):
        return put_first(group == 0, ours, theirs, 1)

    def products(near, far):
        near_product, far_product = add_columns(proj_weight, near), add_columns(proj_weight, far)
        near_kept = at_end == first_core
        kept = jnp.where(near_kept, near_product, far_product)
        sent = jnp.where(near_kept, far_product, near_product)
        parts = [sent[:, width:], kept[:, width:], sent[:, :width]]
        return kept[:, :width], [part.astype(jnp.bfloat16) for part in parts]

    def exchange(parts):
        return [swapped(part, "head", bit) for part, bit in zip(parts, (2, 3, 1))]

    def summed(kept, arrived):
        total = kept
        for block in arrived:
            total = total + block.astype(jnp.float32)
        return total.astype(jnp.bfloat16)

    def finish(total, part):
        finished = []
        for k in range(2):
            entries = total[:, k * width : (k + 1) * width].reshape(token_rows, layers, head_dim)
            entries = entries + bias_part[k, :, part][None]
            if part == 0:
                squares = jnp.mean(entries * entries, axis=-1, keepdims=True)
                entries = entries * lax.rsqrt(squares + eps_norm) * key_gain[None]
            finished.append(entries.reshape(token_rows, width).astype(jnp.bfloat16))
        return jnp.concatenate(finished, axis=1).reshape(tile_slots, shard_len, 2 * width)

    owner_tile, owner_turn, matched = routing(tile_map, tile_count, decode_owner, tile_slots, 4)
    turn_of = jnp.sum(jnp.where(matched, owner_turn[:, None, None], 0), axis=(0, 1))
    owned_by = (owner_tile[:, None] == (tile ^ jnp.arange(4))[None, :]).astype(jnp.float32)
    selector = jnp.einsum("rd,rjs->djs", owned_by, matched.astype(jnp.float32))
    selector = selector.astype(jnp.bfloat16).reshape(4 * most_tiles, tile_slots)

    def rolled(rows, shifted, stride):
        odd = (turn_of // stride % 2 == 1)[:, None, None]
        return jnp.where(odd, shifted, rows)

    def outgoing(rows):
        picked = add_columns(selector, rows.reshape(tile_slots, -1)).astype(jnp.bfloat16)
        picked = picked.reshape(4, most_tiles, shard_len, 2, layers, head_dim)
        return [picked[r] for r in range(4)]

    def to_owners(picked):
        return [picked[0]] + [swapped(picked[r], "tile", r) for r in (1, 2, 3)]

    def in_order(arrived):
        even = [jnp.where(first_core, arrived[r], arrived[r ^ 1]) for r in range(4)]
        ranked = [jnp.where(first_chip, even[r], even[r ^ 2]) for r in range(4)]
        return jnp.stack(ranked, axis=1)

    column, half = group * 2 * head_dim, kv_weight.shape[0] // 2
    key_mine = lax.dynamic_slice_in_dim(kv_weight, column, head_dim, axis=1)
    value_mine = lax.dynamic_slice_in_dim(kv_weight, column + head_dim, head_dim, axis=1)
    stays = lax.dynamic_slice_in_dim(value_mine, tile // 2 * half, half, axis=0)
    leaves = lax.dynamic_slice_in_dim(value_mine, half - tile // 2 * half, half, axis=0)
    bias_rows = moved(proj_bias, lambda t, h: (h, t))
    key_block = moved(key_mine, lambda t, h: (h // 2 * 2 + outer_core(h), t))
    comes = swapped(leaves, "tile", 2)
    bias_rows, key_block, comes, stays = step((bias_rows, key_block, comes, stays))

    value_pieces = []
    for j in range(2):
        piece = jnp.where(tile // 2 == (head // 2) ^ j, stays, comes)
        value_pieces.append(
            moved(piece, lambda t, h: (t // 2 * 2 + outer_core(h), t % 2 + 2 * ((h // 2) ^ j)))
        )
    key_other = swapped(key_block, "tile", 2)
    bias_part = add_columns(bias_rows[None], kv_weight)
    value_pieces, key_block, key_other, bias_part = step(
        (value_pieces, key_block, key_other, bias_part)
    )

    key_near = put_first(tile // 2 == head // 2, key_block, key_other, 1)
    value_half = jnp.concatenate(value_pieces, axis=1)
    key_near, value_half = step((key_near, value_half))
    key_kept, key_parts = products(key_near, swapped(key_near, "tile", 1))
    bias_part = bias_part + swapped(bias_part, "tile", 1)
    key_kept, key_parts, value_half, bias_part = step((key_kept, key_parts, value_half, bias_part))

    key_arrived = exchange(key_parts)
    value_other = swapped(value_half, "tile", 2)
    bias_part = bias_part + swapped(bias_part, "tile", 2)
    value_near = put_first(first_chip, value_half, value_other, 0)
    value_kept, value_parts = products(value_near, swapped(value_near, "tile", 1))
    key_kept, key_arrived, value_kept, value_parts, bias_part = step(
        (key_kept, key_arrived, value_kept, value_parts, bias_part)
    )
    bias_part = bias_part.reshape(2, layers, 2, head_dim)

    value_arrived = exchange(value_parts)
    own = summed(key_kept, key_arrived)
    across_x, across_y = step((swapped(own, "tile", 2), swapped(own, "groups", 1)))
    rows_0 = step(both_heads(own, across_y))
    rows_1, diagonal = step((swapped(rows_0, "tile", 1), swapped(across_y, "tile", 2)))
    rows_2 = step(both_heads(across_x, diagonal))
    total = times_features(rows_0, 0) + times_features(rows_1, 1)
    total = total + times_features(rows_2, 2) + times_features(swapped(rows_2, "tile", 1), 3)
    keys = finish(total, 0)
    keys, value_kept, value_arrived = step((keys, value_kept, value_arrived))

    own = summed(value_kept, value_arrived)
    own, across_x, across_y, shifted, keys = step(
        (
            own,
            swapped(own, "tile", 2),
            swapped(own, "groups", 1),
            shifted_2(keys, "head", 1),
            keys,
        )
    )

    keys = rolled(keys, shifted, 1)
    rows_0, keys = step((both_heads(own, across_y), keys))
    shifted, diagonal = shifted_2(keys, "head", 2), swapped(across_x, "groups", 1)
    total = times_features(rows_0, 0) + times_features(swapped(rows_0, "tile", 1), 1)
    rows_2 = step(both_heads(across_x, diagonal))
    total = total + times_features(rows_2, 2) + times_features(swapped(rows_2, "tile", 1), 3)
    values = finish(total, 1)
    shifted, values, keys = step((shifted, values, keys))

    picked = outgoing(rolled(keys, shifted, 2))
    arrived, shifted, values = step((to_owners(picked), shifted_2(values, "head", 1), values))

    values = rolled(values, shifted, 1)
    key_cache, shifted, values = step((in_order(arrived), shifted_2(values, "head", 2), values))

    value_cache = in_order(to_owners(outgoing(rolled(values, shifted, 2))))
    cache = jnp.stack([key_cache, value_cache], axis=-2)
    return cache.reshape(1, 1, most_tiles * 4 * shard_len, 4 * layers, head_dim)


def solution(mesh):
    placed = (
        P("groups", "tile", None),
        P("tile", "head"),
        P("head"),
        P("tile", "head"),
        P(),
        P("groups", None),
        P("groups"),
        P("groups"),
    )
    sizes = tuple(mesh.shape[name] for name in ("groups", "tile", "head"))
    return jax.shard_map(
        product_plan if sizes == (2, 4, 4) else gather_plan,
        mesh=mesh,
        in_specs=placed,
        out_specs=P(("groups", "tile"), "head", None, None, None),
        check_vma=False,
    )
```

```python
import jax
import jax.numpy as jnp
from jax import lax
from jax.sharding import PartitionSpec as P

eps_norm = 1e-05


def shifted_2(shard, axis, by):
    count = lax.axis_size(axis)
    return lax.ppermute(shard, axis, [(i, (i + by) % count) for i in range(count)])


def swapped(shard, axis, bit):
    return lax.ppermute(shard, axis, [(i, i ^ bit) for i in range(lax.axis_size(axis))])


def add_columns(operand, portion):
    return jnp.dot(operand, portion, preferred_element_type=jnp.float32)


def routing(tile_map, tile_count, decode_owner, tile_slots, head_groups):
    most_tiles = tile_map.shape[1]
    owner_tile = decode_owner // head_groups
    owner_turn = decode_owner % head_groups
    usable = jnp.arange(most_tiles)[None, :] < tile_count[:, None]
    matched = (tile_map[:, :, None] == jnp.arange(tile_slots)[None, None, :]) & usable[:, :, None]
    return owner_tile, owner_turn, matched


def gather_plan(
    features, proj_weight, proj_bias, kv_weight, key_gain, tile_map, tile_count, decode_owner
):
    tile_slots, shard_len, feature_width = features.shape
    token_rows = tile_slots * shard_len
    feature_rows = features.reshape(token_rows, feature_width)
    weight_cols = lax.all_gather(proj_weight, "tile", axis=0, tiled=True)
    projected = jnp.dot(feature_rows, weight_cols, preferred_element_type=jnp.float32)
    projected_local = (projected + proj_bias.astype(jnp.float32)).astype(jnp.bfloat16)
    kv_width = kv_weight.shape[1]
    projected_all = lax.all_gather(projected_local, "head", axis=1, tiled=True)
    key_value = add_columns(projected_all, lax.all_gather(kv_weight, "tile", axis=0, tiled=True))
    layers, head_dim = key_gain.shape
    blocks = key_value.reshape(token_rows, -1, layers, 2, head_dim)
    keys_raw = blocks[:, :, :, 0]
    inv_rms = lax.rsqrt(jnp.mean(keys_raw * keys_raw, axis=-1, keepdims=True) + eps_norm)
    keys_normed = keys_raw * inv_rms * key_gain[None, None]
    stacked = jnp.stack([keys_normed, blocks[:, :, :, 1]], axis=3).astype(jnp.bfloat16)
    per_tile = stacked.reshape(tile_slots, shard_len * kv_width)
    tile_ranks = lax.axis_size("tile")
    head_groups = lax.axis_size("head")
    most_tiles = tile_map.shape[1]
    owner_tile, owner_turn, matched = routing(
        tile_map, tile_count, decode_owner, tile_slots, head_groups
    )
    owned_by = (owner_tile[:, None] == jnp.arange(tile_ranks)[None, :]).astype(jnp.float32)
    selector = jnp.einsum("rd,rjs->jds", owned_by, matched.astype(jnp.float32))
    selector = selector.astype(jnp.bfloat16).reshape(most_tiles * tile_ranks, tile_slots)
    outgoing = add_columns(selector, per_tile).astype(jnp.bfloat16)
    outgoing = outgoing.reshape(most_tiles, tile_ranks, shard_len, kv_width)
    arrived = lax.all_to_all(outgoing, "tile", split_axis=1, concat_axis=1, tiled=True)
    gathered_rows = arrived.reshape(
        most_tiles * tile_ranks * shard_len, kv_width // head_dim, head_dim
    )
    my_turn = jnp.sum(jnp.where(owner_tile == lax.axis_index("tile"), owner_turn, 0))
    stride = 1
    while stride < head_groups:
        shifted = shifted_2(gathered_rows, "head", stride)
        gathered_rows = jnp.where(my_turn // stride % 2 == 1, shifted, gathered_rows)
        stride = stride * 2
    return gathered_rows[None, None]


def product_plan(
    features, proj_weight, proj_bias, kv_weight, key_gain, tile_map, tile_count, decode_owner
):
    tile_slots, shard_len, feature_width = features.shape
    token_rows = tile_slots * shard_len
    depth = proj_weight.shape[0]
    layers, head_dim = key_gain.shape
    width = layers * head_dim
    most_tiles = tile_map.shape[1]
    group, tile, head = (lax.axis_index(name) for name in ("groups", "tile", "head"))
    first_core, first_chip = tile % 2 == 0, tile < 2
    at_end = (head == 0) | (head == 3)
    feature_rows = features.reshape(token_rows, feature_width)
    step = lax.optimization_barrier

    def moved(shard, target):
        pairs = []
        for t in range(4):
            for h in range(4):
                to_tile, to_head = target(t, h)
                pairs.append((t * 4 + h, to_tile * 4 + to_head))
        return lax.ppermute(shard, ("tile", "head"), pairs)

    def outer_core(h):
        return (h ^ h // 2) % 2

    def times_features(rows, r):
        columns = lax.dynamic_slice_in_dim(feature_rows, (tile ^ r) * depth, depth, axis=1)
        return add_columns(columns, rows)

    def put_first(condition, one, other, axis):
        return jnp.concatenate(
            [jnp.where(condition, one, other), jnp.where(condition, other, one)], axis=axis
        )

    def both_heads(ours, theirs):
        return put_first(group == 0, ours, theirs, 1)

    def products(near, far):
        both = add_columns(proj_weight, jnp.concatenate([near, far], axis=1))
        near_0, near_1, far_0, far_1 = (both[:, k * width : (k + 1) * width] for k in range(4))
        near_kept = at_end == first_core
        return (
            jnp.where(first_core, near_1, far_1).astype(jnp.bfloat16),
            jnp.where(first_core, far_1, near_1),
            jnp.where(near_kept, far_0, near_0),
            jnp.where(near_kept, near_0, far_0),
        )

    def neighbours(block):
        return swapped(block.astype(jnp.bfloat16), "head", 1)

    def middle(block):
        return moved(block.astype(jnp.bfloat16), lambda t, h: (t, (0, 2, 1, 3)[h]))

    def plus(block, arrived):
        return block.astype(jnp.float32) + arrived.astype(jnp.float32)

    def finish(total, part):
        finished = []
        for k in range(2):
            entries = total[:, k * width : (k + 1) * width].reshape(token_rows, layers, head_dim)
            entries = entries + bias_part[k, :, part][None]
            if part == 0:
                squares = jnp.mean(entries * entries, axis=-1, keepdims=True)
                entries = entries * lax.rsqrt(squares + eps_norm) * key_gain[None]
            finished.append(entries.reshape(token_rows, width).astype(jnp.bfloat16))
        return jnp.concatenate(finished, axis=1).reshape(tile_slots, shard_len, 2 * width)

    owner_tile, owner_turn, matched = routing(tile_map, tile_count, decode_owner, tile_slots, 4)
    turn_of = jnp.sum(jnp.where(matched, owner_turn[:, None, None], 0), axis=(0, 1))
    owned_by = (owner_tile[:, None] == (tile ^ jnp.arange(4))[None, :]).astype(jnp.float32)
    selector = jnp.einsum("rd,rjs->djs", owned_by, matched.astype(jnp.float32))
    selector = selector.astype(jnp.bfloat16).reshape(4 * most_tiles, tile_slots)

    def rolled(rows, shifted, stride):
        odd = (turn_of // stride % 2 == 1)[:, None, None]
        return jnp.where(odd, shifted, rows)

    def outgoing(rows):
        picked = add_columns(selector, rows.reshape(tile_slots, -1)).astype(jnp.bfloat16)
        picked = picked.reshape(4, most_tiles, shard_len, 2, layers, head_dim)
        return [picked[r] for r in range(4)]

    def to_owners(picked):
        return [picked[0]] + [swapped(picked[r], "tile", r) for r in (1, 2, 3)]

    def in_order(arrived):
        even = [jnp.where(first_core, arrived[r], arrived[r ^ 1]) for r in range(4)]
        ranked = [jnp.where(first_chip, even[r], even[r ^ 2]) for r in range(4)]
        return jnp.stack(ranked, axis=1)

    column, half = group * 2 * head_dim, kv_weight.shape[0] // 2
    key_mine = lax.dynamic_slice_in_dim(kv_weight, column, head_dim, axis=1)
    value_mine = lax.dynamic_slice_in_dim(kv_weight, column + head_dim, head_dim, axis=1)
    stays = lax.dynamic_slice_in_dim(value_mine, tile // 2 * half, half, axis=0)
    leaves = lax.dynamic_slice_in_dim(value_mine, half - tile // 2 * half, half, axis=0)
    bias_rows = moved(proj_bias, lambda t, h: (h, t))
    key_block = moved(key_mine, lambda t, h: (h // 2 * 2 + outer_core(h), t))
    comes = swapped(leaves, "tile", 2)
    bias_rows, key_block, comes, stays = step((bias_rows, key_block, comes, stays))

    value_pieces = []
    for j in range(2):
        piece = jnp.where(tile // 2 == (head // 2) ^ j, stays, comes)
        value_pieces.append(
            moved(piece, lambda t, h: (t // 2 * 2 + outer_core(h), t % 2 + 2 * ((h // 2) ^ j)))
        )
    key_other = swapped(key_block, "tile", 2)
    bias_part = add_columns(bias_rows[None], kv_weight)
    value_pieces, key_block, key_other, bias_part = step(
        (value_pieces, key_block, key_other, bias_part)
    )

    key_near = put_first(tile // 2 == head // 2, key_block, key_other, 1)
    value_half = jnp.concatenate(value_pieces, axis=1)
    key_near, value_half = step((key_near, value_half))
    first, second, third, own = products(key_near, swapped(key_near, "tile", 1))
    bias_part = bias_part + swapped(bias_part, "tile", 1)
    first, second, third, own, value_half, bias_part = step(
        (first, second, third, own, value_half, bias_part)
    )

    in_1, value_other, bias_other = step(
        (neighbours(first), swapped(value_half, "tile", 2), swapped(bias_part, "tile", 2))
    )
    bias_part = (bias_part + bias_other).reshape(2, layers, 2, head_dim)

    value_near = put_first(first_chip, value_half, value_other, 0)
    relayed = plus(first, in_1).astype(jnp.bfloat16)
    value_near, relayed = step((value_near, relayed))
    in_2, across_2 = neighbours(second), middle(relayed)
    value_products = products(value_near, swapped(value_near, "tile", 1))
    in_2, across_2, value_products = step((in_2, across_2, value_products))

    relayed = jnp.where(at_end, third, plus(third, across_2)).astype(jnp.bfloat16)
    in_3, across_3 = step((neighbours(relayed), middle(plus(second, in_2))))
    own = plus(own, in_3) + jnp.where(at_end, 0.0, across_3.astype(jnp.float32))
    own = own.astype(jnp.bfloat16)

    first, second, third, value_own = value_products
    in_1, across_x, across_y = step(
        (neighbours(first), swapped(own, "tile", 2), swapped(own, "groups", 1))
    )

    rows_0, relayed = step((both_heads(own, across_y), plus(first, in_1).astype(jnp.bfloat16)))
    in_2, across_2, diagonal, rows_1 = step(
        (
            neighbours(second),
            middle(relayed),
            swapped(across_y, "tile", 2),
            swapped(rows_0, "tile", 1),
        )
    )

    relayed = jnp.where(at_end, third, plus(third, across_2)).astype(jnp.bfloat16)
    rows_2, relayed = step((both_heads(across_x, diagonal), relayed))
    in_3, across_3 = neighbours(relayed), middle(plus(second, in_2))
    total = times_features(rows_0, 0) + times_features(rows_1, 1)
    total = total + times_features(rows_2, 2) + times_features(swapped(rows_2, "tile", 1), 3)
    keys = finish(total, 0)
    in_3, across_3, keys = step((in_3, across_3, keys))
    own = plus(value_own, in_3) + jnp.where(at_end, 0.0, across_3.astype(jnp.float32))
    own = own.astype(jnp.bfloat16)

    shifted, across_x, across_y = step(
        (shifted_2(keys, "head", 1), swapped(own, "tile", 2), swapped(own, "groups", 1))
    )

    rows_0, keys = step((both_heads(own, across_y), rolled(keys, shifted, 1)))
    shifted, diagonal, rows_1 = step(
        (
            shifted_2(keys, "head", 2),
            swapped(across_x, "groups", 1),
            swapped(rows_0, "tile", 1),
        )
    )

    rows_2, keys = step((both_heads(across_x, diagonal), rolled(keys, shifted, 2)))
    total = times_features(rows_0, 0) + times_features(rows_1, 1)
    total = total + times_features(rows_2, 2) + times_features(swapped(rows_2, "tile", 1), 3)
    values = finish(total, 1)
    picked, values = step((outgoing(keys), values))

    arrived, shifted = step((to_owners(picked), shifted_2(values, "head", 1)))

    values = step(rolled(values, shifted, 1))
    key_cache, shifted = step((in_order(arrived), shifted_2(values, "head", 2)))

    value_cache = in_order(to_owners(outgoing(rolled(values, shifted, 2))))
    cache = jnp.stack([key_cache, value_cache], axis=-2)
    return cache.reshape(1, 1, most_tiles * 4 * shard_len, 4 * layers, head_dim)


def solution(mesh):
    placed = (
        P("groups", "tile", None),
        P("tile", "head"),
        P("head"),
        P("tile", "head"),
        P(),
        P("groups", None),
        P("groups"),
        P("groups"),
    )
    sizes = tuple(mesh.shape[name] for name in ("groups", "tile", "head"))
    return jax.shard_map(
        product_plan if sizes == (2, 4, 4) else gather_plan,
        mesh=mesh,
        in_specs=placed,
        out_specs=P(("groups", "tile"), "head", None, None, None),
        check_vma=False,
    )
```

```python
import jax
import jax.numpy as jnp
from jax import lax
from jax.sharding import PartitionSpec as P

eps_norm = 1e-05


def shifted_2(shard, axis, by):
    count = lax.axis_size(axis)
    return lax.ppermute(shard, axis, [(i, (i + by) % count) for i in range(count)])


def swapped(shard, axis, bit):
    return lax.ppermute(shard, axis, [(i, i ^ bit) for i in range(lax.axis_size(axis))])


def add_columns(operand, portion):
    return jnp.dot(operand, portion, preferred_element_type=jnp.float32)


def routing(tile_map, tile_count, decode_owner, tile_slots, head_groups):
    most_tiles = tile_map.shape[1]
    owner_tile = decode_owner // head_groups
    owner_turn = decode_owner % head_groups
    usable = jnp.arange(most_tiles)[None, :] < tile_count[:, None]
    matched = (tile_map[:, :, None] == jnp.arange(tile_slots)[None, None, :]) & usable[:, :, None]
    return owner_tile, owner_turn, matched


def gather_plan(
    features, proj_weight, proj_bias, kv_weight, key_gain, tile_map, tile_count, decode_owner
):
    tile_slots, shard_len, feature_width = features.shape
    token_rows = tile_slots * shard_len
    feature_rows = features.reshape(token_rows, feature_width)
    weight_cols = lax.all_gather(proj_weight, "tile", axis=0, tiled=True)
    projected = jnp.dot(feature_rows, weight_cols, preferred_element_type=jnp.float32)
    projected_local = (projected + proj_bias.astype(jnp.float32)).astype(jnp.bfloat16)
    kv_width = kv_weight.shape[1]
    projected_all = lax.all_gather(projected_local, "head", axis=1, tiled=True)
    key_value = add_columns(projected_all, lax.all_gather(kv_weight, "tile", axis=0, tiled=True))
    layers, head_dim = key_gain.shape
    blocks = key_value.reshape(token_rows, -1, layers, 2, head_dim)
    keys_raw = blocks[:, :, :, 0]
    inv_rms = lax.rsqrt(jnp.mean(keys_raw * keys_raw, axis=-1, keepdims=True) + eps_norm)
    keys_normed = keys_raw * inv_rms * key_gain[None, None]
    stacked = jnp.stack([keys_normed, blocks[:, :, :, 1]], axis=3).astype(jnp.bfloat16)
    per_tile = stacked.reshape(tile_slots, shard_len * kv_width)
    tile_ranks = lax.axis_size("tile")
    head_groups = lax.axis_size("head")
    most_tiles = tile_map.shape[1]
    owner_tile, owner_turn, matched = routing(
        tile_map, tile_count, decode_owner, tile_slots, head_groups
    )
    owned_by = (owner_tile[:, None] == jnp.arange(tile_ranks)[None, :]).astype(jnp.float32)
    selector = jnp.einsum("rd,rjs->jds", owned_by, matched.astype(jnp.float32))
    selector = selector.astype(jnp.bfloat16).reshape(most_tiles * tile_ranks, tile_slots)
    outgoing = add_columns(selector, per_tile).astype(jnp.bfloat16)
    outgoing = outgoing.reshape(most_tiles, tile_ranks, shard_len, kv_width)
    arrived = lax.all_to_all(outgoing, "tile", split_axis=1, concat_axis=1, tiled=True)
    gathered_rows = arrived.reshape(
        most_tiles * tile_ranks * shard_len, kv_width // head_dim, head_dim
    )
    my_turn = jnp.sum(jnp.where(owner_tile == lax.axis_index("tile"), owner_turn, 0))
    stride = 1
    while stride < head_groups:
        shifted = shifted_2(gathered_rows, "head", stride)
        gathered_rows = jnp.where(my_turn // stride % 2 == 1, shifted, gathered_rows)
        stride = stride * 2
    return gathered_rows[None, None]


def product_plan(
    features, proj_weight, proj_bias, kv_weight, key_gain, tile_map, tile_count, decode_owner
):
    tile_slots, shard_len, feature_width = features.shape
    token_rows = tile_slots * shard_len
    depth = proj_weight.shape[0]
    layers, head_dim = key_gain.shape
    width = layers * head_dim
    most_tiles = tile_map.shape[1]
    group, tile, head = (lax.axis_index(name) for name in ("groups", "tile", "head"))
    first_core, first_chip = tile % 2 == 0, tile < 2
    at_end = (head == 0) | (head == 3)
    feature_rows = features.reshape(token_rows, feature_width)
    step = lax.optimization_barrier

    def moved(shard, target):
        pairs = []
        for t in range(4):
            for h in range(4):
                to_tile, to_head = target(t, h)
                pairs.append((t * 4 + h, to_tile * 4 + to_head))
        return lax.ppermute(shard, ("tile", "head"), pairs)

    def outer_core(h):
        return (h ^ h // 2) % 2

    def times_features(rows, r):
        columns = lax.dynamic_slice_in_dim(feature_rows, (tile ^ r) * depth, depth, axis=1)
        return add_columns(columns, rows)

    def put_first(condition, one, other, axis):
        return jnp.concatenate(
            [jnp.where(condition, one, other), jnp.where(condition, other, one)], axis=axis
        )

    def both_heads(ours, theirs):
        return put_first(group == 0, ours, theirs, 1)

    def products(near, far):
        both = add_columns(proj_weight, jnp.concatenate([near, far], axis=1))
        near_0, near_1, far_0, far_1 = (both[:, k * width : (k + 1) * width] for k in range(4))
        near_kept = at_end == first_core
        parts = (
            jnp.where(near_kept, far_1, near_1),
            jnp.where(near_kept, near_1, far_1),
            jnp.where(near_kept, far_0, near_0),
        )
        own = jnp.where(near_kept, near_0, far_0)
        return own, tuple(part.astype(jnp.bfloat16) for part in parts)

    def exchange(parts):
        return tuple(swapped(part, "head", bit) for part, bit in zip(parts, (2, 3, 1)))

    def summed(own, arrived):
        for block in arrived:
            own = own + block.astype(jnp.float32)
        return own.astype(jnp.bfloat16)

    once = jnp.minimum(jnp.max(tile_count), 1)

    def in_loop(chain, given):
        shapes = jax.eval_shape(chain, given)[1]
        empty = jax.tree.map(lambda x: jnp.zeros(x.shape, x.dtype), shapes)
        return lax.fori_loop(0, once, lambda _, carry: chain(carry[0]), (given, empty))[1]

    def finish(total, part):
        finished = []
        for k in range(2):
            entries = total[:, k * width : (k + 1) * width].reshape(token_rows, layers, head_dim)
            entries = entries + bias_part[k, :, part][None]
            if part == 0:
                squares = jnp.mean(entries * entries, axis=-1, keepdims=True)
                entries = entries * lax.rsqrt(squares + eps_norm) * key_gain[None]
            finished.append(entries.reshape(token_rows, width).astype(jnp.bfloat16))
        return jnp.concatenate(finished, axis=1).reshape(tile_slots, shard_len, 2 * width)

    owner_tile, owner_turn, matched = routing(tile_map, tile_count, decode_owner, tile_slots, 4)
    turn_of = jnp.sum(jnp.where(matched, owner_turn[:, None, None], 0), axis=(0, 1))
    owned_by = (owner_tile[:, None] == (tile ^ jnp.arange(4))[None, :]).astype(jnp.float32)
    selector = jnp.einsum("rd,rjs->djs", owned_by, matched.astype(jnp.float32))
    selector = selector.astype(jnp.bfloat16).reshape(4 * most_tiles, tile_slots)

    def rolled(rows, shifted, stride):
        odd = (turn_of // stride % 2 == 1)[:, None, None]
        return jnp.where(odd, shifted, rows)

    def outgoing(rows):
        picked = add_columns(selector, rows.reshape(tile_slots, -1)).astype(jnp.bfloat16)
        picked = picked.reshape(4, most_tiles, shard_len, 2, layers, head_dim)
        return [picked[r] for r in range(4)]

    def to_owners(picked):
        return [picked[0]] + [swapped(picked[r], "tile", r) for r in (1, 2, 3)]

    def in_order(arrived):
        even = [jnp.where(first_core, arrived[r], arrived[r ^ 1]) for r in range(4)]
        ranked = [jnp.where(first_chip, even[r], even[r ^ 2]) for r in range(4)]
        return jnp.stack(ranked, axis=1)

    column, half = group * 2 * head_dim, kv_weight.shape[0] // 2

    def to_planes(part):
        mine = lax.dynamic_slice_in_dim(kv_weight, column + part * head_dim, head_dim, axis=1)
        return (
            moved(mine[:half], lambda t, h: (h // 2 * 2 + outer_core(h), t)),
            moved(mine[half:], lambda t, h: ((1 - h // 2) * 2 + outer_core(h), t)),
        )

    def across(rows):
        return swapped(jnp.concatenate(rows, axis=0), "tile", 2)

    def with_other(rows, other):
        one = jnp.concatenate([rows[0], other[half:]], axis=0)
        two = jnp.concatenate([other[:half], rows[1]], axis=0)
        return put_first(tile // 2 == head // 2, one, two, 1)

    bias_rows = moved(proj_bias, lambda t, h: (h, t))
    bias_rows, key_rows = step((bias_rows, to_planes(0)))

    bias_part = add_columns(bias_rows[None], kv_weight)
    value_rows, key_rows, key_other, bias_part = step(
        (to_planes(1), key_rows, across(key_rows), bias_part)
    )

    key_near = step(with_other(key_rows, key_other))
    own, parts = products(key_near, swapped(key_near, "tile", 1))
    bias_part = bias_part + swapped(bias_part, "tile", 1)
    own, parts, value_rows, bias_part = step((own, parts, value_rows, bias_part))

    def values_product(given):
        rows, bias = given
        other, bias_other = step((across(rows), swapped(bias, "tile", 2)))
        near = step(with_other(rows, other))
        given = (other[:half], other[half:]), bias_other
        return given, (products(near, swapped(near, "tile", 1)), bias + bias_other)

    arrived, beside = step((exchange(parts), in_loop(values_product, (value_rows, bias_part))))
    own = summed(own, arrived)
    (value_own, parts), bias_part = beside
    bias_part = bias_part.reshape(2, layers, 2, head_dim)

    def keys_product(own):
        across_x, across_y = step((swapped(own, "tile", 2), swapped(own, "groups", 1)))
        rows_0 = step(both_heads(own, across_y))
        diagonal, rows_1 = step((swapped(across_y, "tile", 2), swapped(rows_0, "tile", 1)))
        rows_2 = step(both_heads(across_x, diagonal))
        total = times_features(rows_0, 0) + times_features(rows_1, 1)
        total = total + times_features(rows_2, 2) + times_features(swapped(rows_2, "tile", 1), 3)
        return across_x, finish(total, 0)

    arrived, keys = step((exchange(parts), in_loop(keys_product, own)))
    own = summed(value_own, arrived)

    shifted, across_x, across_y = step(
        (shifted_2(keys, "head", 1), swapped(own, "tile", 2), swapped(own, "groups", 1))
    )

    rows_0, keys = step((both_heads(own, across_y), rolled(keys, shifted, 1)))
    shifted, diagonal, rows_1 = step(
        (
            shifted_2(keys, "head", 2),
            swapped(across_x, "groups", 1),
            swapped(rows_0, "tile", 1),
        )
    )

    rows_2, keys = step((both_heads(across_x, diagonal), rolled(keys, shifted, 2)))
    total = times_features(rows_0, 0) + times_features(rows_1, 1)
    total = total + times_features(rows_2, 2) + times_features(swapped(rows_2, "tile", 1), 3)
    values = finish(total, 1)
    picked, values = step((outgoing(keys), values))

    arrived, shifted = step((to_owners(picked), shifted_2(values, "head", 1)))

    values = step(rolled(values, shifted, 1))
    key_cache, shifted = step((in_order(arrived), shifted_2(values, "head", 2)))

    value_cache = in_order(to_owners(outgoing(rolled(values, shifted, 2))))
    cache = jnp.stack([key_cache, value_cache], axis=-2)
    return cache.reshape(1, 1, most_tiles * 4 * shard_len, 4 * layers, head_dim)


def solution(mesh):
    placed = (
        P("groups", "tile", None),
        P("tile", "head"),
        P("head"),
        P("tile", "head"),
        P(),
        P("groups", None),
        P("groups"),
        P("groups"),
    )
    sizes = tuple(mesh.shape[name] for name in ("groups", "tile", "head"))
    return jax.shard_map(
        product_plan if sizes == (2, 4, 4) else gather_plan,
        mesh=mesh,
        in_specs=placed,
        out_specs=P(("groups", "tile"), "head", None, None, None),
        check_vma=False,
    )
```

```python
import jax
import jax.numpy as jnp
from jax import lax
from jax.sharding import PartitionSpec as P

eps_norm = 1e-05


def shifted_2(shard, axis, by):
    count = lax.axis_size(axis)
    return lax.ppermute(shard, axis, [(i, (i + by) % count) for i in range(count)])


def swapped(shard, axis, bit):
    return lax.ppermute(shard, axis, [(i, i ^ bit) for i in range(lax.axis_size(axis))])


def add_columns(operand, portion):
    return jnp.dot(operand, portion, preferred_element_type=jnp.float32)


def routing(tile_map, tile_count, decode_owner, tile_slots, head_groups):
    most_tiles = tile_map.shape[1]
    owner_tile = decode_owner // head_groups
    owner_turn = decode_owner % head_groups
    usable = jnp.arange(most_tiles)[None, :] < tile_count[:, None]
    matched = (tile_map[:, :, None] == jnp.arange(tile_slots)[None, None, :]) & usable[:, :, None]
    return owner_tile, owner_turn, matched


def gather_plan(
    features, proj_weight, proj_bias, kv_weight, key_gain, tile_map, tile_count, decode_owner
):
    tile_slots, shard_len, feature_width = features.shape
    token_rows = tile_slots * shard_len
    feature_rows = features.reshape(token_rows, feature_width)
    weight_cols = lax.all_gather(proj_weight, "tile", axis=0, tiled=True)
    projected = jnp.dot(feature_rows, weight_cols, preferred_element_type=jnp.float32)
    projected_local = (projected + proj_bias.astype(jnp.float32)).astype(jnp.bfloat16)
    kv_width = kv_weight.shape[1]
    projected_all = lax.all_gather(projected_local, "head", axis=1, tiled=True)
    key_value = add_columns(projected_all, lax.all_gather(kv_weight, "tile", axis=0, tiled=True))
    layers, head_dim = key_gain.shape
    blocks = key_value.reshape(token_rows, -1, layers, 2, head_dim)
    keys_raw = blocks[:, :, :, 0]
    inv_rms = lax.rsqrt(jnp.mean(keys_raw * keys_raw, axis=-1, keepdims=True) + eps_norm)
    keys_normed = keys_raw * inv_rms * key_gain[None, None]
    stacked = jnp.stack([keys_normed, blocks[:, :, :, 1]], axis=3).astype(jnp.bfloat16)
    per_tile = stacked.reshape(tile_slots, shard_len * kv_width)
    tile_ranks = lax.axis_size("tile")
    head_groups = lax.axis_size("head")
    most_tiles = tile_map.shape[1]
    owner_tile, owner_turn, matched = routing(
        tile_map, tile_count, decode_owner, tile_slots, head_groups
    )
    owned_by = (owner_tile[:, None] == jnp.arange(tile_ranks)[None, :]).astype(jnp.float32)
    selector = jnp.einsum("rd,rjs->jds", owned_by, matched.astype(jnp.float32))
    selector = selector.astype(jnp.bfloat16).reshape(most_tiles * tile_ranks, tile_slots)
    outgoing = add_columns(selector, per_tile).astype(jnp.bfloat16)
    outgoing = outgoing.reshape(most_tiles, tile_ranks, shard_len, kv_width)
    arrived = lax.all_to_all(outgoing, "tile", split_axis=1, concat_axis=1, tiled=True)
    gathered_rows = arrived.reshape(
        most_tiles * tile_ranks * shard_len, kv_width // head_dim, head_dim
    )
    my_turn = jnp.sum(jnp.where(owner_tile == lax.axis_index("tile"), owner_turn, 0))
    stride = 1
    while stride < head_groups:
        shifted = shifted_2(gathered_rows, "head", stride)
        gathered_rows = jnp.where(my_turn // stride % 2 == 1, shifted, gathered_rows)
        stride = stride * 2
    return gathered_rows[None, None]


def product_plan(
    features, proj_weight, proj_bias, kv_weight, key_gain, tile_map, tile_count, decode_owner
):
    tile_slots, shard_len, feature_width = features.shape
    token_rows = tile_slots * shard_len
    depth = proj_weight.shape[0]
    layers, head_dim = key_gain.shape
    width = layers * head_dim
    most_tiles = tile_map.shape[1]
    group, tile, head = (lax.axis_index(name) for name in ("groups", "tile", "head"))
    first_core, first_chip = tile % 2 == 0, tile < 2
    at_end = (head == 0) | (head == 3)
    feature_rows = features.reshape(token_rows, feature_width)
    step = lax.optimization_barrier

    def moved(shard, target):
        pairs = []
        for t in range(4):
            for h in range(4):
                to_tile, to_head = target(t, h)
                pairs.append((t * 4 + h, to_tile * 4 + to_head))
        return lax.ppermute(shard, ("tile", "head"), pairs)

    def outer_core(h):
        return (h ^ h // 2) % 2

    feature_parts = [
        lax.dynamic_slice_in_dim(feature_rows, (tile ^ r) * depth, depth, axis=1) for r in range(4)
    ]

    def put_first(condition, one, other, axis):
        return jnp.concatenate(
            [jnp.where(condition, one, other), jnp.where(condition, other, one)], axis=axis
        )

    def both_heads(ours, theirs):
        return put_first(group == 0, ours, theirs, 1)

    def products(near, far):
        both = add_columns(proj_weight, jnp.concatenate([near, far], axis=1))
        near_0, near_1, far_0, far_1 = (both[:, k * width : (k + 1) * width] for k in range(4))
        near_kept = at_end == first_core
        parts = (
            jnp.where(near_kept, far_1, near_1),
            jnp.where(near_kept, near_1, far_1),
            jnp.where(near_kept, far_0, near_0),
        )
        own = jnp.where(near_kept, near_0, far_0)
        return own, tuple(part.astype(jnp.bfloat16) for part in parts)

    def exchange(parts):
        return tuple(swapped(part, "head", bit) for part, bit in zip(parts, (2, 3, 1)))

    def summed(own, arrived):
        for block in arrived:
            own = own + block.astype(jnp.float32)
        return own.astype(jnp.bfloat16)

    once = jnp.minimum(jnp.max(tile_count), 1)

    def in_loop(chain, given, empty):
        return lax.fori_loop(0, once, lambda _, carry: chain(carry[0]), (given, empty))[1]

    def times_features(rows, parts):
        return sum(add_columns(parts[r], rows[r]) for r in range(4))

    def finish(total, part):
        finished = []
        for k in range(2):
            entries = total[:, k * width : (k + 1) * width].reshape(token_rows, layers, head_dim)
            entries = entries + bias_part[k, :, part][None]
            if part == 0:
                squares = jnp.mean(entries * entries, axis=-1, keepdims=True)
                entries = entries * lax.rsqrt(squares + eps_norm) * key_gain[None]
            finished.append(entries.reshape(token_rows, width).astype(jnp.bfloat16))
        return jnp.concatenate(finished, axis=1).reshape(tile_slots, shard_len, 2 * width)

    owner_tile, owner_turn, matched = routing(tile_map, tile_count, decode_owner, tile_slots, 4)
    turn_of = jnp.sum(jnp.where(matched, owner_turn[:, None, None], 0), axis=(0, 1))
    owned_by = (owner_tile[:, None] == (tile ^ jnp.arange(4))[None, :]).astype(jnp.float32)
    selector = jnp.einsum("rd,rjs->djs", owned_by, matched.astype(jnp.float32))
    selector = selector.astype(jnp.bfloat16).reshape(4 * most_tiles, tile_slots)

    def rolled(rows, shifted, stride):
        odd = (turn_of // stride % 2 == 1)[:, None, None]
        return jnp.where(odd, shifted, rows)

    def outgoing(rows):
        picked = add_columns(selector, rows.reshape(tile_slots, -1)).astype(jnp.bfloat16)
        picked = picked.reshape(4, most_tiles, shard_len, 2, layers, head_dim)
        return [picked[r] for r in range(4)]

    def to_owners(picked):
        return [picked[0]] + [swapped(picked[r], "tile", r) for r in (1, 2, 3)]

    def in_order(arrived):
        even = [jnp.where(first_core, arrived[r], arrived[r ^ 1]) for r in range(4)]
        ranked = [jnp.where(first_chip, even[r], even[r ^ 2]) for r in range(4)]
        return jnp.stack(ranked, axis=1)

    column, half = group * 2 * head_dim, kv_weight.shape[0] // 2
    key_mine = lax.dynamic_slice_in_dim(kv_weight, column, head_dim, axis=1)
    value_mine = lax.dynamic_slice_in_dim(kv_weight, column + head_dim, head_dim, axis=1)
    stays = lax.dynamic_slice_in_dim(value_mine, tile // 2 * half, half, axis=0)
    leaves = lax.dynamic_slice_in_dim(value_mine, half - tile // 2 * half, half, axis=0)
    bias_rows = moved(proj_bias, lambda t, h: (h, t))
    key_block = moved(key_mine, lambda t, h: (h // 2 * 2 + outer_core(h), t))
    comes = swapped(leaves, "tile", 2)
    no_block = jnp.zeros((depth, width), jnp.float32)
    no_terms = no_block, tuple(jnp.zeros((depth, width), jnp.bfloat16) for _ in range(3))
    no_tokens = tuple(
        jnp.zeros((tile_slots, shard_len, 2 * width), jnp.bfloat16) for _ in range(2)
    )
    bias_rows, key_block, comes, stays, feature_parts, no_terms, no_tokens, once = step(
        (bias_rows, key_block, comes, stays, feature_parts, no_terms, no_tokens, once)
    )

    value_pieces = []
    for j in range(2):
        piece = jnp.where(tile // 2 == (head // 2) ^ j, stays, comes)
        value_pieces.append(
            moved(piece, lambda t, h: (t // 2 * 2 + outer_core(h), t % 2 + 2 * ((h // 2) ^ j)))
        )
    key_other = swapped(key_block, "tile", 2)
    bias_part = add_columns(bias_rows[None], kv_weight)
    value_pieces, key_block, key_other, bias_part = step(
        (value_pieces, key_block, key_other, bias_part)
    )

    key_near = put_first(tile // 2 == head // 2, key_block, key_other, 1)
    value_half = jnp.concatenate(value_pieces, axis=1)
    key_near, value_half = step((key_near, value_half))
    own, parts = products(key_near, swapped(key_near, "tile", 1))
    bias_part = bias_part + swapped(bias_part, "tile", 1)
    own, parts, value_half, bias_part = step((own, parts, value_half, bias_part))

    def values_terms(given):
        value_half, bias_part = given
        other, bias_other = step((swapped(value_half, "tile", 2), swapped(bias_part, "tile", 2)))
        near = step(put_first(first_chip, value_half, other, 0))
        terms = products(near, swapped(near, "tile", 1))
        return (other, bias_other), (terms, bias_part + bias_other)

    empty = no_terms, bias_part
    arrived, beside = step(
        (exchange(parts), in_loop(values_terms, (value_half, bias_part), empty))
    )
    own = summed(own, arrived)
    (value_own, parts), bias_part = beside
    bias_part = bias_part.reshape(2, layers, 2, head_dim)

    def keys_product(own):
        across_x, across_y = step((swapped(own, "tile", 2), swapped(own, "groups", 1)))
        rows_0 = step(both_heads(own, across_y))
        diagonal, rows_1 = step((swapped(across_y, "tile", 2), swapped(rows_0, "tile", 1)))
        rows_2 = step(both_heads(across_x, diagonal))
        rows = [rows_0, rows_1, rows_2, swapped(rows_2, "tile", 1)]
        return across_x, finish(times_features(rows, feature_parts), 0)

    arrived, keys = step((exchange(parts), in_loop(keys_product, own, no_tokens[0])))
    own = summed(value_own, arrived)

    shifted, across_x, across_y = step(
        (shifted_2(keys, "head", 1), swapped(own, "tile", 2), swapped(own, "groups", 1))
    )

    def values_product(given):
        own, across_x, across_y = given
        rows_0 = step(both_heads(own, across_y))
        middle = depth // 2
        upper, lower, rows_1 = step(
            (
                swapped(across_x[:middle], "groups", 1),
                swapped(across_y[middle:], "tile", 2),
                swapped(rows_0, "tile", 1),
            )
        )
        rows_2 = step(both_heads(across_x, jnp.concatenate([upper, lower], axis=0)))
        rows = [rows_0, rows_1, rows_2, swapped(rows_2, "tile", 1)]
        total = times_features(rows, feature_parts)
        return (across_y, own, across_x), finish(total, 1)

    keys = step(rolled(keys, shifted, 1))
    values = in_loop(values_product, (own, across_x, across_y), no_tokens[1])
    shifted, values = step((shifted_2(keys, "head", 2), values))

    picked = outgoing(rolled(keys, shifted, 2))
    shifted, picked = step((shifted_2(values, "head", 1), picked))

    values = step(rolled(values, shifted, 1))
    arrived, shifted = step((to_owners(picked), shifted_2(values, "head", 2)))

    value_cache = in_order(to_owners(outgoing(rolled(values, shifted, 2))))
    cache = jnp.stack([in_order(arrived), value_cache], axis=-2)
    return cache.reshape(1, 1, most_tiles * 4 * shard_len, 4 * layers, head_dim)


def solution(mesh):
    placed = (
        P("groups", "tile", None),
        P("tile", "head"),
        P("head"),
        P("tile", "head"),
        P(),
        P("groups", None),
        P("groups"),
        P("groups"),
    )
    sizes = tuple(mesh.shape[name] for name in ("groups", "tile", "head"))
    return jax.shard_map(
        product_plan if sizes == (2, 4, 4) else gather_plan,
        mesh=mesh,
        in_specs=placed,
        out_specs=P(("groups", "tile"), "head", None, None, None),
        check_vma=False,
    )
```

```python
import jax
import jax.numpy as jnp
from jax import lax
from jax.experimental import pallas as pl
from jax.experimental.pallas import tpu as pltpu
from jax.sharding import PartitionSpec as P

eps_norm = 1e-05


def shifted_2(shard, axis, by):
    count = lax.axis_size(axis)
    return lax.ppermute(shard, axis, [(i, (i + by) % count) for i in range(count)])


def swapped(shard, axis, bit):
    return lax.ppermute(shard, axis, [(i, i ^ bit) for i in range(lax.axis_size(axis))])


def add_columns(operand, portion):
    return jnp.dot(operand, portion, preferred_element_type=jnp.float32)


def routing(tile_map, tile_count, decode_owner, tile_slots, head_groups):
    most_tiles = tile_map.shape[1]
    owner_tile = decode_owner // head_groups
    owner_turn = decode_owner % head_groups
    usable = jnp.arange(most_tiles)[None, :] < tile_count[:, None]
    matched = (tile_map[:, :, None] == jnp.arange(tile_slots)[None, None, :]) & usable[:, :, None]
    return owner_tile, owner_turn, matched


def gather_plan(
    features, proj_weight, proj_bias, kv_weight, key_gain, tile_map, tile_count, decode_owner
):
    tile_slots, shard_len, feature_width = features.shape
    token_rows = tile_slots * shard_len
    feature_rows = features.reshape(token_rows, feature_width)
    weight_cols = lax.all_gather(proj_weight, "tile", axis=0, tiled=True)
    projected = jnp.dot(feature_rows, weight_cols, preferred_element_type=jnp.float32)
    projected_local = (projected + proj_bias.astype(jnp.float32)).astype(jnp.bfloat16)
    kv_width = kv_weight.shape[1]
    projected_all = lax.all_gather(projected_local, "head", axis=1, tiled=True)
    key_value = add_columns(projected_all, lax.all_gather(kv_weight, "tile", axis=0, tiled=True))
    layers, head_dim = key_gain.shape
    blocks = key_value.reshape(token_rows, -1, layers, 2, head_dim)
    keys_raw = blocks[:, :, :, 0]
    inv_rms = lax.rsqrt(jnp.mean(keys_raw * keys_raw, axis=-1, keepdims=True) + eps_norm)
    keys_normed = keys_raw * inv_rms * key_gain[None, None]
    stacked = jnp.stack([keys_normed, blocks[:, :, :, 1]], axis=3).astype(jnp.bfloat16)
    per_tile = stacked.reshape(tile_slots, shard_len * kv_width)
    tile_ranks = lax.axis_size("tile")
    head_groups = lax.axis_size("head")
    most_tiles = tile_map.shape[1]
    owner_tile, owner_turn, matched = routing(
        tile_map, tile_count, decode_owner, tile_slots, head_groups
    )
    owned_by = (owner_tile[:, None] == jnp.arange(tile_ranks)[None, :]).astype(jnp.float32)
    selector = jnp.einsum("rd,rjs->jds", owned_by, matched.astype(jnp.float32))
    selector = selector.astype(jnp.bfloat16).reshape(most_tiles * tile_ranks, tile_slots)
    outgoing = add_columns(selector, per_tile).astype(jnp.bfloat16)
    outgoing = outgoing.reshape(most_tiles, tile_ranks, shard_len, kv_width)
    arrived = lax.all_to_all(outgoing, "tile", split_axis=1, concat_axis=1, tiled=True)
    gathered_rows = arrived.reshape(
        most_tiles * tile_ranks * shard_len, kv_width // head_dim, head_dim
    )
    my_turn = jnp.sum(jnp.where(owner_tile == lax.axis_index("tile"), owner_turn, 0))
    stride = 1
    while stride < head_groups:
        shifted = shifted_2(gathered_rows, "head", stride)
        gathered_rows = jnp.where(my_turn // stride % 2 == 1, shifted, gathered_rows)
        stride = stride * 2
    return gathered_rows[None, None]


def terms_body(choice, ours, others, near_ours, near_others, far_ours, far_others, own, *parts):
    near = add_columns(ours[...], near_ours[...]) + add_columns(others[...], near_others[...])
    far = add_columns(ours[...], far_ours[...]) + add_columns(others[...], far_others[...])
    width = own.shape[1]
    near_kept = choice[0] == 1
    kept, sent = jnp.where(near_kept, near, far), jnp.where(near_kept, far, near)
    own[...] = kept[:, :width]
    blocks = (sent[:, width:], kept[:, width:], sent[:, :width])
    for part, block in zip(parts, blocks):
        part[...] = block.astype(part.dtype)


def product_terms(choice, weight, near, far):
    depth, rows = weight.shape
    half, columns = rows // 2, near[0].shape[1]
    width = columns // 2
    tall = 240 if depth % 240 == 0 else depth
    whole = pl.BlockSpec((half, columns), lambda i, choice: (0, 0))
    narrow = pl.BlockSpec((tall, width), lambda i, choice: (i, 0))
    shapes = [jax.ShapeDtypeStruct((depth, width), t) for t in (jnp.float32,) + 3 * (jnp.bfloat16,)]
    return pl.pallas_call(
        terms_body,
        out_shape=shapes,
        grid_spec=pltpu.PrefetchScalarGridSpec(
            num_scalar_prefetch=1,
            grid=(depth // tall,),
            in_specs=[
                pl.BlockSpec((tall, half), lambda i, choice: (i, choice[1])),
                pl.BlockSpec((tall, half), lambda i, choice: (i, 1 - choice[1])),
                whole,
                whole,
                whole,
                whole,
            ],
            out_specs=[narrow] * 4,
        ),
        compiler_params=pltpu.CompilerParams(vmem_limit_bytes=32 * 1024 * 1024),
        cost_estimate=pl.CostEstimate(
            flops=4 * depth * rows * columns,
            bytes_accessed=2 * depth * rows + 4 * rows * columns + 10 * depth * width,
            transcendentals=0,
        ),
    )(choice, weight, weight, *near, *far)


def product_plan(
    features, proj_weight, proj_bias, kv_weight, key_gain, tile_map, tile_count, decode_owner
):
    tile_slots, shard_len, feature_width = features.shape
    token_rows = tile_slots * shard_len
    depth = proj_weight.shape[0]
    layers, head_dim = key_gain.shape
    width = layers * head_dim
    most_tiles = tile_map.shape[1]
    group, tile, head = (lax.axis_index(name) for name in ("groups", "tile", "head"))
    first_core, first_chip = tile % 2 == 0, tile < 2
    at_end = (head == 0) | (head == 3)
    feature_rows = features.reshape(token_rows, feature_width)
    step = lax.optimization_barrier

    def moved(shard, target):
        pairs = []
        for t in range(4):
            for h in range(4):
                to_tile, to_head = target(t, h)
                pairs.append((t * 4 + h, to_tile * 4 + to_head))
        return lax.ppermute(shard, ("tile", "head"), pairs)

    def outer_core(h):
        return (h ^ h // 2) % 2

    feature_parts = [
        lax.dynamic_slice_in_dim(feature_rows, (tile ^ r) * depth, depth, axis=1) for r in range(4)
    ]

    def put_first(condition, one, other, axis):
        return jnp.concatenate(
            [jnp.where(condition, one, other), jnp.where(condition, other, one)], axis=axis
        )

    def both_heads(ours, theirs):
        return put_first(group == 0, ours, theirs, 1)

    choice = jnp.stack([(at_end == first_core).astype(jnp.int32), head // 2])

    def products(near, far):
        own, *parts = product_terms(choice, proj_weight, near, far)
        return own, tuple(parts)

    def exchange(parts):
        return tuple(swapped(part, "head", bit) for part, bit in zip(parts, (2, 3, 1)))

    def summed(own, arrived):
        for block in arrived:
            own = own + block.astype(jnp.float32)
        return own.astype(jnp.bfloat16)

    once = jnp.minimum(jnp.max(tile_count), 1)

    def in_loop(chain, given, empty):
        return lax.fori_loop(0, once, lambda _, carry: chain(carry[0]), (given, empty))[1]

    def times_features(rows, parts):
        return sum(add_columns(parts[r], rows[r]) for r in range(4))

    def finish(total, part):
        finished = []
        for k in range(2):
            entries = total[:, k * width : (k + 1) * width].reshape(token_rows, layers, head_dim)
            entries = entries + bias_part[k, :, part][None]
            if part == 0:
                squares = jnp.mean(entries * entries, axis=-1, keepdims=True)
                entries = entries * lax.rsqrt(squares + eps_norm) * key_gain[None]
            finished.append(entries.reshape(token_rows, width).astype(jnp.bfloat16))
        return jnp.concatenate(finished, axis=1).reshape(tile_slots, shard_len, 2 * width)

    owner_tile, owner_turn, matched = routing(tile_map, tile_count, decode_owner, tile_slots, 4)
    turn_of = jnp.sum(jnp.where(matched, owner_turn[:, None, None], 0), axis=(0, 1))
    owned_by = (owner_tile[:, None] == (tile ^ jnp.arange(4))[None, :]).astype(jnp.float32)
    selector = jnp.einsum("rd,rjs->djs", owned_by, matched.astype(jnp.float32))
    selector = selector.astype(jnp.bfloat16).reshape(4 * most_tiles, tile_slots)

    def rolled(rows, shifted, stride):
        odd = (turn_of // stride % 2 == 1)[:, None, None]
        return jnp.where(odd, shifted, rows)

    def outgoing(rows):
        picked = add_columns(selector, rows.reshape(tile_slots, -1)).astype(jnp.bfloat16)
        picked = picked.reshape(4, most_tiles, shard_len, 2, layers, head_dim)
        return [picked[r] for r in range(4)]

    def to_owners(picked):
        return [picked[0]] + [swapped(picked[r], "tile", r) for r in (1, 2, 3)]

    def in_order(arrived):
        even = [jnp.where(first_core, arrived[r], arrived[r ^ 1]) for r in range(4)]
        ranked = [jnp.where(first_chip, even[r], even[r ^ 2]) for r in range(4)]
        return jnp.stack(ranked, axis=1)

    column, half = group * 2 * head_dim, kv_weight.shape[0] // 2

    def halves(part):
        mine = lax.dynamic_slice_in_dim(kv_weight, column + part * head_dim, head_dim, axis=1)
        ours = lax.dynamic_slice_in_dim(mine, tile // 2 * half, half, axis=0)
        return ours, lax.dynamic_slice_in_dim(mine, half - tile // 2 * half, half, axis=0)

    def ours_to_plane(rows):
        return moved(rows, lambda t, h: (h // 2 * 2 + outer_core(h), t))

    def others_to_plane(rows):
        return moved(rows, lambda t, h: (h // 2 * 2 + outer_core(h), t ^ 2))

    def both_blocks(rows, other):
        return put_first(tile // 2 == head // 2, rows, other, 1)

    key_ours, key_others = halves(0)
    value_ours, value_others = halves(1)
    bias_rows = moved(proj_bias, lambda t, h: (h, t))
    key_ours = ours_to_plane(key_ours)
    key_others, value_others = swapped(key_others, "tile", 2), swapped(value_others, "tile", 2)
    no_terms = (
        jnp.zeros((depth, width), jnp.float32),
        tuple(jnp.full((depth, width), k, jnp.bfloat16) for k in range(3)),
    )
    no_tokens = tuple(
        jnp.full((tile_slots, shard_len, 2 * width), k, jnp.bfloat16) for k in range(2)
    )
    bias_rows, key_ours, key_others, value_ours, value_others = step(
        (bias_rows, key_ours, key_others, value_ours, value_others)
    )

    key_others, value_ours = others_to_plane(key_others), ours_to_plane(value_ours)
    other = swapped(key_ours, "tile", 2)
    bias_part = add_columns(bias_rows[None], kv_weight)
    key_ours, key_others, value_ours, other, bias_part, feature_parts, no_terms, no_tokens, once = step(
        (
            key_ours,
            key_others,
            value_ours,
            other,
            bias_part,
            feature_parts,
            no_terms,
            no_tokens,
            once,
        )
    )

    near_ours = step(both_blocks(key_ours, other))
    value_others = others_to_plane(value_others)
    other, far_ours = step((swapped(key_others, "tile", 2), swapped(near_ours, "tile", 1)))
    near_others = step(both_blocks(key_others, other))
    far_others = swapped(near_others, "tile", 1)
    bias_part = bias_part + swapped(bias_part, "tile", 1)
    own, parts = products((near_ours, near_others), (far_ours, far_others))
    own, parts, value_ours, value_others, bias_part = step(
        (own, parts, value_ours, value_others, bias_part)
    )

    def values_terms(given):
        value_ours, value_others, bias_part = given
        other_ours, other_others, bias_other = step(
            (
                swapped(value_ours, "tile", 2),
                swapped(value_others, "tile", 2),
                swapped(bias_part, "tile", 2),
            )
        )
        near = both_blocks(value_ours, other_ours), both_blocks(value_others, other_others)
        near = step(near)
        terms = products(near, tuple(swapped(rows, "tile", 1) for rows in near))
        return (other_ours, other_others, bias_other), (terms, bias_part + bias_other)

    empty = no_terms, bias_part
    arrived, beside = step(
        (exchange(parts), in_loop(values_terms, (value_ours, value_others, bias_part), empty))
    )
    own = summed(own, arrived)
    (value_own, parts), bias_part = beside
    bias_part = bias_part.reshape(2, layers, 2, head_dim)

    def keys_product(own):
        across_x, across_y = step((swapped(own, "tile", 2), swapped(own, "groups", 1)))
        rows_0 = step(both_heads(own, across_y))
        diagonal, rows_1 = step((swapped(across_y, "tile", 2), swapped(rows_0, "tile", 1)))
        rows_2 = step(both_heads(across_x, diagonal))
        rows = [rows_0, rows_1, rows_2, swapped(rows_2, "tile", 1)]
        return across_x, finish(times_features(rows, feature_parts), 0)

    arrived, keys = step((exchange(parts), in_loop(keys_product, own, no_tokens[0])))
    own = summed(value_own, arrived)

    shifted, across_x, across_y = step(
        (shifted_2(keys, "head", 1), swapped(own, "tile", 2), swapped(own, "groups", 1))
    )

    def values_product(given):
        own, across_x, across_y = given
        rows_0 = step(both_heads(own, across_y))
        middle = depth // 2
        upper, lower, rows_1 = step(
            (
                swapped(across_x[:middle], "groups", 1),
                swapped(across_y[middle:], "tile", 2),
                swapped(rows_0, "tile", 1),
            )
        )
        rows_2 = step(both_heads(across_x, jnp.concatenate([upper, lower], axis=0)))
        rows = [rows_0, rows_1, rows_2, swapped(rows_2, "tile", 1)]
        total = times_features(rows, feature_parts)
        return (across_y, own, across_x), finish(total, 1)

    keys = step(rolled(keys, shifted, 1))
    values = in_loop(values_product, (own, across_x, across_y), no_tokens[1])
    shifted, values = step((shifted_2(keys, "head", 2), values))

    picked = outgoing(rolled(keys, shifted, 2))
    shifted, picked = step((shifted_2(values, "head", 1), picked))

    values = step(rolled(values, shifted, 1))
    arrived, shifted = step((to_owners(picked), shifted_2(values, "head", 2)))

    value_cache = in_order(to_owners(outgoing(rolled(values, shifted, 2))))
    cache = jnp.stack([in_order(arrived), value_cache], axis=-2)
    return cache.reshape(1, 1, most_tiles * 4 * shard_len, 4 * layers, head_dim)


def solution(mesh):
    placed = (
        P("groups", "tile", None),
        P("tile", "head"),
        P("head"),
        P("tile", "head"),
        P(),
        P("groups", None),
        P("groups"),
        P("groups"),
    )
    sizes = tuple(mesh.shape[name] for name in ("groups", "tile", "head"))
    return jax.shard_map(
        product_plan if sizes == (2, 4, 4) else gather_plan,
        mesh=mesh,
        in_specs=placed,
        out_specs=P(("groups", "tile"), "head", None, None, None),
        check_vma=False,
    )
```

```python
import jax
import jax.numpy as jnp
from jax import lax
from jax.experimental import pallas as pl
from jax.experimental.pallas import tpu as pltpu
from jax.sharding import PartitionSpec as P

eps_norm = 1e-05


def shifted_2(shard, axis, by):
    count = lax.axis_size(axis)
    return lax.ppermute(shard, axis, [(i, (i + by) % count) for i in range(count)])


def swapped(shard, axis, bit):
    return lax.ppermute(shard, axis, [(i, i ^ bit) for i in range(lax.axis_size(axis))])


def add_columns(operand, portion):
    return jnp.dot(operand, portion, preferred_element_type=jnp.float32)


def routing(tile_map, tile_count, decode_owner, tile_slots, head_groups):
    most_tiles = tile_map.shape[1]
    owner_tile = decode_owner // head_groups
    owner_turn = decode_owner % head_groups
    usable = jnp.arange(most_tiles)[None, :] < tile_count[:, None]
    matched = (tile_map[:, :, None] == jnp.arange(tile_slots)[None, None, :]) & usable[:, :, None]
    return owner_tile, owner_turn, matched


def gather_plan(
    features, proj_weight, proj_bias, kv_weight, key_gain, tile_map, tile_count, decode_owner
):
    tile_slots, shard_len, feature_width = features.shape
    token_rows = tile_slots * shard_len
    feature_rows = features.reshape(token_rows, feature_width)
    weight_cols = lax.all_gather(proj_weight, "tile", axis=0, tiled=True)
    projected = jnp.dot(feature_rows, weight_cols, preferred_element_type=jnp.float32)
    projected_local = (projected + proj_bias.astype(jnp.float32)).astype(jnp.bfloat16)
    kv_width = kv_weight.shape[1]
    projected_all = lax.all_gather(projected_local, "head", axis=1, tiled=True)
    key_value = add_columns(projected_all, lax.all_gather(kv_weight, "tile", axis=0, tiled=True))
    layers, head_dim = key_gain.shape
    blocks = key_value.reshape(token_rows, -1, layers, 2, head_dim)
    keys_raw = blocks[:, :, :, 0]
    inv_rms = lax.rsqrt(jnp.mean(keys_raw * keys_raw, axis=-1, keepdims=True) + eps_norm)
    keys_normed = keys_raw * inv_rms * key_gain[None, None]
    stacked = jnp.stack([keys_normed, blocks[:, :, :, 1]], axis=3).astype(jnp.bfloat16)
    per_tile = stacked.reshape(tile_slots, shard_len * kv_width)
    tile_ranks = lax.axis_size("tile")
    head_groups = lax.axis_size("head")
    most_tiles = tile_map.shape[1]
    owner_tile, owner_turn, matched = routing(
        tile_map, tile_count, decode_owner, tile_slots, head_groups
    )
    owned_by = (owner_tile[:, None] == jnp.arange(tile_ranks)[None, :]).astype(jnp.float32)
    selector = jnp.einsum("rd,rjs->jds", owned_by, matched.astype(jnp.float32))
    selector = selector.astype(jnp.bfloat16).reshape(most_tiles * tile_ranks, tile_slots)
    outgoing = add_columns(selector, per_tile).astype(jnp.bfloat16)
    outgoing = outgoing.reshape(most_tiles, tile_ranks, shard_len, kv_width)
    arrived = lax.all_to_all(outgoing, "tile", split_axis=1, concat_axis=1, tiled=True)
    gathered_rows = arrived.reshape(
        most_tiles * tile_ranks * shard_len, kv_width // head_dim, head_dim
    )
    my_turn = jnp.sum(jnp.where(owner_tile == lax.axis_index("tile"), owner_turn, 0))
    stride = 1
    while stride < head_groups:
        shifted = shifted_2(gathered_rows, "head", stride)
        gathered_rows = jnp.where(my_turn // stride % 2 == 1, shifted, gathered_rows)
        stride = stride * 2
    return gathered_rows[None, None]


def terms_body(choice, weight, near, far, terms):
    near_product = add_columns(weight[...], near[...])
    far_product = add_columns(weight[...], far[...])
    width = terms.shape[2]
    terms[choice[0]] = near_product[:, :width].astype(terms.dtype)
    terms[choice[1]] = near_product[:, width:].astype(terms.dtype)
    terms[choice[2]] = far_product[:, :width].astype(terms.dtype)
    terms[choice[3]] = far_product[:, width:].astype(terms.dtype)


def product_terms(choice, weight, near, far):
    depth, rows = weight.shape
    columns = near.shape[1]
    width = columns // 2
    tall = 640 if depth % 640 == 0 else depth
    whole = pl.BlockSpec((rows, columns), lambda i, choice: (0, 0))
    return pl.pallas_call(
        terms_body,
        out_shape=jax.ShapeDtypeStruct((4, depth, width), jnp.bfloat16),
        grid_spec=pltpu.PrefetchScalarGridSpec(
            num_scalar_prefetch=1,
            grid=(depth // tall,),
            in_specs=[pl.BlockSpec((tall, rows), lambda i, choice: (i, 0)), whole, whole],
            out_specs=pl.BlockSpec((4, tall, width), lambda i, choice: (0, i, 0)),
        ),
        compiler_params=pltpu.CompilerParams(vmem_limit_bytes=32 * 1024 * 1024),
        cost_estimate=pl.CostEstimate(
            flops=4 * depth * rows * columns,
            bytes_accessed=2 * depth * rows + 4 * rows * columns + 8 * depth * width,
            transcendentals=0,
        ),
    )(choice, weight, near, far)


def product_plan(
    features, proj_weight, proj_bias, kv_weight, key_gain, tile_map, tile_count, decode_owner
):
    tile_slots, shard_len, feature_width = features.shape
    token_rows = tile_slots * shard_len
    depth = proj_weight.shape[0]
    layers, head_dim = key_gain.shape
    width = layers * head_dim
    most_tiles = tile_map.shape[1]
    group, tile, head = (lax.axis_index(name) for name in ("groups", "tile", "head"))
    first_core, first_chip = tile % 2 == 0, tile < 2
    feature_rows = features.reshape(token_rows, feature_width)
    step = lax.optimization_barrier

    def moved(shard, target):
        pairs = []
        for t in range(4):
            for h in range(4):
                to_tile, to_head = target(t, h)
                pairs.append((t * 4 + h, to_tile * 4 + to_head))
        return lax.ppermute(shard, ("tile", "head"), pairs)

    def outer_core(h):
        return (h ^ h // 2) % 2

    feature_parts = [
        lax.dynamic_slice_in_dim(feature_rows, (tile ^ r) * depth, depth, axis=1) for r in range(4)
    ]

    def put_first(condition, one, other, axis):
        return jnp.concatenate(
            [jnp.where(condition, one, other), jnp.where(condition, other, one)], axis=axis
        )

    def both_heads(ours, theirs):
        return put_first(group == 0, ours, theirs, 1)

    outer = jnp.where(head < 2, jnp.array([0, 3]), jnp.array([3, 0]))
    inner = jnp.where(head < 2, jnp.array([1, 2]), jnp.array([2, 1]))
    choice = jnp.where(
        first_core, jnp.concatenate([outer, inner]), jnp.concatenate([inner, outer])
    ).astype(jnp.int32)

    def products(near, far):
        return product_terms(choice, proj_weight, near, far)

    def summed(terms):
        return lax.psum_scatter(terms, "head", scatter_dimension=0)

    once = jnp.minimum(jnp.max(tile_count), 1)

    def in_loop(chain, given, empty):
        return lax.fori_loop(0, once, lambda _, carry: chain(carry[0]), (given, empty))[1]

    def times_features(rows, parts):
        return sum(add_columns(parts[r], rows[r]) for r in range(4))

    def finish(total, part):
        finished = []
        for k in range(2):
            entries = total[:, k * width : (k + 1) * width].reshape(token_rows, layers, head_dim)
            entries = entries + bias_part[k, :, part][None]
            if part == 0:
                squares = jnp.mean(entries * entries, axis=-1, keepdims=True)
                entries = entries * lax.rsqrt(squares + eps_norm) * key_gain[None]
            finished.append(entries.reshape(token_rows, width).astype(jnp.bfloat16))
        return jnp.concatenate(finished, axis=1).reshape(tile_slots, shard_len, 2 * width)

    owner_tile, owner_turn, matched = routing(tile_map, tile_count, decode_owner, tile_slots, 4)
    turn_of = jnp.sum(jnp.where(matched, owner_turn[:, None, None], 0), axis=(0, 1))
    owned_by = (owner_tile[:, None] == (tile ^ jnp.arange(4))[None, :]).astype(jnp.float32)
    selector = jnp.einsum("rd,rjs->djs", owned_by, matched.astype(jnp.float32))
    selector = selector.astype(jnp.bfloat16).reshape(4 * most_tiles, tile_slots)

    def rolled(rows, shifted, stride):
        odd = (turn_of // stride % 2 == 1)[:, None, None]
        return jnp.where(odd, shifted, rows)

    def outgoing(rows):
        picked = add_columns(selector, rows.reshape(tile_slots, -1)).astype(jnp.bfloat16)
        picked = picked.reshape(4, most_tiles, shard_len, 2, layers, head_dim)
        return [picked[r] for r in range(4)]

    def to_owners(picked):
        return [picked[0]] + [swapped(picked[r], "tile", r) for r in (1, 2, 3)]

    def in_order(arrived):
        even = [jnp.where(first_core, arrived[r], arrived[r ^ 1]) for r in range(4)]
        ranked = [jnp.where(first_chip, even[r], even[r ^ 2]) for r in range(4)]
        return jnp.stack(ranked, axis=1)

    column, half = group * 2 * head_dim, kv_weight.shape[0] // 2
    key_mine = lax.dynamic_slice_in_dim(kv_weight, column, head_dim, axis=1)
    value_mine = lax.dynamic_slice_in_dim(kv_weight, column + head_dim, head_dim, axis=1)
    stays = lax.dynamic_slice_in_dim(value_mine, tile // 2 * half, half, axis=0)
    leaves = lax.dynamic_slice_in_dim(value_mine, half - tile // 2 * half, half, axis=0)
    bias_rows = moved(proj_bias, lambda t, h: (h, t))
    key_block = moved(key_mine, lambda t, h: (h // 2 * 2 + outer_core(h), t))
    comes = swapped(leaves, "tile", 2)
    no_terms = jnp.zeros((4, depth, width), jnp.bfloat16)
    no_tokens = tuple(
        jnp.full((tile_slots, shard_len, 2 * width), k, jnp.bfloat16) for k in range(2)
    )
    bias_rows, key_block, comes, stays, feature_parts, no_terms, no_tokens, once = step(
        (bias_rows, key_block, comes, stays, feature_parts, no_terms, no_tokens, once)
    )

    value_pieces = []
    for j in range(2):
        piece = jnp.where(tile // 2 == (head // 2) ^ j, stays, comes)
        value_pieces.append(
            moved(piece, lambda t, h: (t // 2 * 2 + outer_core(h), t % 2 + 2 * ((h // 2) ^ j)))
        )
    key_other = swapped(key_block, "tile", 2)
    bias_part = add_columns(bias_rows[None], kv_weight)
    value_pieces, key_block, key_other, bias_part = step(
        (value_pieces, key_block, key_other, bias_part)
    )

    key_near = put_first(tile // 2 == head // 2, key_block, key_other, 1)
    value_half = jnp.concatenate(value_pieces, axis=1)
    key_near, value_half = step((key_near, value_half))
    terms = products(key_near, swapped(key_near, "tile", 1))
    bias_part = bias_part + swapped(bias_part, "tile", 1)
    terms, value_half, bias_part = step((terms, value_half, bias_part))

    def values_terms(given):
        value_half, bias_part = given
        other, bias_other = step((swapped(value_half, "tile", 2), swapped(bias_part, "tile", 2)))
        near = step(put_first(first_chip, value_half, other, 0))
        terms = products(near, swapped(near, "tile", 1))
        return (other, bias_other), (terms, bias_part + bias_other)

    empty = no_terms, bias_part
    own, beside = step((summed(terms), in_loop(values_terms, (value_half, bias_part), empty)))
    terms, bias_part = beside
    bias_part = bias_part.reshape(2, layers, 2, head_dim)

    def keys_product(own):
        across_x, across_y = step((swapped(own, "tile", 2), swapped(own, "groups", 1)))
        rows_0 = step(both_heads(own, across_y))
        diagonal, rows_1 = step((swapped(across_y, "tile", 2), swapped(rows_0, "tile", 1)))
        rows_2 = step(both_heads(across_x, diagonal))
        rows = [rows_0, rows_1, rows_2, swapped(rows_2, "tile", 1)]
        return across_x, finish(times_features(rows, feature_parts), 0)

    own, keys = step((summed(terms), in_loop(keys_product, own, no_tokens[0])))

    shifted, across_x, across_y = step(
        (shifted_2(keys, "head", 1), swapped(own, "tile", 2), swapped(own, "groups", 1))
    )

    def values_product(given):
        own, across_x, across_y = given
        rows_0 = step(both_heads(own, across_y))
        middle = depth // 2
        upper, lower, rows_1 = step(
            (
                swapped(across_x[:middle], "groups", 1),
                swapped(across_y[middle:], "tile", 2),
                swapped(rows_0, "tile", 1),
            )
        )
        rows_2 = step(both_heads(across_x, jnp.concatenate([upper, lower], axis=0)))
        rows = [rows_0, rows_1, rows_2, swapped(rows_2, "tile", 1)]
        total = times_features(rows, feature_parts)
        return (across_y, own, across_x), finish(total, 1)

    keys = step(rolled(keys, shifted, 1))
    values = in_loop(values_product, (own, across_x, across_y), no_tokens[1])
    shifted, values = step((shifted_2(keys, "head", 2), values))

    picked = outgoing(rolled(keys, shifted, 2))
    shifted, picked = step((shifted_2(values, "head", 1), picked))

    values = step(rolled(values, shifted, 1))
    arrived, shifted = step((to_owners(picked), shifted_2(values, "head", 2)))

    value_cache = in_order(to_owners(outgoing(rolled(values, shifted, 2))))
    cache = jnp.stack([in_order(arrived), value_cache], axis=-2)
    return cache.reshape(1, 1, most_tiles * 4 * shard_len, 4 * layers, head_dim)


def solution(mesh):
    placed = (
        P("groups", "tile", None),
        P("tile", "head"),
        P("head"),
        P("tile", "head"),
        P(),
        P("groups", None),
        P("groups"),
        P("groups"),
    )
    sizes = tuple(mesh.shape[name] for name in ("groups", "tile", "head"))
    return jax.shard_map(
        product_plan if sizes == (2, 4, 4) else gather_plan,
        mesh=mesh,
        in_specs=placed,
        out_specs=P(("groups", "tile"), "head", None, None, None),
        check_vma=False,
    )
```

```python
import functools

import jax
import jax.numpy as jnp
from jax import lax
from jax.experimental import pallas as pl
from jax.experimental.pallas import tpu as pltpu
from jax.sharding import PartitionSpec as P

eps_norm = 1e-05


def shifted_2(shard, axis, by):
    count = lax.axis_size(axis)
    return lax.ppermute(shard, axis, [(i, (i + by) % count) for i in range(count)])


def swapped(shard, axis, bit):
    return lax.ppermute(shard, axis, [(i, i ^ bit) for i in range(lax.axis_size(axis))])


def add_columns(operand, portion):
    return jnp.dot(operand, portion, preferred_element_type=jnp.float32)


def routing(tile_map, tile_count, decode_owner, tile_slots, head_groups):
    most_tiles = tile_map.shape[1]
    owner_tile = decode_owner // head_groups
    owner_turn = decode_owner % head_groups
    usable = jnp.arange(most_tiles)[None, :] < tile_count[:, None]
    matched = (tile_map[:, :, None] == jnp.arange(tile_slots)[None, None, :]) & usable[:, :, None]
    return owner_tile, owner_turn, matched


def gather_plan(
    features, proj_weight, proj_bias, kv_weight, key_gain, tile_map, tile_count, decode_owner
):
    tile_slots, shard_len, feature_width = features.shape
    token_rows = tile_slots * shard_len
    feature_rows = features.reshape(token_rows, feature_width)
    weight_cols = lax.all_gather(proj_weight, "tile", axis=0, tiled=True)
    projected = jnp.dot(feature_rows, weight_cols, preferred_element_type=jnp.float32)
    projected_local = (projected + proj_bias.astype(jnp.float32)).astype(jnp.bfloat16)
    kv_width = kv_weight.shape[1]
    projected_all = lax.all_gather(projected_local, "head", axis=1, tiled=True)
    key_value = add_columns(projected_all, lax.all_gather(kv_weight, "tile", axis=0, tiled=True))
    layers, head_dim = key_gain.shape
    blocks = key_value.reshape(token_rows, -1, layers, 2, head_dim)
    keys_raw = blocks[:, :, :, 0]
    inv_rms = lax.rsqrt(jnp.mean(keys_raw * keys_raw, axis=-1, keepdims=True) + eps_norm)
    keys_normed = keys_raw * inv_rms * key_gain[None, None]
    stacked = jnp.stack([keys_normed, blocks[:, :, :, 1]], axis=3).astype(jnp.bfloat16)
    per_tile = stacked.reshape(tile_slots, shard_len * kv_width)
    tile_ranks = lax.axis_size("tile")
    head_groups = lax.axis_size("head")
    most_tiles = tile_map.shape[1]
    owner_tile, owner_turn, matched = routing(
        tile_map, tile_count, decode_owner, tile_slots, head_groups
    )
    owned_by = (owner_tile[:, None] == jnp.arange(tile_ranks)[None, :]).astype(jnp.float32)
    selector = jnp.einsum("rd,rjs->jds", owned_by, matched.astype(jnp.float32))
    selector = selector.astype(jnp.bfloat16).reshape(most_tiles * tile_ranks, tile_slots)
    outgoing = add_columns(selector, per_tile).astype(jnp.bfloat16)
    outgoing = outgoing.reshape(most_tiles, tile_ranks, shard_len, kv_width)
    arrived = lax.all_to_all(outgoing, "tile", split_axis=1, concat_axis=1, tiled=True)
    gathered_rows = arrived.reshape(
        most_tiles * tile_ranks * shard_len, kv_width // head_dim, head_dim
    )
    my_turn = jnp.sum(jnp.where(owner_tile == lax.axis_index("tile"), owner_turn, 0))
    stride = 1
    while stride < head_groups:
        shifted = shifted_2(gathered_rows, "head", stride)
        gathered_rows = jnp.where(my_turn // stride % 2 == 1, shifted, gathered_rows)
        stride = stride * 2
    return gathered_rows[None, None]


scalars, vmem = pl.BlockSpec(memory_space=pltpu.SMEM), pl.BlockSpec(memory_space=pltpu.VMEM)
kernel_memory = pltpu.CompilerParams(vmem_limit_bytes=40 * 1024 * 1024)


def terms_body(choice, weight, near, far, own, *parts):
    depth, width = own.shape
    tall = 640 if depth % 640 == 0 else depth

    @pl.loop(0, depth // tall)
    def _(i):
        rows = pl.ds(pl.multiple_of(i * tall, tall), tall)
        near_product = add_columns(weight[rows, :], near[...])
        far_product = add_columns(weight[rows, :], far[...])
        near_kept = choice[0] == 1
        kept = jnp.where(near_kept, near_product, far_product)
        sent = jnp.where(near_kept, far_product, near_product)
        own[rows, :] = kept[:, :width]
        for part, block in zip(parts, (sent[:, width:], kept[:, width:], sent[:, :width])):
            part[rows, :] = block.astype(part.dtype)


def product_terms(choice, weight, near, far):
    depth, rows = weight.shape
    columns = near.shape[1]
    width = columns // 2
    return pl.pallas_call(
        terms_body,
        out_shape=[
            jax.ShapeDtypeStruct((depth, width), dtype)
            for dtype in (jnp.float32, jnp.bfloat16, jnp.bfloat16, jnp.bfloat16)
        ],
        in_specs=[scalars, vmem, vmem, vmem],
        out_specs=[vmem] * 4,
        compiler_params=kernel_memory,
        cost_estimate=pl.CostEstimate(
            flops=4 * depth * rows * columns,
            bytes_accessed=2 * depth * rows + 4 * rows * columns + 10 * depth * width,
            transcendentals=0,
        ),
    )(choice, weight, near, far)


def tokens_body(normed, tile, features, bias, gain, *refs):
    *parts, out, total = refs
    depth, columns = parts[0].shape
    for r, part in enumerate(parts):
        start = pl.multiple_of((tile[0] ^ r) * depth, 128)
        product = add_columns(features[:, pl.ds(start, depth)], part[...])
        total[...] = product if r == 0 else total[...] + product
    width = columns // 2
    for k in range(2):
        block = pl.ds(k * width, width)
        entries = total[:, block] + bias[:, block]
        if normed:
            squares = jnp.mean(entries * entries, axis=-1, keepdims=True)
            entries = entries * lax.rsqrt(squares + eps_norm) * gain[...]
        out[:, block] = entries.astype(out.dtype)


def token_entries(normed, tile, features, bias, gain, parts):
    rows, columns = features.shape[0], parts[0].shape[1]
    return pl.pallas_call(
        functools.partial(tokens_body, normed),
        out_shape=jax.ShapeDtypeStruct((rows, columns), jnp.bfloat16),
        in_specs=[scalars] + [vmem] * 7,
        out_specs=vmem,
        scratch_shapes=[pltpu.VMEM((rows, columns), jnp.float32)],
        compiler_params=kernel_memory,
        cost_estimate=pl.CostEstimate(
            flops=2 * rows * features.shape[1] * columns,
            bytes_accessed=2 * features.shape[1] * (rows + columns) + 2 * rows * columns,
            transcendentals=rows,
        ),
    )(tile, features, bias, gain, *parts)


def product_plan(
    features, proj_weight, proj_bias, kv_weight, key_gain, tile_map, tile_count, decode_owner
):
    tile_slots, shard_len, feature_width = features.shape
    token_rows = tile_slots * shard_len
    depth = proj_weight.shape[0]
    layers, head_dim = key_gain.shape
    width = layers * head_dim
    most_tiles = tile_map.shape[1]
    group, tile, head = (lax.axis_index(name) for name in ("groups", "tile", "head"))
    first_core, first_chip = tile % 2 == 0, tile < 2
    at_end = (head == 0) | (head == 3)
    feature_rows = features.reshape(token_rows, feature_width)
    step = lax.optimization_barrier

    def moved(shard, target):
        pairs = []
        for t in range(4):
            for h in range(4):
                to_tile, to_head = target(t, h)
                pairs.append((t * 4 + h, to_tile * 4 + to_head))
        return lax.ppermute(shard, ("tile", "head"), pairs)

    def outer_core(h):
        return (h ^ h // 2) % 2

    def put_first(condition, one, other, axis):
        return jnp.concatenate(
            [jnp.where(condition, one, other), jnp.where(condition, other, one)], axis=axis
        )

    def both_heads(ours, theirs):
        return put_first(group == 0, ours, theirs, 1)

    choice = (at_end == first_core).astype(jnp.int32).reshape(1)

    def products(near, far):
        own, *parts = product_terms(choice, proj_weight, near, far)
        return own, tuple(parts)

    def exchange(parts):
        return tuple(swapped(part, "head", bit) for part, bit in zip(parts, (2, 3, 1)))

    def summed(own, arrived):
        for block in arrived:
            own = own + block.astype(jnp.float32)
        return own.astype(jnp.bfloat16)

    once = jnp.minimum(jnp.max(tile_count), 1)

    def in_loop(chain, given, empty):
        return lax.fori_loop(0, once, lambda _, carry: chain(carry[0]), (given, empty))[1]

    def times_features(parts, part, bias_part):
        bias = bias_part[:, :, part].reshape(1, 2 * width)
        entries = token_entries(part == 0, tile.reshape(1), feature_rows, bias, key_gain, parts)
        return entries.reshape(tile_slots, shard_len, 2 * width)

    owner_tile, owner_turn, matched = routing(tile_map, tile_count, decode_owner, tile_slots, 4)
    turn_of = jnp.sum(jnp.where(matched, owner_turn[:, None, None], 0), axis=(0, 1))
    owned_by = (owner_tile[:, None] == (tile ^ jnp.arange(4))[None, :]).astype(jnp.float32)
    selector = jnp.einsum("rd,rjs->djs", owned_by, matched.astype(jnp.float32))
    selector = selector.astype(jnp.bfloat16).reshape(4 * most_tiles, tile_slots)

    def rolled(rows, shifted, stride):
        odd = (turn_of // stride % 2 == 1)[:, None, None]
        return jnp.where(odd, shifted, rows)

    def outgoing(rows):
        picked = add_columns(selector, rows.reshape(tile_slots, -1)).astype(jnp.bfloat16)
        picked = picked.reshape(4, most_tiles, shard_len, 2, layers, head_dim)
        return [picked[r] for r in range(4)]

    def to_owners(picked):
        return [picked[0]] + [swapped(picked[r], "tile", r) for r in (1, 2, 3)]

    def in_order(arrived):
        even = [jnp.where(first_core, arrived[r], arrived[r ^ 1]) for r in range(4)]
        ranked = [jnp.where(first_chip, even[r], even[r ^ 2]) for r in range(4)]
        return jnp.stack(ranked, axis=1)

    column, half = group * 2 * head_dim, kv_weight.shape[0] // 2
    key_mine = lax.dynamic_slice_in_dim(kv_weight, column, head_dim, axis=1)
    value_mine = lax.dynamic_slice_in_dim(kv_weight, column + head_dim, head_dim, axis=1)
    stays = lax.dynamic_slice_in_dim(value_mine, tile // 2 * half, half, axis=0)
    leaves = lax.dynamic_slice_in_dim(value_mine, half - tile // 2 * half, half, axis=0)
    bias_rows = moved(proj_bias, lambda t, h: (h, t))
    key_block = moved(key_mine, lambda t, h: (h // 2 * 2 + outer_core(h), t))
    comes = swapped(leaves, "tile", 2)
    no_terms = (
        jnp.zeros((depth, width), jnp.float32),
        tuple(jnp.full((depth, width), k, jnp.bfloat16) for k in range(3)),
    )
    no_tokens = tuple(
        jnp.full((tile_slots, shard_len, 2 * width), k, jnp.bfloat16) for k in range(2)
    )
    bias_rows, key_block, comes, stays, once = step(
        (bias_rows, key_block, comes, stays, once)
    )

    value_pieces = []
    for j in range(2):
        piece = jnp.where(tile // 2 == (head // 2) ^ j, stays, comes)
        value_pieces.append(
            moved(piece, lambda t, h: (t // 2 * 2 + outer_core(h), t % 2 + 2 * ((h // 2) ^ j)))
        )
    key_other = swapped(key_block, "tile", 2)
    bias_part = add_columns(bias_rows[None], kv_weight)
    value_pieces, key_block, key_other, bias_part = step(
        (value_pieces, key_block, key_other, bias_part)
    )

    key_near = put_first(tile // 2 == head // 2, key_block, key_other, 1)
    value_half = jnp.concatenate(value_pieces, axis=1)
    key_near, value_half = step((key_near, value_half))
    own, parts = products(key_near, swapped(key_near, "tile", 1))
    bias_part = bias_part + swapped(bias_part, "tile", 1)
    own, parts, value_half, bias_part = step((own, parts, value_half, bias_part))

    def values_terms(given):
        value_half, bias_part = given
        other, bias_other = step((swapped(value_half, "tile", 2), swapped(bias_part, "tile", 2)))
        near = step(put_first(first_chip, value_half, other, 0))
        terms = products(near, swapped(near, "tile", 1))
        return (other, bias_other), (terms, bias_part + bias_other)

    empty = no_terms, bias_part
    arrived, beside = step(
        (exchange(parts), in_loop(values_terms, (value_half, bias_part), empty))
    )
    own = summed(own, arrived)
    (value_own, parts), bias_part = beside
    bias_part = bias_part.reshape(2, layers, 2, head_dim)

    def keys_product(own):
        across_x, across_y = step((swapped(own, "tile", 2), swapped(own, "groups", 1)))
        rows_0 = step(both_heads(own, across_y))
        diagonal, rows_1 = step((swapped(across_y, "tile", 2), swapped(rows_0, "tile", 1)))
        rows_2 = step(both_heads(across_x, diagonal))
        rows = [rows_0, rows_1, rows_2, swapped(rows_2, "tile", 1)]
        return across_x, times_features(rows, 0, bias_part)

    arrived, keys = step((exchange(parts), in_loop(keys_product, own, no_tokens[0])))
    own = summed(value_own, arrived)

    shifted, across_x, across_y = step(
        (shifted_2(keys, "head", 1), swapped(own, "tile", 2), swapped(own, "groups", 1))
    )

    def values_product(given):
        own, across_x, across_y = given
        rows_0 = step(both_heads(own, across_y))
        middle = depth // 2
        upper, lower, rows_1 = step(
            (
                swapped(across_x[:middle], "groups", 1),
                swapped(across_y[middle:], "tile", 2),
                swapped(rows_0, "tile", 1),
            )
        )
        rows_2 = step(both_heads(across_x, jnp.concatenate([upper, lower], axis=0)))
        rows = [rows_0, rows_1, rows_2, swapped(rows_2, "tile", 1)]
        return (across_y, own, across_x), times_features(rows, 1, bias_part)

    keys = step(rolled(keys, shifted, 1))
    values = in_loop(values_product, (own, across_x, across_y), no_tokens[1])
    shifted, values = step((shifted_2(keys, "head", 2), values))

    picked = outgoing(rolled(keys, shifted, 2))
    shifted, picked = step((shifted_2(values, "head", 1), picked))

    values = step(rolled(values, shifted, 1))
    arrived, shifted = step((to_owners(picked), shifted_2(values, "head", 2)))

    value_cache = in_order(to_owners(outgoing(rolled(values, shifted, 2))))
    cache = jnp.stack([in_order(arrived), value_cache], axis=-2)
    return cache.reshape(1, 1, most_tiles * 4 * shard_len, 4 * layers, head_dim)


def solution(mesh):
    placed = (
        P("groups", "tile", None),
        P("tile", "head"),
        P("head"),
        P("tile", "head"),
        P(),
        P("groups", None),
        P("groups"),
        P("groups"),
    )
    sizes = tuple(mesh.shape[name] for name in ("groups", "tile", "head"))
    return jax.shard_map(
        product_plan if sizes == (2, 4, 4) else gather_plan,
        mesh=mesh,
        in_specs=placed,
        out_specs=P(("groups", "tile"), "head", None, None, None),
        check_vma=False,
    )
```

```python
import jax
import jax.numpy as jnp
from jax import lax
from jax.experimental import pallas as pl
from jax.experimental.pallas import tpu as pltpu
from jax.sharding import PartitionSpec as P

eps_norm = 1e-05


def shifted_2(shard, axis, by):
    count = lax.axis_size(axis)
    return lax.ppermute(shard, axis, [(i, (i + by) % count) for i in range(count)])


def swapped(shard, axis, bit):
    return lax.ppermute(shard, axis, [(i, i ^ bit) for i in range(lax.axis_size(axis))])


def add_columns(operand, portion):
    return jnp.dot(operand, portion, preferred_element_type=jnp.float32)


def routing(tile_map, tile_count, decode_owner, tile_slots, head_groups):
    most_tiles = tile_map.shape[1]
    owner_tile = decode_owner // head_groups
    owner_turn = decode_owner % head_groups
    usable = jnp.arange(most_tiles)[None, :] < tile_count[:, None]
    matched = (tile_map[:, :, None] == jnp.arange(tile_slots)[None, None, :]) & usable[:, :, None]
    return owner_tile, owner_turn, matched


def gather_plan(
    features, proj_weight, proj_bias, kv_weight, key_gain, tile_map, tile_count, decode_owner
):
    tile_slots, shard_len, feature_width = features.shape
    token_rows = tile_slots * shard_len
    feature_rows = features.reshape(token_rows, feature_width)
    weight_cols = lax.all_gather(proj_weight, "tile", axis=0, tiled=True)
    projected = jnp.dot(feature_rows, weight_cols, preferred_element_type=jnp.float32)
    projected_local = (projected + proj_bias.astype(jnp.float32)).astype(jnp.bfloat16)
    kv_width = kv_weight.shape[1]
    projected_all = lax.all_gather(projected_local, "head", axis=1, tiled=True)
    key_value = add_columns(projected_all, lax.all_gather(kv_weight, "tile", axis=0, tiled=True))
    layers, head_dim = key_gain.shape
    blocks = key_value.reshape(token_rows, -1, layers, 2, head_dim)
    keys_raw = blocks[:, :, :, 0]
    inv_rms = lax.rsqrt(jnp.mean(keys_raw * keys_raw, axis=-1, keepdims=True) + eps_norm)
    keys_normed = keys_raw * inv_rms * key_gain[None, None]
    stacked = jnp.stack([keys_normed, blocks[:, :, :, 1]], axis=3).astype(jnp.bfloat16)
    per_tile = stacked.reshape(tile_slots, shard_len * kv_width)
    tile_ranks = lax.axis_size("tile")
    head_groups = lax.axis_size("head")
    most_tiles = tile_map.shape[1]
    owner_tile, owner_turn, matched = routing(
        tile_map, tile_count, decode_owner, tile_slots, head_groups
    )
    owned_by = (owner_tile[:, None] == jnp.arange(tile_ranks)[None, :]).astype(jnp.float32)
    selector = jnp.einsum("rd,rjs->jds", owned_by, matched.astype(jnp.float32))
    selector = selector.astype(jnp.bfloat16).reshape(most_tiles * tile_ranks, tile_slots)
    outgoing = add_columns(selector, per_tile).astype(jnp.bfloat16)
    outgoing = outgoing.reshape(most_tiles, tile_ranks, shard_len, kv_width)
    arrived = lax.all_to_all(outgoing, "tile", split_axis=1, concat_axis=1, tiled=True)
    gathered_rows = arrived.reshape(
        most_tiles * tile_ranks * shard_len, kv_width // head_dim, head_dim
    )
    my_turn = jnp.sum(jnp.where(owner_tile == lax.axis_index("tile"), owner_turn, 0))
    stride = 1
    while stride < head_groups:
        shifted = shifted_2(gathered_rows, "head", stride)
        gathered_rows = jnp.where(my_turn // stride % 2 == 1, shifted, gathered_rows)
        stride = stride * 2
    return gathered_rows[None, None]


def terms_body(choice, ours, others, near_ours, near_others, far_ours, far_others, own, *parts):
    near = add_columns(ours[...], near_ours[...]) + add_columns(others[...], near_others[...])
    far = add_columns(ours[...], far_ours[...]) + add_columns(others[...], far_others[...])
    width = own.shape[1]
    near_kept = choice[0] == 1
    kept, sent = jnp.where(near_kept, near, far), jnp.where(near_kept, far, near)
    own[...] = kept[:, :width]
    blocks = (sent[:, width:], kept[:, width:], sent[:, :width])
    for part, block in zip(parts, blocks):
        part[...] = block.astype(part.dtype)


def product_terms(choice, weight, near, far):
    depth, rows = weight.shape
    half, columns = rows // 2, near[0].shape[1]
    width = columns // 2
    tall = 640 if depth % 640 == 0 else depth
    whole = pl.BlockSpec((half, columns), lambda i, choice: (0, 0))
    narrow = pl.BlockSpec((tall, width), lambda i, choice: (i, 0))
    shapes = [jax.ShapeDtypeStruct((depth, width), t) for t in (jnp.float32,) + 3 * (jnp.bfloat16,)]
    return pl.pallas_call(
        terms_body,
        out_shape=shapes,
        grid_spec=pltpu.PrefetchScalarGridSpec(
            num_scalar_prefetch=1,
            grid=(depth // tall,),
            in_specs=[
                pl.BlockSpec((tall, half), lambda i, choice: (i, choice[1])),
                pl.BlockSpec((tall, half), lambda i, choice: (i, 1 - choice[1])),
                whole,
                whole,
                whole,
                whole,
            ],
            out_specs=[narrow] * 4,
        ),
        compiler_params=pltpu.CompilerParams(vmem_limit_bytes=32 * 1024 * 1024),
        cost_estimate=pl.CostEstimate(
            flops=4 * depth * rows * columns,
            bytes_accessed=2 * depth * rows + 4 * rows * columns + 10 * depth * width,
            transcendentals=0,
        ),
    )(choice, weight, weight, *near, *far)


def product_plan(
    features, proj_weight, proj_bias, kv_weight, key_gain, tile_map, tile_count, decode_owner
):
    tile_slots, shard_len, feature_width = features.shape
    token_rows = tile_slots * shard_len
    depth = proj_weight.shape[0]
    layers, head_dim = key_gain.shape
    width = layers * head_dim
    most_tiles = tile_map.shape[1]
    group, tile, head = (lax.axis_index(name) for name in ("groups", "tile", "head"))
    first_core, first_chip = tile % 2 == 0, tile < 2
    at_end = (head == 0) | (head == 3)
    feature_rows = features.reshape(token_rows, feature_width)
    step = lax.optimization_barrier

    def moved(shard, target):
        pairs = []
        for t in range(4):
            for h in range(4):
                to_tile, to_head = target(t, h)
                pairs.append((t * 4 + h, to_tile * 4 + to_head))
        return lax.ppermute(shard, ("tile", "head"), pairs)

    def outer_core(h):
        return (h ^ h // 2) % 2

    def put_first(condition, one, other, axis):
        return jnp.concatenate(
            [jnp.where(condition, one, other), jnp.where(condition, other, one)], axis=axis
        )

    def both_heads(ours, theirs):
        return put_first(group == 0, ours, theirs, 1)

    choice = jnp.stack([(at_end == first_core).astype(jnp.int32), head // 2])

    def products(near, far):
        own, *parts = product_terms(choice, proj_weight, near, far)
        return own, tuple(parts)

    def exchange(parts):
        return tuple(swapped(part, "head", bit) for part, bit in zip(parts, (2, 3, 1)))

    def summed(own, arrived):
        for block in arrived:
            own = own + block.astype(jnp.float32)
        return own.astype(jnp.bfloat16)

    once = jnp.minimum(jnp.max(tile_count), 1)

    def in_loop(chain, given, empty):
        return lax.fori_loop(0, once, lambda _, carry: chain(carry[0]), (given, empty))[1]

    def times_features(rows, parts):
        return sum(add_columns(parts[r], rows[r]) for r in range(4))

    def finish(total, part):
        finished = []
        for k in range(2):
            entries = total[:, k * width : (k + 1) * width].reshape(token_rows, layers, head_dim)
            entries = entries + bias_part[k, :, part][None]
            if part == 0:
                squares = jnp.mean(entries * entries, axis=-1, keepdims=True)
                entries = entries * lax.rsqrt(squares + eps_norm) * key_gain[None]
            finished.append(entries.reshape(token_rows, width).astype(jnp.bfloat16))
        return jnp.concatenate(finished, axis=1).reshape(tile_slots, shard_len, 2 * width)

    owner_tile, owner_turn, matched = routing(tile_map, tile_count, decode_owner, tile_slots, 4)
    turn_of = jnp.sum(jnp.where(matched, owner_turn[:, None, None], 0), axis=(0, 1))
    owned_by = (owner_tile[:, None] == (tile ^ jnp.arange(4))[None, :]).astype(jnp.float32)
    selector = jnp.einsum("rd,rjs->djs", owned_by, matched.astype(jnp.float32))
    selector = selector.astype(jnp.bfloat16).reshape(4 * most_tiles, tile_slots)

    def rolled(rows, shifted, stride):
        odd = (turn_of // stride % 2 == 1)[:, None, None]
        return jnp.where(odd, shifted, rows)

    def outgoing(rows):
        picked = add_columns(selector, rows.reshape(tile_slots, -1)).astype(jnp.bfloat16)
        picked = picked.reshape(4, most_tiles, shard_len, 2, layers, head_dim)
        return [picked[r] for r in range(4)]

    def to_owners(picked):
        return [picked[0]] + [swapped(picked[r], "tile", r) for r in (1, 2, 3)]

    def in_order(arrived):
        even = [jnp.where(first_core, arrived[r], arrived[r ^ 1]) for r in range(4)]
        ranked = [jnp.where(first_chip, even[r], even[r ^ 2]) for r in range(4)]
        return jnp.stack(ranked, axis=1)

    column, half = group * 2 * head_dim, kv_weight.shape[0] // 2

    def halves(part):
        mine = lax.dynamic_slice_in_dim(kv_weight, column + part * head_dim, head_dim, axis=1)
        ours = lax.dynamic_slice_in_dim(mine, tile // 2 * half, half, axis=0)
        return ours, lax.dynamic_slice_in_dim(mine, half - tile // 2 * half, half, axis=0)

    def ours_to_plane(rows):
        return moved(rows, lambda t, h: (h // 2 * 2 + outer_core(h), t))

    def others_to_plane(rows):
        return moved(rows, lambda t, h: (h // 2 * 2 + outer_core(h), t ^ 2))

    def both_blocks(rows, other):
        return put_first(tile // 2 == head // 2, rows, other, 1)

    ours = [halves(part)[0] for part in range(2)]
    others = jnp.concatenate([halves(part)[1] for part in range(2)], axis=1)

    def cross_x(given):
        others, bias_rows = given
        comes, bias_rows = step(
            (swapped(others, "tile", 2), moved(bias_rows, lambda t, h: (h, t)))
        )
        return (comes, bias_rows), (comes, bias_rows)

    no_terms = (
        jnp.zeros((depth, width), jnp.float32),
        tuple(jnp.full((depth, width), k, jnp.bfloat16) for k in range(3)),
    )
    no_tokens = tuple(
        jnp.full((tile_slots, shard_len, 2 * width), k, jnp.bfloat16) for k in range(2)
    )
    empty = jnp.zeros_like(others), jnp.zeros_like(proj_bias)
    key_ours, (comes, bias_rows), value_ours, feature_rows = step(
        (
            ours_to_plane(ours[0]),
            in_loop(cross_x, (others, proj_bias), empty),
            ours[1],
            feature_rows,
        )
    )

    key_others, value_others = comes[:, :width], comes[:, width:]
    bias_part = add_columns(bias_rows[None], kv_weight)
    feature_parts = [
        lax.dynamic_slice_in_dim(feature_rows, (tile ^ r) * depth, depth, axis=1) for r in range(4)
    ]
    key_ours, key_others, value_ours, value_others, other, bias_part, feature_parts = step(
        (
            key_ours,
            others_to_plane(key_others),
            ours_to_plane(value_ours),
            value_others,
            swapped(key_ours, "tile", 2),
            bias_part,
            feature_parts,
        )
    )

    near_ours = step(both_blocks(key_ours, other))
    value_others = others_to_plane(value_others)
    other, far_ours = step((swapped(key_others, "tile", 2), swapped(near_ours, "tile", 1)))
    near_others = step(both_blocks(key_others, other))
    far_others = swapped(near_others, "tile", 1)
    bias_part = bias_part + swapped(bias_part, "tile", 1)
    own, parts = products((near_ours, near_others), (far_ours, far_others))
    own, parts, value_ours, value_others, bias_part = step(
        (own, parts, value_ours, value_others, bias_part)
    )

    def values_terms(given):
        value_ours, value_others, bias_part = given
        other_ours, other_others, bias_other = step(
            (
                swapped(value_ours, "tile", 2),
                swapped(value_others, "tile", 2),
                swapped(bias_part, "tile", 2),
            )
        )
        near = both_blocks(value_ours, other_ours), both_blocks(value_others, other_others)
        near = step(near)
        terms = products(near, tuple(swapped(rows, "tile", 1) for rows in near))
        return (other_ours, other_others, bias_other), (terms, bias_part + bias_other)

    empty = no_terms, bias_part
    arrived, beside = step(
        (exchange(parts), in_loop(values_terms, (value_ours, value_others, bias_part), empty))
    )
    own = summed(own, arrived)
    (value_own, parts), bias_part = beside
    bias_part = bias_part.reshape(2, layers, 2, head_dim)

    def keys_product(own):
        across_x, across_y = step((swapped(own, "tile", 2), swapped(own, "groups", 1)))
        rows_0 = step(both_heads(own, across_y))
        diagonal, rows_1 = step((swapped(across_y, "tile", 2), swapped(rows_0, "tile", 1)))
        rows_2 = step(both_heads(across_x, diagonal))
        rows = [rows_0, rows_1, rows_2, swapped(rows_2, "tile", 1)]
        return across_x, finish(times_features(rows, feature_parts), 0)

    arrived, keys = step((exchange(parts), in_loop(keys_product, own, no_tokens[0])))
    own = summed(value_own, arrived)

    shifted, across_x, across_y = step(
        (shifted_2(keys, "head", 1), swapped(own, "tile", 2), swapped(own, "groups", 1))
    )

    def values_product(given):
        own, across_x, across_y = given
        rows_0 = step(both_heads(own, across_y))
        middle = depth // 2
        upper, lower, rows_1 = step(
            (
                swapped(across_x[:middle], "groups", 1),
                swapped(across_y[middle:], "tile", 2),
                swapped(rows_0, "tile", 1),
            )
        )
        rows_2 = step(both_heads(across_x, jnp.concatenate([upper, lower], axis=0)))
        rows = [rows_0, rows_1, rows_2, swapped(rows_2, "tile", 1)]
        total = times_features(rows, feature_parts)
        return (across_y, own, across_x), finish(total, 1)

    keys = step(rolled(keys, shifted, 1))
    values = in_loop(values_product, (own, across_x, across_y), no_tokens[1])
    shifted, values = step((shifted_2(keys, "head", 2), values))

    picked = outgoing(rolled(keys, shifted, 2))
    shifted, picked = step((shifted_2(values, "head", 1), picked))

    values = step(rolled(values, shifted, 1))
    arrived, shifted = step((to_owners(picked), shifted_2(values, "head", 2)))

    value_cache = in_order(to_owners(outgoing(rolled(values, shifted, 2))))
    cache = jnp.stack([in_order(arrived), value_cache], axis=-2)
    return cache.reshape(1, 1, most_tiles * 4 * shard_len, 4 * layers, head_dim)


def solution(mesh):
    placed = (
        P("groups", "tile", None),
        P("tile", "head"),
        P("head"),
        P("tile", "head"),
        P(),
        P("groups", None),
        P("groups"),
        P("groups"),
    )
    sizes = tuple(mesh.shape[name] for name in ("groups", "tile", "head"))
    return jax.shard_map(
        product_plan if sizes == (2, 4, 4) else gather_plan,
        mesh=mesh,
        in_specs=placed,
        out_specs=P(("groups", "tile"), "head", None, None, None),
        check_vma=False,
    )
```

```python
import jax
import jax.numpy as jnp
from jax import lax
from jax.experimental import pallas as pl
from jax.experimental.pallas import tpu as pltpu
from jax.sharding import PartitionSpec as P

eps_norm = 1e-05


def shifted_2(shard, axis, by):
    count = lax.axis_size(axis)
    return lax.ppermute(shard, axis, [(i, (i + by) % count) for i in range(count)])


def swapped(shard, axis, bit):
    return lax.ppermute(shard, axis, [(i, i ^ bit) for i in range(lax.axis_size(axis))])


def add_columns(operand, portion):
    return jnp.dot(operand, portion, preferred_element_type=jnp.float32)


def routing(tile_map, tile_count, decode_owner, tile_slots, head_groups):
    most_tiles = tile_map.shape[1]
    owner_tile = decode_owner // head_groups
    owner_turn = decode_owner % head_groups
    usable = jnp.arange(most_tiles)[None, :] < tile_count[:, None]
    matched = (tile_map[:, :, None] == jnp.arange(tile_slots)[None, None, :]) & usable[:, :, None]
    return owner_tile, owner_turn, matched


def gather_plan(
    features, proj_weight, proj_bias, kv_weight, key_gain, tile_map, tile_count, decode_owner
):
    tile_slots, shard_len, feature_width = features.shape
    token_rows = tile_slots * shard_len
    feature_rows = features.reshape(token_rows, feature_width)
    weight_cols = lax.all_gather(proj_weight, "tile", axis=0, tiled=True)
    projected = jnp.dot(feature_rows, weight_cols, preferred_element_type=jnp.float32)
    projected_local = (projected + proj_bias.astype(jnp.float32)).astype(jnp.bfloat16)
    kv_width = kv_weight.shape[1]
    projected_all = lax.all_gather(projected_local, "head", axis=1, tiled=True)
    key_value = add_columns(projected_all, lax.all_gather(kv_weight, "tile", axis=0, tiled=True))
    layers, head_dim = key_gain.shape
    blocks = key_value.reshape(token_rows, -1, layers, 2, head_dim)
    keys_raw = blocks[:, :, :, 0]
    inv_rms = lax.rsqrt(jnp.mean(keys_raw * keys_raw, axis=-1, keepdims=True) + eps_norm)
    keys_normed = keys_raw * inv_rms * key_gain[None, None]
    stacked = jnp.stack([keys_normed, blocks[:, :, :, 1]], axis=3).astype(jnp.bfloat16)
    per_tile = stacked.reshape(tile_slots, shard_len * kv_width)
    tile_ranks = lax.axis_size("tile")
    head_groups = lax.axis_size("head")
    most_tiles = tile_map.shape[1]
    owner_tile, owner_turn, matched = routing(
        tile_map, tile_count, decode_owner, tile_slots, head_groups
    )
    owned_by = (owner_tile[:, None] == jnp.arange(tile_ranks)[None, :]).astype(jnp.float32)
    selector = jnp.einsum("rd,rjs->jds", owned_by, matched.astype(jnp.float32))
    selector = selector.astype(jnp.bfloat16).reshape(most_tiles * tile_ranks, tile_slots)
    outgoing = add_columns(selector, per_tile).astype(jnp.bfloat16)
    outgoing = outgoing.reshape(most_tiles, tile_ranks, shard_len, kv_width)
    arrived = lax.all_to_all(outgoing, "tile", split_axis=1, concat_axis=1, tiled=True)
    gathered_rows = arrived.reshape(
        most_tiles * tile_ranks * shard_len, kv_width // head_dim, head_dim
    )
    my_turn = jnp.sum(jnp.where(owner_tile == lax.axis_index("tile"), owner_turn, 0))
    stride = 1
    while stride < head_groups:
        shifted = shifted_2(gathered_rows, "head", stride)
        gathered_rows = jnp.where(my_turn // stride % 2 == 1, shifted, gathered_rows)
        stride = stride * 2
    return gathered_rows[None, None]


def terms_body(choice, weight, near, far, own, second, mirror, first, kept_rest):
    near_product = add_columns(weight[...], near[...])
    far_product = add_columns(weight[...], far[...])
    near_kept = choice[0] == 1
    kept = jnp.where(near_kept, near_product, far_product)
    sent = jnp.where(near_kept, far_product, near_product)
    tall, width = weight.shape[0], own.shape[1]
    i = pl.program_id(0)
    rows = pl.ds(pl.multiple_of(i * tall, tall), tall)
    first[rows, :] = sent[:, :width].astype(first.dtype)

    @pl.when(i < 2)
    def _():
        own[rows, :] = kept[:, :width]
        second[rows, :] = sent[:, width:].astype(second.dtype)
        mirror[rows, :] = kept[:, width:].astype(mirror.dtype)

    @pl.when(i == 2)
    def _():
        kept_rest[...] = kept
        first[3 * tall :, :] = sent[:, width:].astype(first.dtype)


def product_terms(choice, weight, near, far):
    depth, rows = weight.shape
    columns = near.shape[1]
    width, tall = columns // 2, depth // 3
    wide, narrow = jnp.float32, jnp.bfloat16
    shapes = [
        jax.ShapeDtypeStruct((2 * tall, width), wide),
        jax.ShapeDtypeStruct((2 * tall, width), narrow),
        jax.ShapeDtypeStruct((2 * tall, width), narrow),
        jax.ShapeDtypeStruct((4 * tall, width), narrow),
        jax.ShapeDtypeStruct((tall, columns), wide),
    ]
    whole = [pl.BlockSpec(array.shape, lambda i, choice: (0, 0)) for array in (near, *shapes)]
    return pl.pallas_call(
        terms_body,
        out_shape=shapes,
        grid_spec=pltpu.PrefetchScalarGridSpec(
            num_scalar_prefetch=1,
            grid=(3,),
            in_specs=[pl.BlockSpec((tall, rows), lambda i, choice: (i, 0)), whole[0], whole[0]],
            out_specs=whole[1:],
        ),
        compiler_params=pltpu.CompilerParams(vmem_limit_bytes=32 * 1024 * 1024),
        cost_estimate=pl.CostEstimate(
            flops=4 * depth * rows * columns,
            bytes_accessed=2 * depth * rows + 4 * rows * columns + 10 * depth * width,
            transcendentals=0,
        ),
    )(choice, weight, near, far)


def product_plan(
    features, proj_weight, proj_bias, kv_weight, key_gain, tile_map, tile_count, decode_owner
):
    tile_slots, shard_len, feature_width = features.shape
    token_rows = tile_slots * shard_len
    depth = proj_weight.shape[0]
    layers, head_dim = key_gain.shape
    width = layers * head_dim
    most_tiles = tile_map.shape[1]
    group, tile, head = (lax.axis_index(name) for name in ("groups", "tile", "head"))
    first_core, first_chip = tile % 2 == 0, tile < 2
    at_end = (head == 0) | (head == 3)
    feature_rows = features.reshape(token_rows, feature_width)
    step = lax.optimization_barrier

    def moved(shard, target):
        pairs = []
        for t in range(4):
            for h in range(4):
                to_tile, to_head = target(t, h)
                pairs.append((t * 4 + h, to_tile * 4 + to_head))
        return lax.ppermute(shard, ("tile", "head"), pairs)

    def outer_core(h):
        return (h ^ h // 2) % 2

    feature_parts = [
        lax.dynamic_slice_in_dim(feature_rows, (tile ^ r) * depth, depth, axis=1) for r in range(4)
    ]

    def put_first(condition, one, other, axis):
        return jnp.concatenate(
            [jnp.where(condition, one, other), jnp.where(condition, other, one)], axis=axis
        )

    def both_heads(ours, theirs):
        return put_first(group == 0, ours, theirs, 1)

    choice = (at_end == first_core).astype(jnp.int32).reshape(1)

    def products(near, far):
        return tuple(product_terms(choice, proj_weight, near, far))

    rest = depth // 3

    def to_neighbour(block):
        return swapped(block, "head", 1)

    def over_middle(block):
        return swapped(block, "head", 3)

    def plus(block, *arrived):
        for other in arrived:
            block = block + other.astype(jnp.float32)
        return block

    def pair_sum(kept_rest, arrived):
        return plus(kept_rest, jnp.concatenate([arrived[:rest], arrived[rest:]], axis=1))

    def summed(own, arrived, pair, mirrored):
        rows = [plus(own, *arrived), plus(pair[:, :width], mirrored)]
        return jnp.concatenate([block.astype(jnp.bfloat16) for block in rows], axis=0)

    once = jnp.minimum(jnp.max(tile_count), 1)

    def in_loop(chain, given, empty):
        return lax.fori_loop(0, once, lambda _, carry: chain(carry[0]), (given, empty))[1]

    def times_features(rows, parts):
        return sum(add_columns(parts[r], rows[r]) for r in range(4))

    def finish(total, part):
        finished = []
        for k in range(2):
            entries = total[:, k * width : (k + 1) * width].reshape(token_rows, layers, head_dim)
            entries = entries + bias_part[k, :, part][None]
            if part == 0:
                squares = jnp.mean(entries * entries, axis=-1, keepdims=True)
                entries = entries * lax.rsqrt(squares + eps_norm) * key_gain[None]
            finished.append(entries.reshape(token_rows, width).astype(jnp.bfloat16))
        return jnp.concatenate(finished, axis=1).reshape(tile_slots, shard_len, 2 * width)

    owner_tile, owner_turn, matched = routing(tile_map, tile_count, decode_owner, tile_slots, 4)
    turn_of = jnp.sum(jnp.where(matched, owner_turn[:, None, None], 0), axis=(0, 1))
    owned_by = (owner_tile[:, None] == (tile ^ jnp.arange(4))[None, :]).astype(jnp.float32)
    selector = jnp.einsum("rd,rjs->djs", owned_by, matched.astype(jnp.float32))
    selector = selector.astype(jnp.bfloat16).reshape(4 * most_tiles, tile_slots)

    def rolled(rows, shifted, stride):
        odd = (turn_of // stride % 2 == 1)[:, None, None]
        return jnp.where(odd, shifted, rows)

    def outgoing(rows):
        picked = add_columns(selector, rows.reshape(tile_slots, -1)).astype(jnp.bfloat16)
        picked = picked.reshape(4, most_tiles, shard_len, 2, layers, head_dim)
        return [picked[r] for r in range(4)]

    def to_owners(picked):
        return [picked[0]] + [swapped(picked[r], "tile", r) for r in (1, 2, 3)]

    def in_order(arrived):
        even = [jnp.where(first_core, arrived[r], arrived[r ^ 1]) for r in range(4)]
        ranked = [jnp.where(first_chip, even[r], even[r ^ 2]) for r in range(4)]
        return jnp.stack(ranked, axis=1)

    column, half = group * 2 * head_dim, kv_weight.shape[0] // 2
    key_mine = lax.dynamic_slice_in_dim(kv_weight, column, head_dim, axis=1)
    value_mine = lax.dynamic_slice_in_dim(kv_weight, column + head_dim, head_dim, axis=1)
    stays = lax.dynamic_slice_in_dim(value_mine, tile // 2 * half, half, axis=0)
    leaves = lax.dynamic_slice_in_dim(value_mine, half - tile // 2 * half, half, axis=0)
    bias_rows = moved(proj_bias, lambda t, h: (h, t))
    key_block = moved(key_mine, lambda t, h: (h // 2 * 2 + outer_core(h), t))
    comes = swapped(leaves, "tile", 2)
    no_terms = tuple(
        jnp.full(shape.shape, k, shape.dtype)
        for k, shape in enumerate(jax.eval_shape(products, *[kv_weight[:, : 2 * width]] * 2))
    )
    no_tokens = tuple(
        jnp.full((tile_slots, shard_len, 2 * width), k, jnp.bfloat16) for k in range(2)
    )
    bias_rows, key_block, comes, stays, once, feature_parts = step(
        (bias_rows, key_block, comes, stays, once, feature_parts)
    )

    value_pieces = []
    for j in range(2):
        piece = jnp.where(tile // 2 == (head // 2) ^ j, stays, comes)
        value_pieces.append(
            moved(piece, lambda t, h: (t // 2 * 2 + outer_core(h), t % 2 + 2 * ((h // 2) ^ j)))
        )
    key_other = swapped(key_block, "tile", 2)
    bias_part = add_columns(bias_rows[None], kv_weight)
    value_pieces, key_block, key_other, bias_part = step(
        (value_pieces, key_block, key_other, bias_part)
    )

    key_near = put_first(tile // 2 == head // 2, key_block, key_other, 1)
    value_half = jnp.concatenate(value_pieces, axis=1)
    key_near, value_half = step((key_near, value_half))
    terms = products(key_near, swapped(key_near, "tile", 1))
    bias_part = bias_part + swapped(bias_part, "tile", 1)
    terms, value_half, bias_part = step((terms, value_half, bias_part))

    def values_terms(given):
        value_half, bias_part = given
        other, bias_other = step((swapped(value_half, "tile", 2), swapped(bias_part, "tile", 2)))
        near = step(put_first(first_chip, value_half, other, 0))
        terms = products(near, swapped(near, "tile", 1))
        return (other, bias_other), (terms, bias_part + bias_other)

    empty = no_terms, bias_part
    own, second, mirror, first, kept_rest = terms
    second, mirror, first, (value_terms, bias_part) = step(
        (
            swapped(second, "head", 2),
            over_middle(mirror),
            to_neighbour(first),
            in_loop(values_terms, (value_half, bias_part), empty),
        )
    )
    bias_part = bias_part.reshape(2, layers, 2, head_dim)

    value_own, value_second, value_mirror, value_first, value_kept = value_terms
    pair = pair_sum(kept_rest, first[2 * rest :])
    pair, value_rest = step((pair, value_first[2 * rest :]))
    mirrored, value_rest, value_first, value_second, value_mirror = step(
        (
            over_middle(pair[:, width:].astype(jnp.bfloat16)),
            to_neighbour(value_rest),
            value_first[: 2 * rest],
            value_second,
            value_mirror,
        )
    )
    own = summed(own, (second, mirror, first[: 2 * rest]), pair, mirrored)

    def keys_product(own):
        across_x, across_y = step((swapped(own, "tile", 2), swapped(own, "groups", 1)))
        rows_0 = step(both_heads(own, across_y))
        diagonal, rows_1 = step((swapped(across_y, "tile", 2), swapped(rows_0, "tile", 1)))
        rows_2 = step(both_heads(across_x, diagonal))
        rows = [rows_0, rows_1, rows_2, swapped(rows_2, "tile", 1)]
        return across_x, finish(times_features(rows, feature_parts), 0)

    pair = pair_sum(value_kept, value_rest)
    middle = jnp.concatenate([value_mirror, pair[:, width:].astype(jnp.bfloat16)], axis=0)
    pair, middle = step((pair, middle))
    second, middle, first, keys = step(
        (
            swapped(value_second, "head", 2),
            over_middle(middle),
            to_neighbour(value_first),
            in_loop(keys_product, own, no_tokens[0]),
        )
    )
    arrived = second, middle[: 2 * rest], first
    own = summed(value_own, arrived, pair, middle[2 * rest :])

    shifted, across_x, across_y = step(
        (shifted_2(keys, "head", 1), swapped(own, "tile", 2), swapped(own, "groups", 1))
    )

    def values_product(given):
        own, across_x, across_y = given
        rows_0 = step(both_heads(own, across_y))
        middle = depth // 2
        upper, lower, rows_1 = step(
            (
                swapped(across_x[:middle], "groups", 1),
                swapped(across_y[middle:], "tile", 2),
                swapped(rows_0, "tile", 1),
            )
        )
        rows_2 = step(both_heads(across_x, jnp.concatenate([upper, lower], axis=0)))
        rows = [rows_0, rows_1, rows_2, swapped(rows_2, "tile", 1)]
        return (across_y, own, across_x), finish(times_features(rows, feature_parts), 1)

    keys = step(rolled(keys, shifted, 1))
    values = in_loop(values_product, (own, across_x, across_y), no_tokens[1])
    shifted, values = step((shifted_2(keys, "head", 2), values))

    picked = outgoing(rolled(keys, shifted, 2))
    shifted, picked = step((shifted_2(values, "head", 1), picked))

    values = step(rolled(values, shifted, 1))
    arrived, shifted = step((to_owners(picked), shifted_2(values, "head", 2)))

    value_cache = in_order(to_owners(outgoing(rolled(values, shifted, 2))))
    cache = jnp.stack([in_order(arrived), value_cache], axis=-2)
    return cache.reshape(1, 1, most_tiles * 4 * shard_len, 4 * layers, head_dim)


def solution(mesh):
    placed = (
        P("groups", "tile", None),
        P("tile", "head"),
        P("head"),
        P("tile", "head"),
        P(),
        P("groups", None),
        P("groups"),
        P("groups"),
    )
    sizes = tuple(mesh.shape[name] for name in ("groups", "tile", "head"))
    return jax.shard_map(
        product_plan if sizes == (2, 4, 4) else gather_plan,
        mesh=mesh,
        in_specs=placed,
        out_specs=P(("groups", "tile"), "head", None, None, None),
        check_vma=False,
    )
```

```python
import jax
import jax.numpy as jnp
from jax import lax
from jax.experimental import pallas as pl
from jax.experimental.pallas import tpu as pltpu
from jax.sharding import PartitionSpec as P

eps_norm = 1e-05


def shifted_2(shard, axis, by):
    count = lax.axis_size(axis)
    return lax.ppermute(shard, axis, [(i, (i + by) % count) for i in range(count)])


def swapped(shard, axis, bit):
    return lax.ppermute(shard, axis, [(i, i ^ bit) for i in range(lax.axis_size(axis))])


def add_columns(operand, portion):
    return jnp.dot(operand, portion, preferred_element_type=jnp.float32)


def routing(tile_map, tile_count, decode_owner, tile_slots, head_groups):
    most_tiles = tile_map.shape[1]
    owner_tile = decode_owner // head_groups
    owner_turn = decode_owner % head_groups
    usable = jnp.arange(most_tiles)[None, :] < tile_count[:, None]
    matched = (tile_map[:, :, None] == jnp.arange(tile_slots)[None, None, :]) & usable[:, :, None]
    return owner_tile, owner_turn, matched


def gather_plan(
    features, proj_weight, proj_bias, kv_weight, key_gain, tile_map, tile_count, decode_owner
):
    tile_slots, shard_len, feature_width = features.shape
    token_rows = tile_slots * shard_len
    feature_rows = features.reshape(token_rows, feature_width)
    weight_cols = lax.all_gather(proj_weight, "tile", axis=0, tiled=True)
    projected = jnp.dot(feature_rows, weight_cols, preferred_element_type=jnp.float32)
    projected_local = (projected + proj_bias.astype(jnp.float32)).astype(jnp.bfloat16)
    kv_width = kv_weight.shape[1]
    projected_all = lax.all_gather(projected_local, "head", axis=1, tiled=True)
    key_value = add_columns(projected_all, lax.all_gather(kv_weight, "tile", axis=0, tiled=True))
    layers, head_dim = key_gain.shape
    blocks = key_value.reshape(token_rows, -1, layers, 2, head_dim)
    keys_raw = blocks[:, :, :, 0]
    inv_rms = lax.rsqrt(jnp.mean(keys_raw * keys_raw, axis=-1, keepdims=True) + eps_norm)
    keys_normed = keys_raw * inv_rms * key_gain[None, None]
    stacked = jnp.stack([keys_normed, blocks[:, :, :, 1]], axis=3).astype(jnp.bfloat16)
    per_tile = stacked.reshape(tile_slots, shard_len * kv_width)
    tile_ranks = lax.axis_size("tile")
    head_groups = lax.axis_size("head")
    most_tiles = tile_map.shape[1]
    owner_tile, owner_turn, matched = routing(
        tile_map, tile_count, decode_owner, tile_slots, head_groups
    )
    owned_by = (owner_tile[:, None] == jnp.arange(tile_ranks)[None, :]).astype(jnp.float32)
    selector = jnp.einsum("rd,rjs->jds", owned_by, matched.astype(jnp.float32))
    selector = selector.astype(jnp.bfloat16).reshape(most_tiles * tile_ranks, tile_slots)
    outgoing = add_columns(selector, per_tile).astype(jnp.bfloat16)
    outgoing = outgoing.reshape(most_tiles, tile_ranks, shard_len, kv_width)
    arrived = lax.all_to_all(outgoing, "tile", split_axis=1, concat_axis=1, tiled=True)
    gathered_rows = arrived.reshape(
        most_tiles * tile_ranks * shard_len, kv_width // head_dim, head_dim
    )
    my_turn = jnp.sum(jnp.where(owner_tile == lax.axis_index("tile"), owner_turn, 0))
    stride = 1
    while stride < head_groups:
        shifted = shifted_2(gathered_rows, "head", stride)
        gathered_rows = jnp.where(my_turn // stride % 2 == 1, shifted, gathered_rows)
        stride = stride * 2
    return gathered_rows[None, None]


def terms_body(choice, weight, near, far, own, second, mirror, first, *kept_rest):
    near_product = add_columns(weight[...], near[...])
    far_product = add_columns(weight[...], far[...])
    near_kept = choice[0] == 1
    kept = jnp.where(near_kept, near_product, far_product)
    sent = jnp.where(near_kept, far_product, near_product)
    tall, width = weight.shape[0], own.shape[1]
    i = pl.program_id(0)
    rows = pl.ds(pl.multiple_of(i * tall, tall), tall)
    first[rows, :] = sent[:, :width].astype(first.dtype)

    def write_direct():
        own[rows, :] = kept[:, :width]
        second[rows, :] = sent[:, width:].astype(second.dtype)
        mirror[rows, :] = kept[:, width:].astype(mirror.dtype)

    if len(kept_rest) == 0:
        write_direct()
    else:
        pl.when(i < 2)(write_direct)

        @pl.when(i == 2)
        def _():
            kept_rest[0][...] = kept
            first[3 * tall :, :] = sent[:, width:].astype(first.dtype)


def product_terms(choice, weight, near, far, all_direct):
    depth, rows = weight.shape
    columns = near.shape[1]
    width, tall = columns // 2, depth // 3
    direct = depth if all_direct else 2 * tall
    wide, narrow = jnp.float32, jnp.bfloat16
    shapes = [
        jax.ShapeDtypeStruct((direct, width), wide),
        jax.ShapeDtypeStruct((direct, width), narrow),
        jax.ShapeDtypeStruct((direct, width), narrow),
        jax.ShapeDtypeStruct((2 * depth - direct, width), narrow),
    ]
    if not all_direct:
        shapes = shapes + [jax.ShapeDtypeStruct((tall, columns), wide)]
    whole = [pl.BlockSpec(array.shape, lambda i, choice: (0, 0)) for array in (near, *shapes)]
    return pl.pallas_call(
        terms_body,
        out_shape=shapes,
        grid_spec=pltpu.PrefetchScalarGridSpec(
            num_scalar_prefetch=1,
            grid=(3,),
            in_specs=[pl.BlockSpec((tall, rows), lambda i, choice: (i, 0)), whole[0], whole[0]],
            out_specs=whole[1:],
        ),
        compiler_params=pltpu.CompilerParams(vmem_limit_bytes=32 * 1024 * 1024),
        cost_estimate=pl.CostEstimate(
            flops=4 * depth * rows * columns,
            bytes_accessed=2 * depth * rows + 4 * rows * columns + 10 * depth * width,
            transcendentals=0,
        ),
    )(choice, weight, near, far)


def product_plan(
    features, proj_weight, proj_bias, kv_weight, key_gain, tile_map, tile_count, decode_owner
):
    tile_slots, shard_len, feature_width = features.shape
    token_rows = tile_slots * shard_len
    depth = proj_weight.shape[0]
    layers, head_dim = key_gain.shape
    width = layers * head_dim
    most_tiles = tile_map.shape[1]
    group, tile, head = (lax.axis_index(name) for name in ("groups", "tile", "head"))
    first_core, first_chip = tile % 2 == 0, tile < 2
    at_end = (head == 0) | (head == 3)
    feature_rows = features.reshape(token_rows, feature_width)
    step = lax.optimization_barrier

    def moved(shard, target):
        pairs = []
        for t in range(4):
            for h in range(4):
                to_tile, to_head = target(t, h)
                pairs.append((t * 4 + h, to_tile * 4 + to_head))
        return lax.ppermute(shard, ("tile", "head"), pairs)

    def outer_core(h):
        return (h ^ h // 2) % 2

    feature_parts = [
        lax.dynamic_slice_in_dim(feature_rows, (tile ^ r) * depth, depth, axis=1) for r in range(4)
    ]

    def put_first(condition, one, other, axis):
        return jnp.concatenate(
            [jnp.where(condition, one, other), jnp.where(condition, other, one)], axis=axis
        )

    def both_heads(ours, theirs):
        return put_first(group == 0, ours, theirs, 1)

    choice = (at_end == first_core).astype(jnp.int32).reshape(1)

    def products(near, far, all_direct):
        return tuple(product_terms(choice, proj_weight, near, far, all_direct))

    rest = depth // 3

    def to_neighbour(block):
        return swapped(block, "head", 1)

    def over_middle(block):
        return swapped(block, "head", 3)

    def plus(block, *arrived):
        for other in arrived:
            block = block + other.astype(jnp.float32)
        return block

    once = jnp.minimum(jnp.max(tile_count), 1)

    def in_loop(chain, given, empty):
        return lax.fori_loop(0, once, lambda _, carry: chain(carry[0]), (given, empty))[1]

    def times_features(rows, parts):
        return sum(add_columns(parts[r], rows[r]) for r in range(4))

    def finish(total, part):
        finished = []
        for k in range(2):
            entries = total[:, k * width : (k + 1) * width].reshape(token_rows, layers, head_dim)
            entries = entries + bias_part[k, :, part][None]
            if part == 0:
                squares = jnp.mean(entries * entries, axis=-1, keepdims=True)
                entries = entries * lax.rsqrt(squares + eps_norm) * key_gain[None]
            finished.append(entries.reshape(token_rows, width).astype(jnp.bfloat16))
        return jnp.concatenate(finished, axis=1).reshape(tile_slots, shard_len, 2 * width)

    owner_tile, owner_turn, matched = routing(tile_map, tile_count, decode_owner, tile_slots, 4)
    turn_of = jnp.sum(jnp.where(matched, owner_turn[:, None, None], 0), axis=(0, 1))
    owned_by = (owner_tile[:, None] == (tile ^ jnp.arange(4))[None, :]).astype(jnp.float32)
    selector = jnp.einsum("rd,rjs->djs", owned_by, matched.astype(jnp.float32))
    selector = selector.astype(jnp.bfloat16).reshape(4 * most_tiles, tile_slots)

    def rolled(rows, shifted, stride):
        odd = (turn_of // stride % 2 == 1)[:, None, None]
        return jnp.where(odd, shifted, rows)

    def outgoing(rows):
        picked = add_columns(selector, rows.reshape(tile_slots, -1)).astype(jnp.bfloat16)
        picked = picked.reshape(4, most_tiles, shard_len, 2, layers, head_dim)
        return [picked[r] for r in range(4)]

    def to_owners(picked):
        return [picked[0]] + [swapped(picked[r], "tile", r) for r in (1, 2, 3)]

    def in_order(arrived):
        even = [jnp.where(first_core, arrived[r], arrived[r ^ 1]) for r in range(4)]
        ranked = [jnp.where(first_chip, even[r], even[r ^ 2]) for r in range(4)]
        return jnp.stack(ranked, axis=1)

    column, half = group * 2 * head_dim, kv_weight.shape[0] // 2
    key_mine = lax.dynamic_slice_in_dim(kv_weight, column, head_dim, axis=1)
    value_mine = lax.dynamic_slice_in_dim(kv_weight, column + head_dim, head_dim, axis=1)
    stays = lax.dynamic_slice_in_dim(value_mine, tile // 2 * half, half, axis=0)
    leaves = lax.dynamic_slice_in_dim(value_mine, half - tile // 2 * half, half, axis=0)
    bias_rows = moved(proj_bias, lambda t, h: (h, t))
    key_block = moved(key_mine, lambda t, h: (h // 2 * 2 + outer_core(h), t))
    comes = swapped(leaves, "tile", 2)
    no_terms = tuple(
        jnp.full((depth, width), once + k, dtype)
        for k, dtype in enumerate((jnp.float32, jnp.bfloat16, jnp.bfloat16, jnp.bfloat16))
    )
    no_tokens = tuple(
        jnp.full((tile_slots, shard_len, 2 * width), once + k, jnp.bfloat16) for k in range(2)
    )
    bias_rows, key_block, comes, stays, once, feature_parts, no_terms, no_tokens = step(
        (bias_rows, key_block, comes, stays, once, feature_parts, no_terms, no_tokens)
    )

    value_pieces = []
    for j in range(2):
        piece = jnp.where(tile // 2 == (head // 2) ^ j, stays, comes)
        value_pieces.append(
            moved(piece, lambda t, h: (t // 2 * 2 + outer_core(h), t % 2 + 2 * ((h // 2) ^ j)))
        )
    key_other = swapped(key_block, "tile", 2)
    bias_part = add_columns(bias_rows[None], kv_weight)
    value_pieces, key_block, key_other, bias_part = step(
        (value_pieces, key_block, key_other, bias_part)
    )

    key_near = put_first(tile // 2 == head // 2, key_block, key_other, 1)
    value_half = jnp.concatenate(value_pieces, axis=1)
    key_near, value_half = step((key_near, value_half))
    terms = products(key_near, swapped(key_near, "tile", 1), False)
    bias_part = bias_part + swapped(bias_part, "tile", 1)
    terms, value_half, bias_part = step((terms, value_half, bias_part))

    def values_terms(given):
        value_half, bias_part = given
        other, bias_other = step((swapped(value_half, "tile", 2), swapped(bias_part, "tile", 2)))
        near = step(put_first(first_chip, value_half, other, 0))
        terms = products(near, swapped(near, "tile", 1), True)
        return (other, bias_other), (terms, bias_part + bias_other)

    empty = no_terms, bias_part
    own, second, mirror, first, kept_rest = terms
    second, mirror, first, (value_terms, bias_part) = step(
        (
            swapped(second, "head", 2),
            over_middle(mirror),
            to_neighbour(first),
            in_loop(values_terms, (value_half, bias_part), empty),
        )
    )
    bias_part = bias_part.reshape(2, layers, 2, head_dim)

    direct = 2 * rest
    arrived = jnp.concatenate([first[direct : 3 * rest], first[3 * rest :]], axis=1)
    pair = plus(kept_rest, arrived)
    pair, mirrored, value_terms = step(
        (pair, over_middle(pair[:, width:].astype(jnp.bfloat16)), value_terms)
    )
    blocks = [plus(own, second, mirror, first[:direct]), plus(pair[:, :width], mirrored)]
    own = jnp.concatenate([block.astype(jnp.bfloat16) for block in blocks], axis=0)

    def rest_of_plane(given, part):
        own, across_x, across_y = given
        rows_0 = step(both_heads(own, across_y))
        middle = depth // 2
        upper, lower, rows_1 = step(
            (
                swapped(across_x[:middle], "groups", 1),
                swapped(across_y[middle:], "tile", 2),
                swapped(rows_0, "tile", 1),
            )
        )
        rows_2 = step(both_heads(across_x, jnp.concatenate([upper, lower], axis=0)))
        rows = [rows_0, rows_1, rows_2, swapped(rows_2, "tile", 1)]
        return finish(times_features(rows, feature_parts), part)

    def keys_product(own):
        across_x, across_y = step((swapped(own, "tile", 2), swapped(own, "groups", 1)))
        return across_x, rest_of_plane((own, across_x, across_y), 0)

    value_own, second, mirror, first = value_terms
    second, mirror, first, keys = step(
        (
            swapped(second, "head", 2),
            over_middle(mirror),
            to_neighbour(first),
            in_loop(keys_product, own, no_tokens[0]),
        )
    )
    own = plus(value_own, second, mirror, first).astype(jnp.bfloat16)

    shifted, across_x, across_y = step(
        (shifted_2(keys, "head", 1), swapped(own, "tile", 2), swapped(own, "groups", 1))
    )

    def values_product(given):
        own, across_x, across_y = given
        return (across_y, own, across_x), rest_of_plane(given, 1)

    keys = step(rolled(keys, shifted, 1))
    values = in_loop(values_product, (own, across_x, across_y), no_tokens[1])
    shifted, values = step((shifted_2(keys, "head", 2), values))

    picked = outgoing(rolled(keys, shifted, 2))
    shifted, picked = step((shifted_2(values, "head", 1), picked))

    values = step(rolled(values, shifted, 1))
    arrived, shifted = step((to_owners(picked), shifted_2(values, "head", 2)))

    value_cache = in_order(to_owners(outgoing(rolled(values, shifted, 2))))
    cache = jnp.stack([in_order(arrived), value_cache], axis=-2)
    return cache.reshape(1, 1, most_tiles * 4 * shard_len, 4 * layers, head_dim)


def solution(mesh):
    placed = (
        P("groups", "tile", None),
        P("tile", "head"),
        P("head"),
        P("tile", "head"),
        P(),
        P("groups", None),
        P("groups"),
        P("groups"),
    )
    sizes = tuple(mesh.shape[name] for name in ("groups", "tile", "head"))
    return jax.shard_map(
        product_plan if sizes == (2, 4, 4) else gather_plan,
        mesh=mesh,
        in_specs=placed,
        out_specs=P(("groups", "tile"), "head", None, None, None),
        check_vma=False,
    )
```

```python
import jax
import jax.numpy as jnp
from jax import lax
from jax.experimental import pallas as pl
from jax.experimental.pallas import tpu as pltpu
from jax.sharding import PartitionSpec as P

eps_norm = 1e-05


def shifted_2(shard, axis, by):
    count = lax.axis_size(axis)
    return lax.ppermute(shard, axis, [(i, (i + by) % count) for i in range(count)])


def swapped(shard, axis, bit):
    return lax.ppermute(shard, axis, [(i, i ^ bit) for i in range(lax.axis_size(axis))])


def add_columns(operand, portion):
    return jnp.dot(operand, portion, preferred_element_type=jnp.float32)


def routing(tile_map, tile_count, decode_owner, tile_slots, head_groups):
    most_tiles = tile_map.shape[1]
    owner_tile = decode_owner // head_groups
    owner_turn = decode_owner % head_groups
    usable = jnp.arange(most_tiles)[None, :] < tile_count[:, None]
    matched = (tile_map[:, :, None] == jnp.arange(tile_slots)[None, None, :]) & usable[:, :, None]
    return owner_tile, owner_turn, matched


def gather_plan(
    features, proj_weight, proj_bias, kv_weight, key_gain, tile_map, tile_count, decode_owner
):
    tile_slots, shard_len, feature_width = features.shape
    token_rows = tile_slots * shard_len
    feature_rows = features.reshape(token_rows, feature_width)
    weight_cols = lax.all_gather(proj_weight, "tile", axis=0, tiled=True)
    projected = jnp.dot(feature_rows, weight_cols, preferred_element_type=jnp.float32)
    projected_local = (projected + proj_bias.astype(jnp.float32)).astype(jnp.bfloat16)
    kv_width = kv_weight.shape[1]
    projected_all = lax.all_gather(projected_local, "head", axis=1, tiled=True)
    key_value = add_columns(projected_all, lax.all_gather(kv_weight, "tile", axis=0, tiled=True))
    layers, head_dim = key_gain.shape
    blocks = key_value.reshape(token_rows, -1, layers, 2, head_dim)
    keys_raw = blocks[:, :, :, 0]
    inv_rms = lax.rsqrt(jnp.mean(keys_raw * keys_raw, axis=-1, keepdims=True) + eps_norm)
    keys_normed = keys_raw * inv_rms * key_gain[None, None]
    stacked = jnp.stack([keys_normed, blocks[:, :, :, 1]], axis=3).astype(jnp.bfloat16)
    per_tile = stacked.reshape(tile_slots, shard_len * kv_width)
    tile_ranks = lax.axis_size("tile")
    head_groups = lax.axis_size("head")
    most_tiles = tile_map.shape[1]
    owner_tile, owner_turn, matched = routing(
        tile_map, tile_count, decode_owner, tile_slots, head_groups
    )
    owned_by = (owner_tile[:, None] == jnp.arange(tile_ranks)[None, :]).astype(jnp.float32)
    selector = jnp.einsum("rd,rjs->jds", owned_by, matched.astype(jnp.float32))
    selector = selector.astype(jnp.bfloat16).reshape(most_tiles * tile_ranks, tile_slots)
    outgoing = add_columns(selector, per_tile).astype(jnp.bfloat16)
    outgoing = outgoing.reshape(most_tiles, tile_ranks, shard_len, kv_width)
    arrived = lax.all_to_all(outgoing, "tile", split_axis=1, concat_axis=1, tiled=True)
    gathered_rows = arrived.reshape(
        most_tiles * tile_ranks * shard_len, kv_width // head_dim, head_dim
    )
    my_turn = jnp.sum(jnp.where(owner_tile == lax.axis_index("tile"), owner_turn, 0))
    stride = 1
    while stride < head_groups:
        shifted = shifted_2(gathered_rows, "head", stride)
        gathered_rows = jnp.where(my_turn // stride % 2 == 1, shifted, gathered_rows)
        stride = stride * 2
    return gathered_rows[None, None]


def terms_body(choice, weight, near, far, own, second, mirror, kept_rest, first, *rest):
    near_product = add_columns(weight[...], near[...])
    far_product = add_columns(weight[...], far[...])
    near_kept = choice[0] == 1
    kept = jnp.where(near_kept, near_product, far_product)
    sent = jnp.where(near_kept, far_product, near_product)
    tall, width = weight.shape[0], own.shape[1]
    i = pl.program_id(0)

    @pl.when(i < 2)
    def _():
        rows = pl.ds(pl.multiple_of(i * tall, tall), tall)
        own[rows, :] = kept[:, :width]
        second[rows, :] = sent[:, width:].astype(second.dtype)
        mirror[rows, :] = kept[:, width:].astype(mirror.dtype)
        first[rows, :] = sent[:, :width].astype(first.dtype)

    @pl.when(i == 2)
    def _():
        kept_rest[...] = kept
        target, start = (rest[0], 0) if rest else (first, 2 * tall)
        target[start : start + tall, :] = sent[:, :width].astype(target.dtype)
        target[start + tall :, :] = sent[:, width:].astype(target.dtype)


def term_shapes(depth, width, joined):
    tall, wide, narrow = depth // 3, jnp.float32, jnp.bfloat16
    rows = [(2 * tall, wide), (2 * tall, narrow), (2 * tall, narrow), (tall, wide)]
    rows = rows + ([(4 * tall, narrow)] if joined else [(2 * tall, narrow)] * 2)
    return [jax.ShapeDtypeStruct((n, 2 * width if n == tall else width), t) for n, t in rows]


def product_terms(choice, weight, near, far, joined):
    depth, rows = weight.shape
    columns = near.shape[1]
    tall = depth // 3
    shapes = term_shapes(depth, columns // 2, joined)
    whole = [pl.BlockSpec(array.shape, lambda i, choice: (0, 0)) for array in (near, *shapes)]
    return pl.pallas_call(
        terms_body,
        out_shape=shapes,
        grid_spec=pltpu.PrefetchScalarGridSpec(
            num_scalar_prefetch=1,
            grid=(3,),
            in_specs=[pl.BlockSpec((tall, rows), lambda i, choice: (i, 0)), whole[0], whole[0]],
            out_specs=whole[1:],
        ),
        compiler_params=pltpu.CompilerParams(vmem_limit_bytes=32 * 1024 * 1024),
        cost_estimate=pl.CostEstimate(
            flops=4 * depth * rows * columns,
            bytes_accessed=2 * depth * rows + 4 * rows * columns + 5 * depth * columns,
            transcendentals=0,
        ),
    )(choice, weight, near, far)


def blank_arrays(shapes):
    return pl.pallas_call(
        lambda *refs: None,
        out_shape=shapes,
        out_specs=[pl.BlockSpec(memory_space=pl.ANY)] * len(shapes),
    )()


def product_plan(
    features, proj_weight, proj_bias, kv_weight, key_gain, tile_map, tile_count, decode_owner
):
    tile_slots, shard_len, feature_width = features.shape
    token_rows = tile_slots * shard_len
    depth = proj_weight.shape[0]
    layers, head_dim = key_gain.shape
    width = layers * head_dim
    most_tiles = tile_map.shape[1]
    group, tile, head = (lax.axis_index(name) for name in ("groups", "tile", "head"))
    first_core, first_chip = tile % 2 == 0, tile < 2
    at_end = (head == 0) | (head == 3)
    feature_rows = features.reshape(token_rows, feature_width)
    step = lax.optimization_barrier

    def moved(shard, target):
        pairs = []
        for t in range(4):
            for h in range(4):
                to_tile, to_head = target(t, h)
                pairs.append((t * 4 + h, to_tile * 4 + to_head))
        return lax.ppermute(shard, ("tile", "head"), pairs)

    def outer_core(h):
        return (h ^ h // 2) % 2

    feature_parts = [
        lax.dynamic_slice_in_dim(feature_rows, (tile ^ r) * depth, depth, axis=1) for r in range(4)
    ]

    def put_first(condition, one, other, axis):
        return jnp.concatenate(
            [jnp.where(condition, one, other), jnp.where(condition, other, one)], axis=axis
        )

    def both_heads(ours, theirs):
        return put_first(group == 0, ours, theirs, 1)

    choice = (at_end == first_core).astype(jnp.int32).reshape(1)

    def products(near, far, joined):
        return tuple(product_terms(choice, proj_weight, near, far, joined))

    rest = depth // 3

    def to_neighbour(block):
        return swapped(block, "head", 1)

    def over_middle(block):
        return swapped(block, "head", 3)

    def plus(block, *arrived):
        for other in arrived:
            block = block + other.astype(jnp.float32)
        return block

    once = jnp.minimum(jnp.max(tile_count), 1)

    def in_loop(chain, given, empty):
        return lax.fori_loop(0, once, lambda _, carry: chain(carry[0]), (given, empty))[1]

    def times_features(rows, parts):
        return sum(add_columns(parts[r], rows[r]) for r in range(4))

    def finish(total, part):
        finished = []
        for k in range(2):
            entries = total[:, k * width : (k + 1) * width].reshape(token_rows, layers, head_dim)
            entries = entries + bias_part[k, :, part][None]
            if part == 0:
                squares = jnp.mean(entries * entries, axis=-1, keepdims=True)
                entries = entries * lax.rsqrt(squares + eps_norm) * key_gain[None]
            finished.append(entries.reshape(token_rows, width).astype(jnp.bfloat16))
        return jnp.concatenate(finished, axis=1).reshape(tile_slots, shard_len, 2 * width)

    owner_tile, owner_turn, matched = routing(tile_map, tile_count, decode_owner, tile_slots, 4)
    turn_of = jnp.sum(jnp.where(matched, owner_turn[:, None, None], 0), axis=(0, 1))
    owned_by = (owner_tile[:, None] == (tile ^ jnp.arange(4))[None, :]).astype(jnp.float32)
    selector = jnp.einsum("rd,rjs->djs", owned_by, matched.astype(jnp.float32))
    selector = selector.astype(jnp.bfloat16).reshape(4 * most_tiles, tile_slots)

    turned = [turn_of // stride % 2 == 1 for stride in (1, 2)]

    def rolled(rows, shifted, stride):
        return jnp.where(turned[stride - 1][:, None, None], shifted, rows)

    def outgoing(rows):
        picked = add_columns(selector, rows.reshape(tile_slots, -1)).astype(jnp.bfloat16)
        picked = picked.reshape(4, most_tiles, shard_len, 2, layers, head_dim)
        return [picked[r] for r in range(4)]

    def to_owners(picked):
        return [picked[0]] + [swapped(picked[r], "tile", r) for r in (1, 2, 3)]

    def in_order(arrived):
        even = [jnp.where(first_core, arrived[r], arrived[r ^ 1]) for r in range(4)]
        ranked = [jnp.where(first_chip, even[r], even[r ^ 2]) for r in range(4)]
        return jnp.stack(ranked, axis=1)

    column, half = group * 2 * head_dim, kv_weight.shape[0] // 2

    def halves(part):
        mine = lax.dynamic_slice_in_dim(kv_weight, column + part * head_dim, head_dim, axis=1)
        ours = lax.dynamic_slice_in_dim(mine, tile // 2 * half, half, axis=0)
        return ours, lax.dynamic_slice_in_dim(mine, half - tile // 2 * half, half, axis=0)

    def to_planes(stays, comes):
        pieces = []
        for j in range(2):
            piece = jnp.where(tile // 2 == (head // 2) ^ j, stays, comes)
            pieces.append(
                moved(piece, lambda t, h: (t // 2 * 2 + outer_core(h), t % 2 + 2 * ((h // 2) ^ j)))
            )
        return pieces

    key_stays, key_leaves = halves(0)
    bias_rows = moved(proj_bias, lambda t, h: (h, t))
    key_stays, key_comes, bias_rows, once = step(
        (key_stays, swapped(key_leaves, "tile", 2), bias_rows, once)
    )

    value_stays, value_leaves = halves(1)
    tokens = jax.ShapeDtypeStruct((tile_slots, shard_len, 2 * width), jnp.bfloat16)
    shapes = term_shapes(depth, width, False) + [tokens, tokens]
    *no_terms, no_keys, no_values = blank_arrays(shapes)
    bias_part = add_columns(bias_rows[None], kv_weight)
    key_pieces, value_stays, value_comes, bias_part, turned, selector = step(
        (
            to_planes(key_stays, key_comes),
            value_stays,
            swapped(value_leaves, "tile", 2),
            bias_part,
            turned,
            selector,
        )
    )

    key_half = jnp.concatenate(key_pieces, axis=1)
    key_half, key_other, value_pieces, feature_parts = step(
        (
            key_half,
            swapped(key_half, "tile", 2),
            to_planes(value_stays, value_comes),
            feature_parts,
        )
    )

    key_near = put_first(first_chip, key_half, key_other, 0)
    value_half = jnp.concatenate(value_pieces, axis=1)
    key_near, value_half = step((key_near, value_half))
    terms = products(key_near, swapped(key_near, "tile", 1), True)
    bias_part = bias_part + swapped(bias_part, "tile", 1)
    terms, value_half, bias_part = step((terms, value_half, bias_part))

    def values_terms(given):
        value_half, bias_part = given
        other, bias_other = step((swapped(value_half, "tile", 2), swapped(bias_part, "tile", 2)))
        near = step(put_first(first_chip, value_half, other, 0))
        terms = products(near, swapped(near, "tile", 1), False)
        return (other, bias_other), (terms, bias_part + bias_other)

    empty = tuple(no_terms), bias_part
    own, second, mirror, kept_rest, first = terms
    second, mirror, first, (value_terms, bias_part) = step(
        (
            swapped(second, "head", 2),
            over_middle(mirror),
            to_neighbour(first),
            in_loop(values_terms, (value_half, bias_part), empty),
        )
    )
    bias_part = bias_part.reshape(2, layers, 2, head_dim)

    def pair_sum(kept_rest, arrived):
        return plus(kept_rest, jnp.concatenate([arrived[:rest], arrived[rest:]], axis=1))

    def summed(own, arrived, pair, mirrored):
        blocks = [plus(own, *arrived), plus(pair[:, :width], mirrored)]
        return jnp.concatenate([block.astype(jnp.bfloat16) for block in blocks], axis=0)

    value_own, value_second, value_mirror, value_kept, value_first, value_rest = value_terms
    pair = pair_sum(kept_rest, first[2 * rest :])
    value_rest, mirrored, value_second, value_mirror, value_first = step(
        (
            to_neighbour(value_rest),
            over_middle(pair[:, width:].astype(jnp.bfloat16)),
            value_second,
            value_mirror,
            value_first,
        )
    )
    own = summed(own, (second, mirror, first[: 2 * rest]), pair, mirrored)

    def rest_of_plane(given, part):
        own, across_x, across_y = given
        rows_0 = step(both_heads(own, across_y))
        middle = depth // 2
        upper, lower, rows_1 = step(
            (
                swapped(across_x[:middle], "groups", 1),
                swapped(across_y[middle:], "tile", 2),
                swapped(rows_0, "tile", 1),
            )
        )
        rows_2 = step(both_heads(across_x, jnp.concatenate([upper, lower], axis=0)))
        rows = [rows_0, rows_1, rows_2, swapped(rows_2, "tile", 1)]
        return finish(times_features(rows, feature_parts), part)

    def keys_product(own):
        across_x, across_y = step((swapped(own, "tile", 2), swapped(own, "groups", 1)))
        rows_0 = step(both_heads(own, across_y))
        diagonal, rows_1 = step((swapped(across_y, "tile", 2), swapped(rows_0, "tile", 1)))
        rows_2 = step(both_heads(across_x, diagonal))
        rows = [rows_0, rows_1, rows_2, swapped(rows_2, "tile", 1)]
        return across_x, finish(times_features(rows, feature_parts), 0)

    pair = pair_sum(value_kept, value_rest)
    middle = jnp.concatenate([value_mirror, pair[:, width:].astype(jnp.bfloat16)], axis=0)
    pair, middle = step((pair, middle))
    second, middle, first, keys = step(
        (
            swapped(value_second, "head", 2),
            over_middle(middle),
            to_neighbour(value_first),
            in_loop(keys_product, own, no_keys),
        )
    )
    own = summed(value_own, (second, middle[: 2 * rest], first), pair, middle[2 * rest :])

    shifted, across_x, across_y = step(
        (shifted_2(keys, "head", 1), swapped(own, "tile", 2), swapped(own, "groups", 1))
    )

    def values_product(given):
        own, across_x, across_y = given
        return (across_y, own, across_x), rest_of_plane(given, 1)

    keys = step(rolled(keys, shifted, 1))
    values = in_loop(values_product, (own, across_x, across_y), no_values)
    shifted, values = step((shifted_2(keys, "head", 2), values))

    picked = outgoing(rolled(keys, shifted, 2))
    shifted, picked = step((shifted_2(values, "head", 1), picked))

    values = step(rolled(values, shifted, 1))
    arrived, shifted = step((to_owners(picked), shifted_2(values, "head", 2)))

    value_cache = in_order(to_owners(outgoing(rolled(values, shifted, 2))))
    cache = jnp.stack([in_order(arrived), value_cache], axis=-2)
    return cache.reshape(1, 1, most_tiles * 4 * shard_len, 4 * layers, head_dim)


def solution(mesh):
    placed = (
        P("groups", "tile", None),
        P("tile", "head"),
        P("head"),
        P("tile", "head"),
        P(),
        P("groups", None),
        P("groups"),
        P("groups"),
    )
    sizes = tuple(mesh.shape[name] for name in ("groups", "tile", "head"))
    return jax.shard_map(
        product_plan if sizes == (2, 4, 4) else gather_plan,
        mesh=mesh,
        in_specs=placed,
        out_specs=P(("groups", "tile"), "head", None, None, None),
        check_vma=False,
    )
```

```python
import jax
import jax.numpy as jnp
from jax import lax
from jax.experimental import pallas as pl
from jax.experimental.pallas import tpu as pltpu
from jax.sharding import PartitionSpec as P

eps_norm = 1e-05


def shifted_2(shard, axis, by):
    count = lax.axis_size(axis)
    return lax.ppermute(shard, axis, [(i, (i + by) % count) for i in range(count)])


def swapped(shard, axis, bit):
    return lax.ppermute(shard, axis, [(i, i ^ bit) for i in range(lax.axis_size(axis))])


def add_columns(operand, portion):
    return jnp.dot(operand, portion, preferred_element_type=jnp.float32)


def routing(tile_map, tile_count, decode_owner, tile_slots, head_groups):
    most_tiles = tile_map.shape[1]
    owner_tile = decode_owner // head_groups
    owner_turn = decode_owner % head_groups
    usable = jnp.arange(most_tiles)[None, :] < tile_count[:, None]
    matched = (tile_map[:, :, None] == jnp.arange(tile_slots)[None, None, :]) & usable[:, :, None]
    return owner_tile, owner_turn, matched


def gather_plan(
    features, proj_weight, proj_bias, kv_weight, key_gain, tile_map, tile_count, decode_owner
):
    tile_slots, shard_len, feature_width = features.shape
    token_rows = tile_slots * shard_len
    feature_rows = features.reshape(token_rows, feature_width)
    weight_cols = lax.all_gather(proj_weight, "tile", axis=0, tiled=True)
    projected = jnp.dot(feature_rows, weight_cols, preferred_element_type=jnp.float32)
    projected_local = (projected + proj_bias.astype(jnp.float32)).astype(jnp.bfloat16)
    kv_width = kv_weight.shape[1]
    projected_all = lax.all_gather(projected_local, "head", axis=1, tiled=True)
    key_value = add_columns(projected_all, lax.all_gather(kv_weight, "tile", axis=0, tiled=True))
    layers, head_dim = key_gain.shape
    blocks = key_value.reshape(token_rows, -1, layers, 2, head_dim)
    keys_raw = blocks[:, :, :, 0]
    inv_rms = lax.rsqrt(jnp.mean(keys_raw * keys_raw, axis=-1, keepdims=True) + eps_norm)
    keys_normed = keys_raw * inv_rms * key_gain[None, None]
    stacked = jnp.stack([keys_normed, blocks[:, :, :, 1]], axis=3).astype(jnp.bfloat16)
    per_tile = stacked.reshape(tile_slots, shard_len * kv_width)
    tile_ranks = lax.axis_size("tile")
    head_groups = lax.axis_size("head")
    most_tiles = tile_map.shape[1]
    owner_tile, owner_turn, matched = routing(
        tile_map, tile_count, decode_owner, tile_slots, head_groups
    )
    owned_by = (owner_tile[:, None] == jnp.arange(tile_ranks)[None, :]).astype(jnp.float32)
    selector = jnp.einsum("rd,rjs->jds", owned_by, matched.astype(jnp.float32))
    selector = selector.astype(jnp.bfloat16).reshape(most_tiles * tile_ranks, tile_slots)
    outgoing = add_columns(selector, per_tile).astype(jnp.bfloat16)
    outgoing = outgoing.reshape(most_tiles, tile_ranks, shard_len, kv_width)
    arrived = lax.all_to_all(outgoing, "tile", split_axis=1, concat_axis=1, tiled=True)
    gathered_rows = arrived.reshape(
        most_tiles * tile_ranks * shard_len, kv_width // head_dim, head_dim
    )
    my_turn = jnp.sum(jnp.where(owner_tile == lax.axis_index("tile"), owner_turn, 0))
    stride = 1
    while stride < head_groups:
        shifted = shifted_2(gathered_rows, "head", stride)
        gathered_rows = jnp.where(my_turn // stride % 2 == 1, shifted, gathered_rows)
        stride = stride * 2
    return gathered_rows[None, None]


def terms_body(choice, weight, near, far, own, second, mirror, first, *kept_rest):
    near_product = add_columns(weight[...], near[...])
    far_product = add_columns(weight[...], far[...])
    near_kept = choice[0] == 1
    kept = jnp.where(near_kept, near_product, far_product)
    sent = jnp.where(near_kept, far_product, near_product)
    tall, width = weight.shape[0], own.shape[1]
    i = pl.program_id(0)
    rows = pl.ds(pl.multiple_of(i * tall, tall), tall)
    first[rows, :] = sent[:, :width].astype(first.dtype)

    def write_direct():
        own[rows, :] = kept[:, :width]
        second[rows, :] = sent[:, width:].astype(second.dtype)
        mirror[rows, :] = kept[:, width:].astype(mirror.dtype)

    if len(kept_rest) == 0:
        write_direct()
    else:
        pl.when(i < 2)(write_direct)

        @pl.when(i == 2)
        def _():
            kept_rest[0][...] = kept
            first[3 * tall :, :] = sent[:, width:].astype(first.dtype)


def term_shapes(depth, width, all_direct):
    direct, wide, narrow = depth if all_direct else depth // 3 * 2, jnp.float32, jnp.bfloat16
    shapes = [((direct, width), t) for t in (wide, narrow, narrow)]
    shapes = shapes + [((2 * depth - direct, width), narrow)]
    if not all_direct:
        shapes = shapes + [((depth // 3, 2 * width), wide)]
    return [jax.ShapeDtypeStruct(*shape) for shape in shapes]


def product_terms(choice, weight, near, far, all_direct):
    depth, rows = weight.shape
    columns = near.shape[1]
    tall = depth // 3
    shapes = term_shapes(depth, columns // 2, all_direct)
    whole = [pl.BlockSpec(array.shape, lambda i, choice: (0, 0)) for array in (near, *shapes)]
    return pl.pallas_call(
        terms_body,
        out_shape=shapes,
        grid_spec=pltpu.PrefetchScalarGridSpec(
            num_scalar_prefetch=1,
            grid=(3,),
            in_specs=[pl.BlockSpec((tall, rows), lambda i, choice: (i, 0)), whole[0], whole[0]],
            out_specs=whole[1:],
        ),
        compiler_params=pltpu.CompilerParams(vmem_limit_bytes=32 * 1024 * 1024),
        cost_estimate=pl.CostEstimate(
            flops=4 * depth * rows * columns,
            bytes_accessed=2 * depth * rows + 4 * rows * columns + 5 * depth * columns,
            transcendentals=0,
        ),
    )(choice, weight, near, far)


def blank_arrays(shapes):
    return pl.pallas_call(
        lambda *refs: None,
        out_shape=shapes,
        out_specs=[pl.BlockSpec(memory_space=pl.ANY)] * len(shapes),
    )()


def product_plan(
    features, proj_weight, proj_bias, kv_weight, key_gain, tile_map, tile_count, decode_owner
):
    tile_slots, shard_len, feature_width = features.shape
    token_rows = tile_slots * shard_len
    depth = proj_weight.shape[0]
    layers, head_dim = key_gain.shape
    width = layers * head_dim
    most_tiles = tile_map.shape[1]
    group, tile, head = (lax.axis_index(name) for name in ("groups", "tile", "head"))
    first_core, first_chip = tile % 2 == 0, tile < 2
    at_end = (head == 0) | (head == 3)
    feature_rows = features.reshape(token_rows, feature_width)
    step = lax.optimization_barrier

    def moved(shard, target):
        pairs = []
        for t in range(4):
            for h in range(4):
                to_tile, to_head = target(t, h)
                pairs.append((t * 4 + h, to_tile * 4 + to_head))
        return lax.ppermute(shard, ("tile", "head"), pairs)

    def outer_core(h):
        return (h ^ h // 2) % 2

    feature_parts = [
        lax.dynamic_slice_in_dim(feature_rows, (tile ^ r) * depth, depth, axis=1) for r in range(4)
    ]

    def put_first(condition, one, other, axis):
        return jnp.concatenate(
            [jnp.where(condition, one, other), jnp.where(condition, other, one)], axis=axis
        )

    def both_heads(ours, theirs):
        return put_first(group == 0, ours, theirs, 1)

    choice = (at_end == first_core).astype(jnp.int32).reshape(1)

    def products(near, far, all_direct):
        return tuple(product_terms(choice, proj_weight, near, far, all_direct))

    rest = depth // 3

    def to_neighbour(block):
        return swapped(block, "head", 1)

    def over_middle(block):
        return swapped(block, "head", 3)

    def plus(block, *arrived):
        for other in arrived:
            block = block + other.astype(jnp.float32)
        return block

    once = jnp.minimum(jnp.max(tile_count), 1)

    def in_loop(chain, given, empty):
        return lax.fori_loop(0, once, lambda _, carry: chain(carry[0]), (given, empty))[1]

    def times_features(rows, parts):
        return sum(add_columns(parts[r], rows[r]) for r in range(4))

    def finish(total, part):
        finished = []
        for k in range(2):
            entries = total[:, k * width : (k + 1) * width].reshape(token_rows, layers, head_dim)
            entries = entries + bias_part[k, :, part][None]
            if part == 0:
                squares = jnp.mean(entries * entries, axis=-1, keepdims=True)
                entries = entries * lax.rsqrt(squares + eps_norm) * key_gain[None]
            finished.append(entries.reshape(token_rows, width).astype(jnp.bfloat16))
        return jnp.concatenate(finished, axis=1).reshape(tile_slots, shard_len, 2 * width)

    owner_tile, owner_turn, matched = routing(tile_map, tile_count, decode_owner, tile_slots, 4)
    turn_of = jnp.sum(jnp.where(matched, owner_turn[:, None, None], 0), axis=(0, 1))
    owned_by = (owner_tile[:, None] == (tile ^ jnp.arange(4))[None, :]).astype(jnp.float32)
    selector = jnp.einsum("rd,rjs->djs", owned_by, matched.astype(jnp.float32))
    selector = selector.astype(jnp.bfloat16).reshape(4 * most_tiles, tile_slots)

    turned = [turn_of // stride % 2 == 1 for stride in (1, 2)]

    def rolled(rows, shifted, stride):
        return jnp.where(turned[stride - 1][:, None, None], shifted, rows)

    def outgoing(rows):
        picked = add_columns(selector, rows.reshape(tile_slots, -1)).astype(jnp.bfloat16)
        picked = picked.reshape(4, most_tiles, shard_len, 2, layers, head_dim)
        return [picked[r] for r in range(4)]

    def to_owners(picked):
        return [picked[0]] + [swapped(picked[r], "tile", r) for r in (1, 2, 3)]

    def in_order(arrived):
        even = [jnp.where(first_core, arrived[r], arrived[r ^ 1]) for r in range(4)]
        ranked = [jnp.where(first_chip, even[r], even[r ^ 2]) for r in range(4)]
        return jnp.stack(ranked, axis=1)

    column, half = group * 2 * head_dim, kv_weight.shape[0] // 2

    def halves(part):
        mine = lax.dynamic_slice_in_dim(kv_weight, column + part * head_dim, head_dim, axis=1)
        ours = lax.dynamic_slice_in_dim(mine, tile // 2 * half, half, axis=0)
        return ours, lax.dynamic_slice_in_dim(mine, half - tile // 2 * half, half, axis=0)

    def to_planes(stays, comes):
        pieces = []
        for j in range(2):
            piece = jnp.where(tile // 2 == (head // 2) ^ j, stays, comes)
            pieces.append(
                moved(piece, lambda t, h: (t // 2 * 2 + outer_core(h), t % 2 + 2 * ((h // 2) ^ j)))
            )
        return pieces

    key_stays, key_leaves = halves(0)
    bias_rows = moved(proj_bias, lambda t, h: (h, t))
    key_stays, key_comes, bias_rows = step((key_stays, swapped(key_leaves, "tile", 2), bias_rows))

    value_stays, value_leaves = halves(1)
    tokens = jax.ShapeDtypeStruct((tile_slots, shard_len, 2 * width), jnp.bfloat16)
    shapes = term_shapes(depth, width, True) + [tokens, tokens]
    *no_terms, no_keys, no_values = blank_arrays(shapes)
    bias_part = add_columns(bias_rows[None], kv_weight)
    key_pieces, value_stays, value_comes, bias_part, once = step(
        (
            to_planes(key_stays, key_comes),
            value_stays,
            swapped(value_leaves, "tile", 2),
            bias_part,
            once,
        )
    )

    key_half = jnp.concatenate(key_pieces, axis=1)
    value_pieces = to_planes(value_stays, value_comes)
    key_half, key_other, feature_parts = step(
        (key_half, swapped(key_half, "tile", 2), feature_parts)
    )

    key_near = step(put_first(first_chip, key_half, key_other, 0))
    terms = products(key_near, swapped(key_near, "tile", 1), False)
    bias_part = bias_part + swapped(bias_part, "tile", 1)
    terms, value_pieces, bias_part = step((terms, value_pieces, bias_part))
    value_half = jnp.concatenate(value_pieces, axis=1)

    def values_terms(given):
        value_half, bias_part = given
        other, bias_other = step((swapped(value_half, "tile", 2), swapped(bias_part, "tile", 2)))
        near = step(put_first(first_chip, value_half, other, 0))
        terms = products(near, swapped(near, "tile", 1), True)
        return (other, bias_other), (terms, bias_part + bias_other)

    empty = tuple(no_terms), bias_part
    own, second, mirror, first, kept_rest = terms
    second, mirror, first, (value_terms, bias_part) = step(
        (
            swapped(second, "head", 2),
            over_middle(mirror),
            to_neighbour(first),
            in_loop(values_terms, (value_half, bias_part), empty),
        )
    )
    bias_part = bias_part.reshape(2, layers, 2, head_dim)

    direct = 2 * rest
    arrived = jnp.concatenate([first[direct : 3 * rest], first[3 * rest :]], axis=1)
    pair = plus(kept_rest, arrived)
    pair = step(pair)
    mirrored = over_middle(pair[:, width:].astype(jnp.bfloat16))
    pair, mirrored, value_terms = step((pair, mirrored, value_terms))
    blocks = [plus(own, second, mirror, first[:direct]), plus(pair[:, :width], mirrored)]
    own = jnp.concatenate([block.astype(jnp.bfloat16) for block in blocks], axis=0)

    def rest_of_plane(given, part):
        own, across_x, across_y = given
        rows_0 = step(both_heads(own, across_y))
        middle = depth // 2
        upper, lower, rows_1 = step(
            (
                swapped(across_x[:middle], "groups", 1),
                swapped(across_y[middle:], "tile", 2),
                swapped(rows_0, "tile", 1),
            )
        )
        rows_2 = step(both_heads(across_x, jnp.concatenate([upper, lower], axis=0)))
        rows = [rows_0, rows_1, rows_2, swapped(rows_2, "tile", 1)]
        return finish(times_features(rows, feature_parts), part)

    def keys_product(own):
        across_x, across_y = step((swapped(own, "tile", 2), swapped(own, "groups", 1)))
        rows_0 = step(both_heads(own, across_y))
        diagonal, rows_1 = step((swapped(across_y, "tile", 2), swapped(rows_0, "tile", 1)))
        rows_2 = step(both_heads(across_x, diagonal))
        rows = [rows_0, rows_1, rows_2, swapped(rows_2, "tile", 1)]
        return across_x, finish(times_features(rows, feature_parts), 0)

    value_own, second, mirror, first = value_terms
    second, mirror, first, keys = step(
        (
            swapped(second, "head", 2),
            over_middle(mirror),
            to_neighbour(first),
            in_loop(keys_product, own, no_keys),
        )
    )
    own = plus(value_own, second, mirror, first).astype(jnp.bfloat16)

    shifted, across_x, across_y = step(
        (shifted_2(keys, "head", 1), swapped(own, "tile", 2), swapped(own, "groups", 1))
    )

    def values_product(given):
        own, across_x, across_y = given
        return (across_y, own, across_x), rest_of_plane(given, 1)

    keys = step(rolled(keys, shifted, 1))
    values = in_loop(values_product, (own, across_x, across_y), no_values)
    shifted, values = step((shifted_2(keys, "head", 2), values))

    picked = outgoing(rolled(keys, shifted, 2))
    shifted, picked = step((shifted_2(values, "head", 1), picked))

    values = step(rolled(values, shifted, 1))
    arrived, shifted = step((to_owners(picked), shifted_2(values, "head", 2)))

    value_cache = in_order(to_owners(outgoing(rolled(values, shifted, 2))))
    cache = jnp.stack([in_order(arrived), value_cache], axis=-2)
    return cache.reshape(1, 1, most_tiles * 4 * shard_len, 4 * layers, head_dim)


def solution(mesh):
    placed = (
        P("groups", "tile", None),
        P("tile", "head"),
        P("head"),
        P("tile", "head"),
        P(),
        P("groups", None),
        P("groups"),
        P("groups"),
    )
    sizes = tuple(mesh.shape[name] for name in ("groups", "tile", "head"))
    return jax.shard_map(
        product_plan if sizes == (2, 4, 4) else gather_plan,
        mesh=mesh,
        in_specs=placed,
        out_specs=P(("groups", "tile"), "head", None, None, None),
        check_vma=False,
    )
```

```python
import jax
import jax.numpy as jnp
from jax import lax
from jax.experimental import pallas as pl
from jax.experimental.pallas import tpu as pltpu
from jax.sharding import PartitionSpec as P

eps_norm = 1e-05


def shifted_2(shard, axis, by):
    count = lax.axis_size(axis)
    return lax.ppermute(shard, axis, [(i, (i + by) % count) for i in range(count)])


def swapped(shard, axis, bit):
    return lax.ppermute(shard, axis, [(i, i ^ bit) for i in range(lax.axis_size(axis))])


def add_columns(operand, portion):
    return jnp.dot(operand, portion, preferred_element_type=jnp.float32)


def routing(tile_map, tile_count, decode_owner, tile_slots, head_groups):
    most_tiles = tile_map.shape[1]
    owner_tile = decode_owner // head_groups
    owner_turn = decode_owner % head_groups
    usable = jnp.arange(most_tiles)[None, :] < tile_count[:, None]
    matched = (tile_map[:, :, None] == jnp.arange(tile_slots)[None, None, :]) & usable[:, :, None]
    return owner_tile, owner_turn, matched


def gather_plan(
    features, proj_weight, proj_bias, kv_weight, key_gain, tile_map, tile_count, decode_owner
):
    tile_slots, shard_len, feature_width = features.shape
    token_rows = tile_slots * shard_len
    feature_rows = features.reshape(token_rows, feature_width)
    weight_cols = lax.all_gather(proj_weight, "tile", axis=0, tiled=True)
    projected = jnp.dot(feature_rows, weight_cols, preferred_element_type=jnp.float32)
    projected_local = (projected + proj_bias.astype(jnp.float32)).astype(jnp.bfloat16)
    kv_width = kv_weight.shape[1]
    projected_all = lax.all_gather(projected_local, "head", axis=1, tiled=True)
    key_value = add_columns(projected_all, lax.all_gather(kv_weight, "tile", axis=0, tiled=True))
    layers, head_dim = key_gain.shape
    blocks = key_value.reshape(token_rows, -1, layers, 2, head_dim)
    keys_raw = blocks[:, :, :, 0]
    inv_rms = lax.rsqrt(jnp.mean(keys_raw * keys_raw, axis=-1, keepdims=True) + eps_norm)
    keys_normed = keys_raw * inv_rms * key_gain[None, None]
    stacked = jnp.stack([keys_normed, blocks[:, :, :, 1]], axis=3).astype(jnp.bfloat16)
    per_tile = stacked.reshape(tile_slots, shard_len * kv_width)
    tile_ranks = lax.axis_size("tile")
    head_groups = lax.axis_size("head")
    most_tiles = tile_map.shape[1]
    owner_tile, owner_turn, matched = routing(
        tile_map, tile_count, decode_owner, tile_slots, head_groups
    )
    owned_by = (owner_tile[:, None] == jnp.arange(tile_ranks)[None, :]).astype(jnp.float32)
    selector = jnp.einsum("rd,rjs->jds", owned_by, matched.astype(jnp.float32))
    selector = selector.astype(jnp.bfloat16).reshape(most_tiles * tile_ranks, tile_slots)
    outgoing = add_columns(selector, per_tile).astype(jnp.bfloat16)
    outgoing = outgoing.reshape(most_tiles, tile_ranks, shard_len, kv_width)
    arrived = lax.all_to_all(outgoing, "tile", split_axis=1, concat_axis=1, tiled=True)
    gathered_rows = arrived.reshape(
        most_tiles * tile_ranks * shard_len, kv_width // head_dim, head_dim
    )
    my_turn = jnp.sum(jnp.where(owner_tile == lax.axis_index("tile"), owner_turn, 0))
    stride = 1
    while stride < head_groups:
        shifted = shifted_2(gathered_rows, "head", stride)
        gathered_rows = jnp.where(my_turn // stride % 2 == 1, shifted, gathered_rows)
        stride = stride * 2
    return gathered_rows[None, None]


def terms_body(choice, weight, near, far, own, second, mirror, first, *kept_rest):
    near_product = add_columns(weight[...], near[...])
    far_product = add_columns(weight[...], far[...])
    near_kept = choice[0] == 1
    kept = jnp.where(near_kept, near_product, far_product)
    sent = jnp.where(near_kept, far_product, near_product)
    tall, width = weight.shape[0], own.shape[1]
    i = pl.program_id(0)
    rows = pl.ds(pl.multiple_of(i * tall, tall), tall)
    first[rows, :] = sent[:, :width].astype(first.dtype)

    def write_direct():
        own[rows, :] = kept[:, :width]
        second[rows, :] = sent[:, width:].astype(second.dtype)
        mirror[rows, :] = kept[:, width:].astype(mirror.dtype)

    if len(kept_rest) == 0:
        write_direct()
    else:
        pl.when(i < 2)(write_direct)

        @pl.when(i == 2)
        def _():
            kept_rest[0][...] = kept
            first[3 * tall :, :] = sent[:, width:].astype(first.dtype)


def term_shapes(depth, width, all_direct):
    direct, wide, narrow = depth if all_direct else depth // 3 * 2, jnp.float32, jnp.bfloat16
    shapes = [((direct, width), t) for t in (wide, narrow, narrow)]
    shapes = shapes + [((2 * depth - direct, width), narrow)]
    if not all_direct:
        shapes = shapes + [((depth // 3, 2 * width), wide)]
    return [jax.ShapeDtypeStruct(*shape) for shape in shapes]


def product_terms(choice, weight, near, far, all_direct):
    depth, rows = weight.shape
    columns = near.shape[1]
    tall = depth // 3
    shapes = term_shapes(depth, columns // 2, all_direct)
    whole = [pl.BlockSpec(array.shape, lambda i, choice: (0, 0)) for array in (near, *shapes)]
    return pl.pallas_call(
        terms_body,
        out_shape=shapes,
        grid_spec=pltpu.PrefetchScalarGridSpec(
            num_scalar_prefetch=1,
            grid=(3,),
            in_specs=[pl.BlockSpec((tall, rows), lambda i, choice: (i, 0)), whole[0], whole[0]],
            out_specs=whole[1:],
        ),
        compiler_params=pltpu.CompilerParams(vmem_limit_bytes=32 * 1024 * 1024),
        cost_estimate=pl.CostEstimate(
            flops=4 * depth * rows * columns,
            bytes_accessed=2 * depth * rows + 4 * rows * columns + 5 * depth * columns,
            transcendentals=0,
        ),
    )(choice, weight, near, far)


def blank_arrays(shapes):
    return pl.pallas_call(
        lambda *refs: None,
        out_shape=shapes,
        out_specs=[pl.BlockSpec(memory_space=pl.ANY)] * len(shapes),
    )()


def pick_body(places, odd, rows, shifted, *pieces):
    for d, piece in enumerate(pieces):
        for j in range(piece.shape[0]):
            place = places[d * piece.shape[0] + j]
            found = place >= 0
            place = jnp.maximum(place, 0)
            moves = odd[place] == 1

            @pl.when(jnp.logical_not(found))
            def _():
                piece[j] = jnp.zeros(piece.shape[1:], piece.dtype)

            @pl.when(jnp.logical_and(found, moves))
            def _():
                piece[j] = shifted[place]

            @pl.when(jnp.logical_and(found, jnp.logical_not(moves)))
            def _():
                piece[j] = rows[place]


def picked_tiles(places, odd, rows, shifted):
    scalars, vmem = pl.BlockSpec(memory_space=pltpu.SMEM), pl.BlockSpec(memory_space=pltpu.VMEM)
    owners, most_tiles = places.shape
    shape = jax.ShapeDtypeStruct((most_tiles, *rows.shape[1:]), rows.dtype)
    return pl.pallas_call(
        pick_body,
        out_shape=[shape] * owners,
        in_specs=[scalars, scalars, vmem, vmem],
        out_specs=[vmem] * owners,
    )(places.reshape(-1), odd, rows, shifted)


def cache_body(tile, *refs):
    *pieces, out = refs
    width = out.shape[4]
    for mine in range(4):

        @pl.when(tile[0] == mine)
        def _():
            for source in range(4):
                keys = pieces[mine ^ source][0].astype(jnp.float32)
                values = pieces[4 + (mine ^ source)][0].astype(jnp.float32)
                rows = [keys[:, :width], values[:, :width], keys[:, width:], values[:, width:]]
                out[0, source] = jnp.stack(rows, axis=1).astype(out.dtype)


def cache_rows(tile, keys, values):
    most_tiles, shard_len, columns = keys[0].shape
    piece = pl.BlockSpec((1, shard_len, columns), lambda j: (j, 0, 0))
    shape = (most_tiles, 4, shard_len, 4, columns // 2)
    return pl.pallas_call(
        cache_body,
        out_shape=jax.ShapeDtypeStruct(shape, jnp.bfloat16),
        grid=(most_tiles,),
        in_specs=[pl.BlockSpec(memory_space=pltpu.SMEM)] + [piece] * 8,
        out_specs=pl.BlockSpec((1, *shape[1:]), lambda j: (j, 0, 0, 0, 0)),
        cost_estimate=pl.CostEstimate(
            flops=0, bytes_accessed=32 * most_tiles * shard_len * columns, transcendentals=0
        ),
    )(tile, *keys, *values)


def product_plan(
    features, proj_weight, proj_bias, kv_weight, key_gain, tile_map, tile_count, decode_owner
):
    tile_slots, shard_len, feature_width = features.shape
    token_rows = tile_slots * shard_len
    depth = proj_weight.shape[0]
    layers, head_dim = key_gain.shape
    width = layers * head_dim
    most_tiles = tile_map.shape[1]
    group, tile, head = (lax.axis_index(name) for name in ("groups", "tile", "head"))
    first_core, first_chip = tile % 2 == 0, tile < 2
    at_end = (head == 0) | (head == 3)
    feature_rows = features.reshape(token_rows, feature_width)
    step = lax.optimization_barrier

    def moved(shard, target):
        pairs = []
        for t in range(4):
            for h in range(4):
                to_tile, to_head = target(t, h)
                pairs.append((t * 4 + h, to_tile * 4 + to_head))
        return lax.ppermute(shard, ("tile", "head"), pairs)

    def outer_core(h):
        return (h ^ h // 2) % 2

    feature_parts = [
        lax.dynamic_slice_in_dim(feature_rows, (tile ^ r) * depth, depth, axis=1) for r in range(4)
    ]

    def put_first(condition, one, other, axis):
        return jnp.concatenate(
            [jnp.where(condition, one, other), jnp.where(condition, other, one)], axis=axis
        )

    def both_heads(ours, theirs):
        return put_first(group == 0, ours, theirs, 1)

    choice = (at_end == first_core).astype(jnp.int32).reshape(1)

    def products(near, far, all_direct):
        return tuple(product_terms(choice, proj_weight, near, far, all_direct))

    rest = depth // 3

    def to_neighbour(block):
        return swapped(block, "head", 1)

    def over_middle(block):
        return swapped(block, "head", 3)

    def plus(block, *arrived):
        for other in arrived:
            block = block + other.astype(jnp.float32)
        return block

    once = jnp.minimum(jnp.max(tile_count), 1)

    def in_loop(chain, given, empty):
        return lax.fori_loop(0, once, lambda _, carry: chain(carry[0]), (given, empty))[1]

    def times_features(rows, parts):
        return sum(add_columns(parts[r], rows[r]) for r in range(4))

    def finish(total, part):
        finished = []
        for k in range(2):
            entries = total[:, k * width : (k + 1) * width].reshape(token_rows, layers, head_dim)
            entries = entries + bias_part[k, :, part][None]
            if part == 0:
                squares = jnp.mean(entries * entries, axis=-1, keepdims=True)
                entries = entries * lax.rsqrt(squares + eps_norm) * key_gain[None]
            finished.append(entries.reshape(token_rows, width).astype(jnp.bfloat16))
        return jnp.concatenate(finished, axis=1).reshape(tile_slots, shard_len, 2 * width)

    owner_tile, owner_turn, matched = routing(tile_map, tile_count, decode_owner, tile_slots, 4)
    turn_of = jnp.sum(jnp.where(matched, owner_turn[:, None, None], 0), axis=(0, 1))
    usable = jnp.arange(most_tiles)[None, :] < tile_count[:, None]
    owned_by = owner_tile[:, None] == (tile ^ jnp.arange(4))[None, :]
    places = jnp.where(usable[:, None] & owned_by[:, :, None], tile_map[:, None], -1)
    places = jnp.max(places, axis=0).astype(jnp.int32)
    turned = [turn_of // stride % 2 == 1 for stride in (1, 2)]

    def rolled(rows, shifted, stride):
        return jnp.where(turned[stride - 1][:, None, None], shifted, rows)

    def outgoing(rows, shifted):
        return picked_tiles(places, turned[1].astype(jnp.int32), rows, shifted)

    def to_owners(picked):
        return [picked[0]] + [swapped(picked[r], "tile", r) for r in (1, 2, 3)]

    column, half = group * 2 * head_dim, kv_weight.shape[0] // 2

    def halves(part):
        mine = lax.dynamic_slice_in_dim(kv_weight, column + part * head_dim, head_dim, axis=1)
        ours = lax.dynamic_slice_in_dim(mine, tile // 2 * half, half, axis=0)
        return ours, lax.dynamic_slice_in_dim(mine, half - tile // 2 * half, half, axis=0)

    def to_planes(stays, comes):
        pieces = []
        for j in range(2):
            piece = jnp.where(tile // 2 == (head // 2) ^ j, stays, comes)
            pieces.append(
                moved(piece, lambda t, h: (t // 2 * 2 + outer_core(h), t % 2 + 2 * ((h // 2) ^ j)))
            )
        return pieces

    key_stays, key_leaves = halves(0)
    bias_rows = moved(proj_bias, lambda t, h: (h, t))
    key_stays, key_comes, bias_rows = step((key_stays, swapped(key_leaves, "tile", 2), bias_rows))

    value_stays, value_leaves = halves(1)
    tokens = jax.ShapeDtypeStruct((tile_slots, shard_len, 2 * width), jnp.bfloat16)
    shapes = term_shapes(depth, width, True) + [tokens, tokens]
    *no_terms, no_keys, no_values = blank_arrays(shapes)
    bias_part = add_columns(bias_rows[None], kv_weight)
    key_pieces, value_stays, value_comes, bias_part, once = step(
        (
            to_planes(key_stays, key_comes),
            value_stays,
            swapped(value_leaves, "tile", 2),
            bias_part,
            once,
        )
    )

    key_half = jnp.concatenate(key_pieces, axis=1)
    value_pieces = to_planes(value_stays, value_comes)
    key_half, key_other, feature_parts = step(
        (key_half, swapped(key_half, "tile", 2), feature_parts)
    )

    key_near = step(put_first(first_chip, key_half, key_other, 0))
    terms = products(key_near, swapped(key_near, "tile", 1), False)
    bias_part = bias_part + swapped(bias_part, "tile", 1)
    terms, bias_part = step((terms, bias_part))
    value_pieces, bias_part = step((value_pieces, bias_part))
    value_half = jnp.concatenate(value_pieces, axis=1)

    def values_terms(given):
        value_half, bias_part = given
        other, bias_other = step((swapped(value_half, "tile", 2), swapped(bias_part, "tile", 2)))
        near = step(put_first(first_chip, value_half, other, 0))
        terms = products(near, swapped(near, "tile", 1), True)
        return (other, bias_other), (terms, bias_part + bias_other)

    empty = tuple(no_terms), bias_part
    own, second, mirror, first, kept_rest = terms
    second, mirror, first, (value_terms, bias_part) = step(
        (
            swapped(second, "head", 2),
            over_middle(mirror),
            to_neighbour(first),
            in_loop(values_terms, (value_half, bias_part), empty),
        )
    )
    bias_part = bias_part.reshape(2, layers, 2, head_dim)

    direct = 2 * rest
    arrived = jnp.concatenate([first[direct : 3 * rest], first[3 * rest :]], axis=1)
    pair = plus(kept_rest, arrived)
    pair = step(pair)
    mirrored = over_middle(pair[:, width:].astype(jnp.bfloat16))
    pair, mirrored, value_terms = step((pair, mirrored, value_terms))
    blocks = [plus(own, second, mirror, first[:direct]), plus(pair[:, :width], mirrored)]
    own = jnp.concatenate([block.astype(jnp.bfloat16) for block in blocks], axis=0)

    def keys_product(own):
        across_x, across_y = step((swapped(own, "tile", 2), swapped(own, "groups", 1)))
        rows_0 = step(both_heads(own, across_y))
        diagonal, rows_1 = step((swapped(across_y, "tile", 2), swapped(rows_0, "tile", 1)))
        rows_2 = step(both_heads(across_x, diagonal))
        rows = [rows_0, rows_1, rows_2, swapped(rows_2, "tile", 1)]
        return across_x, finish(times_features(rows, feature_parts), 0)

    value_own, second, mirror, first = value_terms
    second, mirror, first, keys = step(
        (
            swapped(second, "head", 2),
            over_middle(mirror),
            to_neighbour(first),
            in_loop(keys_product, own, no_keys),
        )
    )
    own = plus(value_own, second, mirror, first).astype(jnp.bfloat16)

    shifted, across_x, across_y = step(
        (shifted_2(keys, "head", 1), swapped(own, "tile", 2), swapped(own, "groups", 1))
    )

    def values_product(given):
        own, across_x, across_y = given
        rows_0 = step(both_heads(own, across_y))
        middle = depth // 2
        upper, lower, rows_1, total = step(
            (
                swapped(across_x[:middle], "groups", 1),
                swapped(across_y[middle:], "tile", 2),
                swapped(rows_0, "tile", 1),
                add_columns(feature_parts[0], rows_0),
            )
        )
        rows_2 = step(both_heads(across_x, jnp.concatenate([upper, lower], axis=0)))
        rows = [None, rows_1, rows_2, swapped(rows_2, "tile", 1)]
        for r in (1, 2, 3):
            total = total + add_columns(feature_parts[r], rows[r])
        return (across_y, own, across_x), finish(total, 1)

    keys = step(rolled(keys, shifted, 1))
    values = in_loop(values_product, (own, across_x, across_y), no_values)
    shifted, values = step((shifted_2(keys, "head", 2), values))

    picked = outgoing(keys, shifted)
    shifted, picked = step((shifted_2(values, "head", 1), picked))

    values = step(rolled(values, shifted, 1))
    arrived, shifted = step((to_owners(picked), shifted_2(values, "head", 2)))

    value_pieces = to_owners(outgoing(values, shifted))
    cache = cache_rows(tile.reshape(1), arrived, value_pieces)
    return cache.reshape(1, 1, most_tiles * 4 * shard_len, 4 * layers, head_dim)


def solution(mesh):
    placed = (
        P("groups", "tile", None),
        P("tile", "head"),
        P("head"),
        P("tile", "head"),
        P(),
        P("groups", None),
        P("groups"),
        P("groups"),
    )
    sizes = tuple(mesh.shape[name] for name in ("groups", "tile", "head"))
    return jax.shard_map(
        product_plan if sizes == (2, 4, 4) else gather_plan,
        mesh=mesh,
        in_specs=placed,
        out_specs=P(("groups", "tile"), "head", None, None, None),
        check_vma=False,
    )
```

```python
import jax
import jax.numpy as jnp
from jax import lax
from jax.experimental import pallas as pl
from jax.experimental.pallas import tpu as pltpu
from jax.sharding import PartitionSpec as P

eps_norm = 1e-05


def shifted_2(shard, axis, by):
    count = lax.axis_size(axis)
    return lax.ppermute(shard, axis, [(i, (i + by) % count) for i in range(count)])


def swapped(shard, axis, bit):
    return lax.ppermute(shard, axis, [(i, i ^ bit) for i in range(lax.axis_size(axis))])


def add_columns(operand, portion):
    return jnp.dot(operand, portion, preferred_element_type=jnp.float32)


def routing(tile_map, tile_count, decode_owner, tile_slots, head_groups):
    most_tiles = tile_map.shape[1]
    owner_tile = decode_owner // head_groups
    owner_turn = decode_owner % head_groups
    usable = jnp.arange(most_tiles)[None, :] < tile_count[:, None]
    matched = (tile_map[:, :, None] == jnp.arange(tile_slots)[None, None, :]) & usable[:, :, None]
    return owner_tile, owner_turn, matched


def gather_plan(
    features, proj_weight, proj_bias, kv_weight, key_gain, tile_map, tile_count, decode_owner
):
    tile_slots, shard_len, feature_width = features.shape
    token_rows = tile_slots * shard_len
    feature_rows = features.reshape(token_rows, feature_width)
    weight_cols = lax.all_gather(proj_weight, "tile", axis=0, tiled=True)
    projected = jnp.dot(feature_rows, weight_cols, preferred_element_type=jnp.float32)
    projected_local = (projected + proj_bias.astype(jnp.float32)).astype(jnp.bfloat16)
    kv_width = kv_weight.shape[1]
    projected_all = lax.all_gather(projected_local, "head", axis=1, tiled=True)
    key_value = add_columns(projected_all, lax.all_gather(kv_weight, "tile", axis=0, tiled=True))
    layers, head_dim = key_gain.shape
    blocks = key_value.reshape(token_rows, -1, layers, 2, head_dim)
    keys_raw = blocks[:, :, :, 0]
    inv_rms = lax.rsqrt(jnp.mean(keys_raw * keys_raw, axis=-1, keepdims=True) + eps_norm)
    keys_normed = keys_raw * inv_rms * key_gain[None, None]
    stacked = jnp.stack([keys_normed, blocks[:, :, :, 1]], axis=3).astype(jnp.bfloat16)
    per_tile = stacked.reshape(tile_slots, shard_len * kv_width)
    tile_ranks = lax.axis_size("tile")
    head_groups = lax.axis_size("head")
    most_tiles = tile_map.shape[1]
    owner_tile, owner_turn, matched = routing(
        tile_map, tile_count, decode_owner, tile_slots, head_groups
    )
    owned_by = (owner_tile[:, None] == jnp.arange(tile_ranks)[None, :]).astype(jnp.float32)
    selector = jnp.einsum("rd,rjs->jds", owned_by, matched.astype(jnp.float32))
    selector = selector.astype(jnp.bfloat16).reshape(most_tiles * tile_ranks, tile_slots)
    outgoing = add_columns(selector, per_tile).astype(jnp.bfloat16)
    outgoing = outgoing.reshape(most_tiles, tile_ranks, shard_len, kv_width)
    arrived = lax.all_to_all(outgoing, "tile", split_axis=1, concat_axis=1, tiled=True)
    gathered_rows = arrived.reshape(
        most_tiles * tile_ranks * shard_len, kv_width // head_dim, head_dim
    )
    my_turn = jnp.sum(jnp.where(owner_tile == lax.axis_index("tile"), owner_turn, 0))
    stride = 1
    while stride < head_groups:
        shifted = shifted_2(gathered_rows, "head", stride)
        gathered_rows = jnp.where(my_turn // stride % 2 == 1, shifted, gathered_rows)
        stride = stride * 2
    return gathered_rows[None, None]


def terms_body(choice, weight, near, far, own, second, mirror, first, *kept_rest):
    near_product = add_columns(weight[...], near[...])
    far_product = add_columns(weight[...], far[...])
    near_kept = choice[0] == 1
    kept = jnp.where(near_kept, near_product, far_product)
    sent = jnp.where(near_kept, far_product, near_product)
    tall, width = weight.shape[0], own.shape[1]
    i = pl.program_id(0)
    rows = pl.ds(pl.multiple_of(i * tall, tall), tall)
    first[rows, :] = sent[:, :width].astype(first.dtype)

    def write_direct():
        own[rows, :] = kept[:, :width]
        second[rows, :] = sent[:, width:].astype(second.dtype)
        mirror[rows, :] = kept[:, width:].astype(mirror.dtype)

    if len(kept_rest) == 0:
        write_direct()
    else:
        pl.when(i < 2)(write_direct)

        @pl.when(i == 2)
        def _():
            kept_rest[0][...] = kept
            first[3 * tall :, :] = sent[:, width:].astype(first.dtype)


def term_shapes(depth, width, all_direct):
    direct, wide, narrow = depth if all_direct else depth // 3 * 2, jnp.float32, jnp.bfloat16
    shapes = [((direct, width), t) for t in (wide, narrow, narrow)]
    shapes = shapes + [((2 * depth - direct, width), narrow)]
    if not all_direct:
        shapes = shapes + [((depth // 3, 2 * width), wide)]
    return [jax.ShapeDtypeStruct(*shape) for shape in shapes]


def product_terms(choice, weight, near, far, all_direct):
    depth, rows = weight.shape
    columns = near.shape[1]
    tall = depth // 3
    shapes = term_shapes(depth, columns // 2, all_direct)
    whole = [pl.BlockSpec(array.shape, lambda i, choice: (0, 0)) for array in (near, *shapes)]
    return pl.pallas_call(
        terms_body,
        out_shape=shapes,
        grid_spec=pltpu.PrefetchScalarGridSpec(
            num_scalar_prefetch=1,
            grid=(3,),
            in_specs=[pl.BlockSpec((tall, rows), lambda i, choice: (i, 0)), whole[0], whole[0]],
            out_specs=whole[1:],
        ),
        compiler_params=pltpu.CompilerParams(vmem_limit_bytes=32 * 1024 * 1024),
        cost_estimate=pl.CostEstimate(
            flops=4 * depth * rows * columns,
            bytes_accessed=2 * depth * rows + 4 * rows * columns + 5 * depth * columns,
            transcendentals=0,
        ),
    )(choice, weight, near, far)


def blank_arrays(shapes):
    return pl.pallas_call(
        lambda *refs: None,
        out_shape=shapes,
        out_specs=[pl.BlockSpec(memory_space=pl.ANY)] * len(shapes),
    )()


def product_plan(
    features, proj_weight, proj_bias, kv_weight, key_gain, tile_map, tile_count, decode_owner
):
    tile_slots, shard_len, feature_width = features.shape
    token_rows = tile_slots * shard_len
    depth = proj_weight.shape[0]
    layers, head_dim = key_gain.shape
    width = layers * head_dim
    most_tiles = tile_map.shape[1]
    group, tile, head = (lax.axis_index(name) for name in ("groups", "tile", "head"))
    first_core, first_chip = tile % 2 == 0, tile < 2
    at_end = (head == 0) | (head == 3)
    feature_rows = features.reshape(token_rows, feature_width)
    step = lax.optimization_barrier

    def moved(shard, target):
        pairs = []
        for t in range(4):
            for h in range(4):
                to_tile, to_head = target(t, h)
                pairs.append((t * 4 + h, to_tile * 4 + to_head))
        return lax.ppermute(shard, ("tile", "head"), pairs)

    def outer_core(h):
        return (h ^ h // 2) % 2

    feature_parts = [
        lax.dynamic_slice_in_dim(feature_rows, (tile ^ r) * depth, depth, axis=1) for r in range(4)
    ]

    def put_first(condition, one, other, axis):
        return jnp.concatenate(
            [jnp.where(condition, one, other), jnp.where(condition, other, one)], axis=axis
        )

    def both_heads(ours, theirs):
        return put_first(group == 0, ours, theirs, 1)

    choice = (at_end == first_core).astype(jnp.int32).reshape(1)

    def products(near, far, all_direct):
        return tuple(product_terms(choice, proj_weight, near, far, all_direct))

    rest = depth // 3

    def to_neighbour(block):
        return swapped(block, "head", 1)

    def over_middle(block):
        return swapped(block, "head", 3)

    def plus(block, *arrived):
        for other in arrived:
            block = block + other.astype(jnp.float32)
        return block

    once = jnp.minimum(jnp.max(tile_count), 1)

    def in_loop(chain, given, empty):
        return lax.fori_loop(0, once, lambda _, carry: chain(carry[0]), (given, empty))[1]

    def times_features(rows, parts):
        return sum(add_columns(parts[r], rows[r]) for r in range(4))

    def finish(total, part):
        finished = []
        for k in range(2):
            entries = total[:, k * width : (k + 1) * width].reshape(token_rows, layers, head_dim)
            entries = entries + bias_part[k, :, part][None]
            if part == 0:
                squares = jnp.mean(entries * entries, axis=-1, keepdims=True)
                entries = entries * lax.rsqrt(squares + eps_norm) * key_gain[None]
            finished.append(entries.reshape(token_rows, width).astype(jnp.bfloat16))
        return jnp.concatenate(finished, axis=1).reshape(tile_slots, shard_len, 2 * width)

    owner_tile, owner_turn, matched = routing(tile_map, tile_count, decode_owner, tile_slots, 4)
    turn_of = jnp.sum(jnp.where(matched, owner_turn[:, None, None], 0), axis=(0, 1))
    owned_by = (owner_tile[:, None] == (tile ^ jnp.arange(4))[None, :]).astype(jnp.float32)
    selector = jnp.einsum("rd,rjs->djs", owned_by, matched.astype(jnp.float32))
    selector = selector.astype(jnp.bfloat16).reshape(4 * most_tiles, tile_slots)

    turned = [turn_of // stride % 2 == 1 for stride in (1, 2)]

    def rolled(rows, shifted, stride):
        return jnp.where(turned[stride - 1][:, None, None], shifted, rows)

    def outgoing(rows):
        picked = add_columns(selector, rows.reshape(tile_slots, -1)).astype(jnp.bfloat16)
        picked = picked.reshape(4, most_tiles, shard_len, 2, layers, head_dim)
        return [picked[r] for r in range(4)]

    def to_owners(picked):
        return [picked[0]] + [swapped(picked[r], "tile", r) for r in (1, 2, 3)]

    def in_order(arrived):
        even = [jnp.where(first_core, arrived[r], arrived[r ^ 1]) for r in range(4)]
        ranked = [jnp.where(first_chip, even[r], even[r ^ 2]) for r in range(4)]
        return jnp.stack(ranked, axis=1)

    column, half = group * 2 * head_dim, kv_weight.shape[0] // 2

    def halves(part):
        mine = lax.dynamic_slice_in_dim(kv_weight, column + part * head_dim, head_dim, axis=1)
        ours = lax.dynamic_slice_in_dim(mine, tile // 2 * half, half, axis=0)
        return ours, lax.dynamic_slice_in_dim(mine, half - tile // 2 * half, half, axis=0)

    def to_planes(stays, comes):
        pieces = []
        for j in range(2):
            piece = jnp.where(tile // 2 == (head // 2) ^ j, stays, comes)
            pieces.append(
                moved(piece, lambda t, h: (t // 2 * 2 + outer_core(h), t % 2 + 2 * ((h // 2) ^ j)))
            )
        return pieces

    key_stays, key_leaves = halves(0)
    bias_rows = moved(proj_bias, lambda t, h: (h, t))
    key_stays, key_comes, bias_rows = step((key_stays, swapped(key_leaves, "tile", 2), bias_rows))

    value_stays, value_leaves = halves(1)
    tokens = jax.ShapeDtypeStruct((tile_slots, shard_len, 2 * width), jnp.bfloat16)
    shapes = term_shapes(depth, width, True) + [tokens, tokens]
    *no_terms, no_keys, no_values = blank_arrays(shapes)
    bias_part = add_columns(bias_rows[None], kv_weight)
    key_pieces, value_stays, value_comes, bias_part, once = step(
        (
            to_planes(key_stays, key_comes),
            value_stays,
            swapped(value_leaves, "tile", 2),
            bias_part,
            once,
        )
    )

    key_half = jnp.concatenate(key_pieces, axis=1)
    value_pieces = to_planes(value_stays, value_comes)
    key_half, key_other, feature_parts = step(
        (key_half, swapped(key_half, "tile", 2), feature_parts)
    )

    key_near = step(put_first(first_chip, key_half, key_other, 0))
    terms = products(key_near, swapped(key_near, "tile", 1), False)
    bias_part = bias_part + swapped(bias_part, "tile", 1)
    terms, value_pieces, bias_part = step((terms, value_pieces, bias_part))
    value_half = jnp.concatenate(value_pieces, axis=1)

    def values_terms(given):
        value_half, bias_part = given
        other, bias_other = step((swapped(value_half, "tile", 2), swapped(bias_part, "tile", 2)))
        near = step(put_first(first_chip, value_half, other, 0))
        terms = products(near, swapped(near, "tile", 1), True)
        return (other, bias_other), (terms, bias_part + bias_other)

    empty = tuple(no_terms), bias_part
    own, second, mirror, first, kept_rest = terms
    second, mirror, first, (value_terms, bias_part) = step(
        (
            swapped(second, "head", 2),
            over_middle(mirror),
            to_neighbour(first),
            in_loop(values_terms, (value_half, bias_part), empty),
        )
    )
    bias_part = bias_part.reshape(2, layers, 2, head_dim)

    direct = 2 * rest
    arrived = jnp.concatenate([first[direct : 3 * rest], first[3 * rest :]], axis=1)
    pair = plus(kept_rest, arrived)
    pair = step(pair)
    mirrored = over_middle(pair[:, width:].astype(jnp.bfloat16))
    pair, mirrored = step((pair, mirrored))
    blocks = [plus(own, second, mirror, first[:direct]), plus(pair[:, :width], mirrored)]
    own = jnp.concatenate([block.astype(jnp.bfloat16) for block in blocks], axis=0)

    def rest_of_plane(given, part):
        own, across_x, across_y = given
        rows_0 = step(both_heads(own, across_y))
        middle = depth // 2
        upper, lower, rows_1 = step(
            (
                swapped(across_x[:middle], "groups", 1),
                swapped(across_y[middle:], "tile", 2),
                swapped(rows_0, "tile", 1),
            )
        )
        rows_2 = step(both_heads(across_x, jnp.concatenate([upper, lower], axis=0)))
        rows = [rows_0, rows_1, rows_2, swapped(rows_2, "tile", 1)]
        return finish(times_features(rows, feature_parts), part)

    def keys_product(own):
        across_x, across_y = step((swapped(own, "tile", 2), swapped(own, "groups", 1)))
        rows_0 = step(both_heads(own, across_y))
        diagonal, rows_1 = step((swapped(across_y, "tile", 2), swapped(rows_0, "tile", 1)))
        rows_2 = step(both_heads(across_x, diagonal))
        rows = [rows_0, rows_1, rows_2, swapped(rows_2, "tile", 1)]
        return across_x, finish(times_features(rows, feature_parts), 0)

    value_own, second, mirror, first = value_terms
    second, mirror, first, keys = step(
        (
            swapped(second, "head", 2),
            over_middle(mirror),
            to_neighbour(first),
            in_loop(keys_product, own, no_keys),
        )
    )
    own = plus(value_own, second, mirror, first).astype(jnp.bfloat16)

    shifted, across_x, across_y = step(
        (shifted_2(keys, "head", 1), swapped(own, "tile", 2), swapped(own, "groups", 1))
    )

    def values_product(given):
        own, across_x, across_y = given
        return (across_y, own, across_x), rest_of_plane(given, 1)

    keys = step(rolled(keys, shifted, 1))
    values = in_loop(values_product, (own, across_x, across_y), no_values)
    shifted, values = step((shifted_2(keys, "head", 2), values))

    picked = outgoing(rolled(keys, shifted, 2))
    shifted, picked = step((shifted_2(values, "head", 1), picked))

    values = step(rolled(values, shifted, 1))
    arrived, shifted = step((to_owners(picked), shifted_2(values, "head", 2)))

    value_cache = in_order(to_owners(outgoing(rolled(values, shifted, 2))))
    cache = jnp.stack([in_order(arrived), value_cache], axis=-2)
    return cache.reshape(1, 1, most_tiles * 4 * shard_len, 4 * layers, head_dim)


def solution(mesh):
    placed = (
        P("groups", "tile", None),
        P("tile", "head"),
        P("head"),
        P("tile", "head"),
        P(),
        P("groups", None),
        P("groups"),
        P("groups"),
    )
    sizes = tuple(mesh.shape[name] for name in ("groups", "tile", "head"))
    return jax.shard_map(
        product_plan if sizes == (2, 4, 4) else gather_plan,
        mesh=mesh,
        in_specs=placed,
        out_specs=P(("groups", "tile"), "head", None, None, None),
        check_vma=False,
    )
```

```python
import jax
import jax.numpy as jnp
from jax import lax
from jax.experimental import pallas as pl
from jax.experimental.pallas import tpu as pltpu
from jax.sharding import PartitionSpec as P

eps_norm = 1e-05


def shifted_2(shard, axis, by):
    count = lax.axis_size(axis)
    return lax.ppermute(shard, axis, [(i, (i + by) % count) for i in range(count)])


def swapped(shard, axis, bit):
    return lax.ppermute(shard, axis, [(i, i ^ bit) for i in range(lax.axis_size(axis))])


def add_columns(operand, portion):
    return jnp.dot(operand, portion, preferred_element_type=jnp.float32)


def routing(tile_map, tile_count, decode_owner, tile_slots, head_groups):
    most_tiles = tile_map.shape[1]
    owner_tile = decode_owner // head_groups
    owner_turn = decode_owner % head_groups
    usable = jnp.arange(most_tiles)[None, :] < tile_count[:, None]
    matched = (tile_map[:, :, None] == jnp.arange(tile_slots)[None, None, :]) & usable[:, :, None]
    return owner_tile, owner_turn, matched


def gather_plan(
    features, proj_weight, proj_bias, kv_weight, key_gain, tile_map, tile_count, decode_owner
):
    tile_slots, shard_len, feature_width = features.shape
    token_rows = tile_slots * shard_len
    feature_rows = features.reshape(token_rows, feature_width)
    weight_cols = lax.all_gather(proj_weight, "tile", axis=0, tiled=True)
    projected = jnp.dot(feature_rows, weight_cols, preferred_element_type=jnp.float32)
    projected_local = (projected + proj_bias.astype(jnp.float32)).astype(jnp.bfloat16)
    kv_width = kv_weight.shape[1]
    projected_all = lax.all_gather(projected_local, "head", axis=1, tiled=True)
    key_value = add_columns(projected_all, lax.all_gather(kv_weight, "tile", axis=0, tiled=True))
    layers, head_dim = key_gain.shape
    blocks = key_value.reshape(token_rows, -1, layers, 2, head_dim)
    keys_raw = blocks[:, :, :, 0]
    inv_rms = lax.rsqrt(jnp.mean(keys_raw * keys_raw, axis=-1, keepdims=True) + eps_norm)
    keys_normed = keys_raw * inv_rms * key_gain[None, None]
    stacked = jnp.stack([keys_normed, blocks[:, :, :, 1]], axis=3).astype(jnp.bfloat16)
    per_tile = stacked.reshape(tile_slots, shard_len * kv_width)
    tile_ranks = lax.axis_size("tile")
    head_groups = lax.axis_size("head")
    most_tiles = tile_map.shape[1]
    owner_tile, owner_turn, matched = routing(
        tile_map, tile_count, decode_owner, tile_slots, head_groups
    )
    owned_by = (owner_tile[:, None] == jnp.arange(tile_ranks)[None, :]).astype(jnp.float32)
    selector = jnp.einsum("rd,rjs->jds", owned_by, matched.astype(jnp.float32))
    selector = selector.astype(jnp.bfloat16).reshape(most_tiles * tile_ranks, tile_slots)
    outgoing = add_columns(selector, per_tile).astype(jnp.bfloat16)
    outgoing = outgoing.reshape(most_tiles, tile_ranks, shard_len, kv_width)
    arrived = lax.all_to_all(outgoing, "tile", split_axis=1, concat_axis=1, tiled=True)
    gathered_rows = arrived.reshape(
        most_tiles * tile_ranks * shard_len, kv_width // head_dim, head_dim
    )
    my_turn = jnp.sum(jnp.where(owner_tile == lax.axis_index("tile"), owner_turn, 0))
    stride = 1
    while stride < head_groups:
        shifted = shifted_2(gathered_rows, "head", stride)
        gathered_rows = jnp.where(my_turn // stride % 2 == 1, shifted, gathered_rows)
        stride = stride * 2
    return gathered_rows[None, None]


def terms_body(choice, weight, near, far, own, second, mirror, first, *kept_rest):
    near_product = add_columns(weight[...], near[...])
    far_product = add_columns(weight[...], far[...])
    near_kept = choice[0] == 1
    kept = jnp.where(near_kept, near_product, far_product)
    sent = jnp.where(near_kept, far_product, near_product)
    tall, width = weight.shape[0], own.shape[1]
    i = pl.program_id(0)
    rows = pl.ds(pl.multiple_of(i * tall, tall), tall)
    first[rows, :] = sent[:, :width].astype(first.dtype)

    def write_direct():
        own[rows, :] = kept[:, :width]
        second[rows, :] = sent[:, width:].astype(second.dtype)
        mirror[rows, :] = kept[:, width:].astype(mirror.dtype)

    if len(kept_rest) == 0:
        write_direct()
    else:
        pl.when(i < 2)(write_direct)

        @pl.when(i == 2)
        def _():
            kept_rest[0][...] = kept
            first[3 * tall :, :] = sent[:, width:].astype(first.dtype)


def term_shapes(depth, width, all_direct):
    direct, wide, narrow = depth if all_direct else depth // 3 * 2, jnp.float32, jnp.bfloat16
    shapes = [((direct, width), t) for t in (wide, narrow, narrow)]
    shapes = shapes + [((2 * depth - direct, width), narrow)]
    if not all_direct:
        shapes = shapes + [((depth // 3, 2 * width), wide)]
    return [jax.ShapeDtypeStruct(*shape) for shape in shapes]


def product_terms(choice, weight, near, far, all_direct):
    depth, rows = weight.shape
    columns = near.shape[1]
    tall = depth // 3
    shapes = term_shapes(depth, columns // 2, all_direct)
    whole = [pl.BlockSpec(array.shape, lambda i, choice: (0, 0)) for array in (near, *shapes)]
    return pl.pallas_call(
        terms_body,
        out_shape=shapes,
        grid_spec=pltpu.PrefetchScalarGridSpec(
            num_scalar_prefetch=1,
            grid=(3,),
            in_specs=[pl.BlockSpec((tall, rows), lambda i, choice: (i, 0)), whole[0], whole[0]],
            out_specs=whole[1:],
        ),
        compiler_params=pltpu.CompilerParams(vmem_limit_bytes=32 * 1024 * 1024),
        cost_estimate=pl.CostEstimate(
            flops=4 * depth * rows * columns,
            bytes_accessed=2 * depth * rows + 4 * rows * columns + 5 * depth * columns,
            transcendentals=0,
        ),
    )(choice, weight, near, far)


def blank_arrays(shapes):
    return pl.pallas_call(
        lambda *refs: None,
        out_shape=shapes,
        out_specs=[pl.BlockSpec(memory_space=pl.ANY)] * len(shapes),
    )()


def product_plan(
    features, proj_weight, proj_bias, kv_weight, key_gain, tile_map, tile_count, decode_owner
):
    tile_slots, shard_len, feature_width = features.shape
    token_rows = tile_slots * shard_len
    depth = proj_weight.shape[0]
    layers, head_dim = key_gain.shape
    width = layers * head_dim
    most_tiles = tile_map.shape[1]
    group, tile, head = (lax.axis_index(name) for name in ("groups", "tile", "head"))
    first_core, first_chip = tile % 2 == 0, tile < 2
    at_end = (head == 0) | (head == 3)
    feature_rows = features.reshape(token_rows, feature_width)
    step = lax.optimization_barrier

    def moved(shard, target):
        pairs = []
        for t in range(4):
            for h in range(4):
                to_tile, to_head = target(t, h)
                pairs.append((t * 4 + h, to_tile * 4 + to_head))
        return lax.ppermute(shard, ("tile", "head"), pairs)

    def outer_core(h):
        return (h ^ h // 2) % 2

    feature_parts = [
        lax.dynamic_slice_in_dim(feature_rows, (tile ^ r) * depth, depth, axis=1) for r in range(4)
    ]

    def put_first(condition, one, other, axis):
        return jnp.concatenate(
            [jnp.where(condition, one, other), jnp.where(condition, other, one)], axis=axis
        )

    def both_heads(ours, theirs):
        return put_first(group == 0, ours, theirs, 1)

    choice = (at_end == first_core).astype(jnp.int32).reshape(1)

    def products(near, far, all_direct):
        return tuple(product_terms(choice, proj_weight, near, far, all_direct))

    rest = depth // 3

    def to_neighbour(block):
        return swapped(block, "head", 1)

    def over_middle(block):
        return swapped(block, "head", 3)

    def plus(block, *arrived):
        for other in arrived:
            block = block + other.astype(jnp.float32)
        return block

    def in_loop(chain, given, empty):
        return lax.fori_loop(0, once, lambda _, carry: chain(carry[0]), (given, empty))[1]

    def times_features(rows, parts):
        return sum(add_columns(parts[r], rows[r]) for r in range(4))

    def finish(total, part):
        finished = []
        for k in range(2):
            entries = total[:, k * width : (k + 1) * width].reshape(token_rows, layers, head_dim)
            entries = entries + bias_part[k, :, part][None]
            if part == 0:
                squares = jnp.mean(entries * entries, axis=-1, keepdims=True)
                entries = entries * lax.rsqrt(squares + eps_norm) * key_gain[None]
            finished.append(entries.reshape(token_rows, width).astype(jnp.bfloat16))
        return jnp.concatenate(finished, axis=1).reshape(tile_slots, shard_len, 2 * width)

    owner_tile, owner_turn, matched = routing(tile_map, tile_count, decode_owner, tile_slots, 4)
    turn_of = jnp.sum(jnp.where(matched, owner_turn[:, None, None], 0), axis=(0, 1))
    owned_by = (owner_tile[:, None] == (tile ^ jnp.arange(4))[None, :]).astype(jnp.float32)
    selector = jnp.einsum("rd,rjs->djs", owned_by, matched.astype(jnp.float32))
    selector = selector.astype(jnp.bfloat16).reshape(4 * most_tiles, tile_slots)

    turned = [turn_of // stride % 2 == 1 for stride in (1, 2)]

    def rolled(rows, shifted, stride):
        return jnp.where(turned[stride - 1][:, None, None], shifted, rows)

    def outgoing(rows):
        picked = add_columns(selector, rows.reshape(tile_slots, -1)).astype(jnp.bfloat16)
        picked = picked.reshape(4, most_tiles, shard_len, 2, layers, head_dim)
        return [picked[r] for r in range(4)]

    def to_owners(picked):
        return [picked[0]] + [swapped(picked[r], "tile", r) for r in (1, 2, 3)]

    def in_order(arrived):
        even = [jnp.where(first_core, arrived[r], arrived[r ^ 1]) for r in range(4)]
        ranked = [jnp.where(first_chip, even[r], even[r ^ 2]) for r in range(4)]
        return jnp.stack(ranked, axis=1)

    column, half = group * 2 * head_dim, kv_weight.shape[0] // 2

    def halves(weight, part):
        mine = lax.dynamic_slice_in_dim(weight, column + part * head_dim, head_dim, axis=1)
        ours = lax.dynamic_slice_in_dim(mine, tile // 2 * half, half, axis=0)
        return ours, lax.dynamic_slice_in_dim(mine, half - tile // 2 * half, half, axis=0)

    def to_planes(stays, comes):
        pieces = []
        for j in range(2):
            piece = jnp.where(tile // 2 == (head // 2) ^ j, stays, comes)
            pieces.append(
                moved(piece, lambda t, h: (t // 2 * 2 + outer_core(h), t % 2 + 2 * ((h // 2) ^ j)))
            )
        return pieces

    key_stays, key_leaves, rows_later = step((*halves(kv_weight, 0), kv_weight))
    bias_rows = moved(proj_bias, lambda t, h: (h, t))
    key_stays, key_comes, bias_rows, counts_later = step(
        (key_stays, swapped(key_leaves, "tile", 2), bias_rows, tile_count)
    )

    once = jnp.minimum(jnp.max(counts_later), 1)

    value_stays, value_leaves = halves(rows_later, 1)
    tokens = jax.ShapeDtypeStruct((tile_slots, shard_len, 2 * width), jnp.bfloat16)
    shapes = term_shapes(depth, width, True) + [tokens, tokens]
    *no_terms, no_keys, no_values = blank_arrays(shapes)
    bias_part = add_columns(bias_rows[None], rows_later)
    key_pieces, value_stays, value_comes, bias_part, once = step(
        (
            to_planes(key_stays, key_comes),
            value_stays,
            swapped(value_leaves, "tile", 2),
            bias_part,
            once,
        )
    )

    key_half = jnp.concatenate(key_pieces, axis=1)
    value_pieces = to_planes(value_stays, value_comes)
    key_half, key_other, feature_parts = step(
        (key_half, swapped(key_half, "tile", 2), feature_parts)
    )

    key_near = step(put_first(first_chip, key_half, key_other, 0))
    terms = products(key_near, swapped(key_near, "tile", 1), False)
    bias_part = bias_part + swapped(bias_part, "tile", 1)
    terms, value_pieces, bias_part = step((terms, value_pieces, bias_part))
    value_half = jnp.concatenate(value_pieces, axis=1)

    def values_terms(given):
        value_half, bias_part = given
        other, bias_other = step((swapped(value_half, "tile", 2), swapped(bias_part, "tile", 2)))
        near = step(put_first(first_chip, value_half, other, 0))
        terms = products(near, swapped(near, "tile", 1), True)
        return (other, bias_other), (terms, bias_part + bias_other)

    empty = tuple(no_terms), bias_part
    own, second, mirror, first, kept_rest = terms
    second, mirror, first, (value_terms, bias_part) = step(
        (
            swapped(second, "head", 2),
            over_middle(mirror),
            to_neighbour(first),
            in_loop(values_terms, (value_half, bias_part), empty),
        )
    )
    bias_part = bias_part.reshape(2, layers, 2, head_dim)

    direct = 2 * rest
    arrived = jnp.concatenate([first[direct : 3 * rest], first[3 * rest :]], axis=1)
    pair = plus(kept_rest, arrived)
    pair = step(pair)
    mirrored = over_middle(pair[:, width:].astype(jnp.bfloat16))
    pair, mirrored, value_terms = step((pair, mirrored, value_terms))
    blocks = [plus(own, second, mirror, first[:direct]), plus(pair[:, :width], mirrored)]
    own = jnp.concatenate([block.astype(jnp.bfloat16) for block in blocks], axis=0)

    def rest_of_plane(given, part):
        own, across_x, across_y = given
        rows_0 = step(both_heads(own, across_y))
        middle = depth // 2
        upper, lower, rows_1 = step(
            (
                swapped(across_x[:middle], "groups", 1),
                swapped(across_y[middle:], "tile", 2),
                swapped(rows_0, "tile", 1),
            )
        )
        rows_2 = step(both_heads(across_x, jnp.concatenate([upper, lower], axis=0)))
        rows = [rows_0, rows_1, rows_2, swapped(rows_2, "tile", 1)]
        return finish(times_features(rows, feature_parts), part)

    def keys_product(own):
        across_x, across_y = step((swapped(own, "tile", 2), swapped(own, "groups", 1)))
        rows_0 = step(both_heads(own, across_y))
        diagonal, rows_1 = step((swapped(across_y, "tile", 2), swapped(rows_0, "tile", 1)))
        rows_2 = step(both_heads(across_x, diagonal))
        rows = [rows_0, rows_1, rows_2, swapped(rows_2, "tile", 1)]
        return across_x, finish(times_features(rows, feature_parts), 0)

    value_own, second, mirror, first = value_terms
    second, mirror, first, keys = step(
        (
            swapped(second, "head", 2),
            over_middle(mirror),
            to_neighbour(first),
            in_loop(keys_product, own, no_keys),
        )
    )
    own = plus(value_own, second, mirror, first).astype(jnp.bfloat16)

    shifted, across_x, across_y = step(
        (shifted_2(keys, "head", 1), swapped(own, "tile", 2), swapped(own, "groups", 1))
    )

    def values_product(given):
        own, across_x, across_y = given
        return (across_y, own, across_x), rest_of_plane(given, 1)

    keys = step(rolled(keys, shifted, 1))
    values = in_loop(values_product, (own, across_x, across_y), no_values)
    shifted, values = step((shifted_2(keys, "head", 2), values))

    picked = outgoing(rolled(keys, shifted, 2))
    shifted, picked = step((shifted_2(values, "head", 1), picked))

    values = step(rolled(values, shifted, 1))
    arrived, shifted = step((to_owners(picked), shifted_2(values, "head", 2)))

    value_cache = in_order(to_owners(outgoing(rolled(values, shifted, 2))))
    cache = jnp.stack([in_order(arrived), value_cache], axis=-2)
    return cache.reshape(1, 1, most_tiles * 4 * shard_len, 4 * layers, head_dim)


def solution(mesh):
    placed = (
        P("groups", "tile", None),
        P("tile", "head"),
        P("head"),
        P("tile", "head"),
        P(),
        P("groups", None),
        P("groups"),
        P("groups"),
    )
    sizes = tuple(mesh.shape[name] for name in ("groups", "tile", "head"))
    return jax.shard_map(
        product_plan if sizes == (2, 4, 4) else gather_plan,
        mesh=mesh,
        in_specs=placed,
        out_specs=P(("groups", "tile"), "head", None, None, None),
        check_vma=False,
    )
```

```python
import jax
import jax.numpy as jnp
from jax import lax
from jax.experimental import pallas as pl
from jax.experimental.pallas import tpu as pltpu
from jax.sharding import PartitionSpec as P

eps_norm = 1e-05


def shifted_2(shard, axis, by):
    count = lax.axis_size(axis)
    return lax.ppermute(shard, axis, [(i, (i + by) % count) for i in range(count)])


def swapped(shard, axis, bit):
    return lax.ppermute(shard, axis, [(i, i ^ bit) for i in range(lax.axis_size(axis))])


def add_columns(operand, portion):
    return jnp.dot(operand, portion, preferred_element_type=jnp.float32)


def routing(tile_map, tile_count, decode_owner, tile_slots, head_groups):
    most_tiles = tile_map.shape[1]
    owner_tile = decode_owner // head_groups
    owner_turn = decode_owner % head_groups
    usable = jnp.arange(most_tiles)[None, :] < tile_count[:, None]
    matched = (tile_map[:, :, None] == jnp.arange(tile_slots)[None, None, :]) & usable[:, :, None]
    return owner_tile, owner_turn, matched


def gather_plan(
    features, proj_weight, proj_bias, kv_weight, key_gain, tile_map, tile_count, decode_owner
):
    tile_slots, shard_len, feature_width = features.shape
    token_rows = tile_slots * shard_len
    feature_rows = features.reshape(token_rows, feature_width)
    weight_cols = lax.all_gather(proj_weight, "tile", axis=0, tiled=True)
    projected = jnp.dot(feature_rows, weight_cols, preferred_element_type=jnp.float32)
    projected_local = (projected + proj_bias.astype(jnp.float32)).astype(jnp.bfloat16)
    kv_width = kv_weight.shape[1]
    projected_all = lax.all_gather(projected_local, "head", axis=1, tiled=True)
    key_value = add_columns(projected_all, lax.all_gather(kv_weight, "tile", axis=0, tiled=True))
    layers, head_dim = key_gain.shape
    blocks = key_value.reshape(token_rows, -1, layers, 2, head_dim)
    keys_raw = blocks[:, :, :, 0]
    inv_rms = lax.rsqrt(jnp.mean(keys_raw * keys_raw, axis=-1, keepdims=True) + eps_norm)
    keys_normed = keys_raw * inv_rms * key_gain[None, None]
    stacked = jnp.stack([keys_normed, blocks[:, :, :, 1]], axis=3).astype(jnp.bfloat16)
    per_tile = stacked.reshape(tile_slots, shard_len * kv_width)
    tile_ranks = lax.axis_size("tile")
    head_groups = lax.axis_size("head")
    most_tiles = tile_map.shape[1]
    owner_tile, owner_turn, matched = routing(
        tile_map, tile_count, decode_owner, tile_slots, head_groups
    )
    owned_by = (owner_tile[:, None] == jnp.arange(tile_ranks)[None, :]).astype(jnp.float32)
    selector = jnp.einsum("rd,rjs->jds", owned_by, matched.astype(jnp.float32))
    selector = selector.astype(jnp.bfloat16).reshape(most_tiles * tile_ranks, tile_slots)
    outgoing = add_columns(selector, per_tile).astype(jnp.bfloat16)
    outgoing = outgoing.reshape(most_tiles, tile_ranks, shard_len, kv_width)
    arrived = lax.all_to_all(outgoing, "tile", split_axis=1, concat_axis=1, tiled=True)
    gathered_rows = arrived.reshape(
        most_tiles * tile_ranks * shard_len, kv_width // head_dim, head_dim
    )
    my_turn = jnp.sum(jnp.where(owner_tile == lax.axis_index("tile"), owner_turn, 0))
    stride = 1
    while stride < head_groups:
        shifted = shifted_2(gathered_rows, "head", stride)
        gathered_rows = jnp.where(my_turn // stride % 2 == 1, shifted, gathered_rows)
        stride = stride * 2
    return gathered_rows[None, None]


def terms_body(choice, weight, near, far, own, second, mirror, first, *kept_rest):
    near_product = add_columns(weight[...], near[...])
    far_product = add_columns(weight[...], far[...])
    near_kept = choice[0] == 1
    kept = jnp.where(near_kept, near_product, far_product)
    sent = jnp.where(near_kept, far_product, near_product)
    tall, width = weight.shape[0], own.shape[1]
    i = pl.program_id(0)
    rows = pl.ds(pl.multiple_of(i * tall, tall), tall)
    first[rows, :] = sent[:, :width].astype(first.dtype)

    def write_direct():
        own[rows, :] = kept[:, :width]
        second[rows, :] = sent[:, width:].astype(second.dtype)
        mirror[rows, :] = kept[:, width:].astype(mirror.dtype)

    if len(kept_rest) == 0:
        write_direct()
    else:
        pl.when(i < 2)(write_direct)

        @pl.when(i == 2)
        def _():
            kept_rest[0][...] = kept
            first[3 * tall :, :] = sent[:, width:].astype(first.dtype)


def term_shapes(depth, width, all_direct):
    direct, wide, narrow = depth if all_direct else depth // 3 * 2, jnp.float32, jnp.bfloat16
    shapes = [((direct, width), t) for t in (wide, narrow, narrow)]
    shapes = shapes + [((2 * depth - direct, width), narrow)]
    if not all_direct:
        shapes = shapes + [((depth // 3, 2 * width), wide)]
    return [jax.ShapeDtypeStruct(*shape) for shape in shapes]


def product_terms(choice, weight, near, far, all_direct):
    depth, rows = weight.shape
    columns = near.shape[1]
    tall = depth // 3
    shapes = term_shapes(depth, columns // 2, all_direct)
    whole = [pl.BlockSpec(array.shape, lambda i, choice: (0, 0)) for array in (near, *shapes)]
    return pl.pallas_call(
        terms_body,
        out_shape=shapes,
        grid_spec=pltpu.PrefetchScalarGridSpec(
            num_scalar_prefetch=1,
            grid=(3,),
            in_specs=[pl.BlockSpec((tall, rows), lambda i, choice: (i, 0)), whole[0], whole[0]],
            out_specs=whole[1:],
        ),
        compiler_params=pltpu.CompilerParams(vmem_limit_bytes=32 * 1024 * 1024),
        cost_estimate=pl.CostEstimate(
            flops=4 * depth * rows * columns,
            bytes_accessed=2 * depth * rows + 4 * rows * columns + 5 * depth * columns,
            transcendentals=0,
        ),
    )(choice, weight, near, far)


def blank_arrays(shapes):
    return pl.pallas_call(
        lambda *refs: None,
        out_shape=shapes,
        out_specs=[pl.BlockSpec(memory_space=pl.ANY)] * len(shapes),
    )()


def product_plan(
    features, proj_weight, proj_bias, kv_weight, key_gain, tile_map, tile_count, decode_owner
):
    tile_slots, shard_len, feature_width = features.shape
    token_rows = tile_slots * shard_len
    depth = proj_weight.shape[0]
    layers, head_dim = key_gain.shape
    width = layers * head_dim
    most_tiles = tile_map.shape[1]
    group, tile, head = (lax.axis_index(name) for name in ("groups", "tile", "head"))
    first_core, first_chip = tile % 2 == 0, tile < 2
    at_end = (head == 0) | (head == 3)
    feature_rows = features.reshape(token_rows, feature_width)
    step = lax.optimization_barrier

    def moved(shard, target):
        pairs = []
        for t in range(4):
            for h in range(4):
                to_tile, to_head = target(t, h)
                pairs.append((t * 4 + h, to_tile * 4 + to_head))
        return lax.ppermute(shard, ("tile", "head"), pairs)

    def outer_core(h):
        return (h ^ h // 2) % 2

    feature_parts = [
        lax.dynamic_slice_in_dim(feature_rows, (tile ^ r) * depth, depth, axis=1) for r in range(4)
    ]

    def put_first(condition, one, other, axis):
        return jnp.concatenate(
            [jnp.where(condition, one, other), jnp.where(condition, other, one)], axis=axis
        )

    def both_heads(ours, theirs):
        return put_first(group == 0, ours, theirs, 1)

    choice = (at_end == first_core).astype(jnp.int32).reshape(1)

    def products(near, far, all_direct):
        return tuple(product_terms(choice, proj_weight, near, far, all_direct))

    rest = depth // 3

    def to_neighbour(block):
        return swapped(block, "head", 1)

    def over_middle(block):
        return swapped(block, "head", 3)

    def plus(block, *arrived):
        for other in arrived:
            block = block + other.astype(jnp.float32)
        return block

    def in_loop(chain, given, empty):
        return lax.fori_loop(0, once, lambda _, carry: chain(carry[0]), (given, empty))[1]

    def times_features(rows, parts):
        return sum(add_columns(parts[r], rows[r]) for r in range(4))

    def finish(total, part):
        finished = []
        for k in range(2):
            entries = total[:, k * width : (k + 1) * width].reshape(token_rows, layers, head_dim)
            entries = entries + bias_part[k, :, part][None]
            if part == 0:
                squares = jnp.mean(entries * entries, axis=-1, keepdims=True)
                entries = entries * lax.rsqrt(squares + eps_norm) * key_gain[None]
            finished.append(entries.reshape(token_rows, width).astype(jnp.bfloat16))
        return jnp.concatenate(finished, axis=1).reshape(tile_slots, shard_len, 2 * width)

    owner_tile, owner_turn, matched = routing(tile_map, tile_count, decode_owner, tile_slots, 4)
    turn_of = jnp.sum(jnp.where(matched, owner_turn[:, None, None], 0), axis=(0, 1))
    owned_by = (owner_tile[:, None] == (tile ^ jnp.arange(4))[None, :]).astype(jnp.float32)
    selector = jnp.einsum("rd,rjs->djs", owned_by, matched.astype(jnp.float32))
    selector = selector.astype(jnp.bfloat16).reshape(4 * most_tiles, tile_slots)

    turned = [turn_of // stride % 2 == 1 for stride in (1, 2)]

    def rolled(rows, shifted, stride):
        return jnp.where(turned[stride - 1][:, None, None], shifted, rows)

    def outgoing(rows):
        picked = add_columns(selector, rows.reshape(tile_slots, -1)).astype(jnp.bfloat16)
        picked = picked.reshape(4, most_tiles, shard_len, 2, layers, head_dim)
        return [picked[r] for r in range(4)]

    def to_owners(picked):
        return [picked[0]] + [swapped(picked[r], "tile", r) for r in (1, 2, 3)]

    def in_order(arrived):
        even = [jnp.where(first_core, arrived[r], arrived[r ^ 1]) for r in range(4)]
        ranked = [jnp.where(first_chip, even[r], even[r ^ 2]) for r in range(4)]
        return jnp.stack(ranked, axis=1)

    column, half = group * 2 * head_dim, kv_weight.shape[0] // 2

    def halves(weight, part):
        mine = lax.dynamic_slice_in_dim(weight, column + part * head_dim, head_dim, axis=1)
        ours = lax.dynamic_slice_in_dim(mine, tile // 2 * half, half, axis=0)
        return ours, lax.dynamic_slice_in_dim(mine, half - tile // 2 * half, half, axis=0)

    def to_planes(stays, comes):
        pieces = []
        for j in range(2):
            piece = jnp.where(tile // 2 == (head // 2) ^ j, stays, comes)
            pieces.append(
                moved(piece, lambda t, h: (t // 2 * 2 + outer_core(h), t % 2 + 2 * ((h // 2) ^ j)))
            )
        return pieces

    key_stays, key_leaves, rows_later = step((*halves(kv_weight, 0), kv_weight))
    bias_rows = moved(proj_bias, lambda t, h: (h, t))
    value_stays, value_leaves = halves(rows_later, 1)
    key_stays, key_comes, bias_rows, counts_later, value_stays, value_leaves = step(
        (
            key_stays,
            swapped(key_leaves, "tile", 2),
            bias_rows,
            tile_count,
            value_stays,
            value_leaves,
        )
    )

    once = jnp.minimum(jnp.max(counts_later), 1)

    tokens = jax.ShapeDtypeStruct((tile_slots, shard_len, 2 * width), jnp.bfloat16)
    shapes = term_shapes(depth, width, True) + [tokens, tokens]
    *no_terms, no_keys, no_values = blank_arrays(shapes)
    bias_part = add_columns(bias_rows[None], rows_later)
    key_pieces, value_stays, value_comes, bias_part, once = step(
        (
            to_planes(key_stays, key_comes),
            value_stays,
            swapped(value_leaves, "tile", 2),
            bias_part,
            once,
        )
    )

    key_half = jnp.concatenate(key_pieces, axis=1)
    value_pieces = to_planes(value_stays, value_comes)
    key_half, key_other, feature_parts = step(
        (key_half, swapped(key_half, "tile", 2), feature_parts)
    )

    key_near = step(put_first(first_chip, key_half, key_other, 0))
    terms = products(key_near, swapped(key_near, "tile", 1), False)
    bias_part = bias_part + swapped(bias_part, "tile", 1)
    terms, value_pieces, bias_part = step((terms, value_pieces, bias_part))
    value_half = jnp.concatenate(value_pieces, axis=1)

    def values_terms(given):
        value_half, bias_part = given
        other, bias_other = step((swapped(value_half, "tile", 2), swapped(bias_part, "tile", 2)))
        near = step(put_first(first_chip, value_half, other, 0))
        terms = products(near, swapped(near, "tile", 1), True)
        return (other, bias_other), (terms, bias_part + bias_other)

    empty = tuple(no_terms), bias_part
    own, second, mirror, first, kept_rest = terms
    second, mirror, first, (value_terms, bias_part) = step(
        (
            swapped(second, "head", 2),
            over_middle(mirror),
            to_neighbour(first),
            in_loop(values_terms, (value_half, bias_part), empty),
        )
    )
    bias_part = bias_part.reshape(2, layers, 2, head_dim)

    direct = 2 * rest
    arrived = jnp.concatenate([first[direct : 3 * rest], first[3 * rest :]], axis=1)
    pair = plus(kept_rest, arrived)
    pair = step(pair)
    mirrored = over_middle(pair[:, width:].astype(jnp.bfloat16))
    pair, mirrored, value_terms = step((pair, mirrored, value_terms))
    blocks = [plus(own, second, mirror, first[:direct]), plus(pair[:, :width], mirrored)]
    own = jnp.concatenate([block.astype(jnp.bfloat16) for block in blocks], axis=0)

    def rest_of_plane(given, part):
        own, across_x, across_y = given
        rows_0 = step(both_heads(own, across_y))
        middle = depth // 2
        upper, lower, rows_1 = step(
            (
                swapped(across_x[:middle], "groups", 1),
                swapped(across_y[middle:], "tile", 2),
                swapped(rows_0, "tile", 1),
            )
        )
        rows_2 = step(both_heads(across_x, jnp.concatenate([upper, lower], axis=0)))
        rows = [rows_0, rows_1, rows_2, swapped(rows_2, "tile", 1)]
        return finish(times_features(rows, feature_parts), part)

    def keys_product(own):
        across_x, across_y = step((swapped(own, "tile", 2), swapped(own, "groups", 1)))
        rows_0 = step(both_heads(own, across_y))
        diagonal, rows_1 = step((swapped(across_y, "tile", 2), swapped(rows_0, "tile", 1)))
        rows_2 = step(both_heads(across_x, diagonal))
        rows = [rows_0, rows_1, rows_2, swapped(rows_2, "tile", 1)]
        return across_x, finish(times_features(rows, feature_parts), 0)

    value_own, second, mirror, first = value_terms
    second, mirror, first, keys = step(
        (
            swapped(second, "head", 2),
            over_middle(mirror),
            to_neighbour(first),
            in_loop(keys_product, own, no_keys),
        )
    )
    own = plus(value_own, second, mirror, first).astype(jnp.bfloat16)

    shifted, across_x, across_y = step(
        (shifted_2(keys, "head", 1), swapped(own, "tile", 2), swapped(own, "groups", 1))
    )

    def values_product(given):
        own, across_x, across_y = given
        return (across_y, own, across_x), rest_of_plane(given, 1)

    keys = step(rolled(keys, shifted, 1))
    values = in_loop(values_product, (own, across_x, across_y), no_values)
    shifted, values = step((shifted_2(keys, "head", 2), values))

    picked = outgoing(rolled(keys, shifted, 2))
    shifted, picked = step((shifted_2(values, "head", 1), picked))

    values = step(rolled(values, shifted, 1))
    arrived, shifted = step((to_owners(picked), shifted_2(values, "head", 2)))

    value_cache = in_order(to_owners(outgoing(rolled(values, shifted, 2))))
    cache = jnp.stack([in_order(arrived), value_cache], axis=-2)
    return cache.reshape(1, 1, most_tiles * 4 * shard_len, 4 * layers, head_dim)


def solution(mesh):
    placed = (
        P("groups", "tile", None),
        P("tile", "head"),
        P("head"),
        P("tile", "head"),
        P(),
        P("groups", None),
        P("groups"),
        P("groups"),
    )
    sizes = tuple(mesh.shape[name] for name in ("groups", "tile", "head"))
    return jax.shard_map(
        product_plan if sizes == (2, 4, 4) else gather_plan,
        mesh=mesh,
        in_specs=placed,
        out_specs=P(("groups", "tile"), "head", None, None, None),
        check_vma=False,
    )
```

```python
import jax
import jax.numpy as jnp
from jax import lax
from jax.experimental import pallas as pl
from jax.experimental.pallas import tpu as pltpu
from jax.sharding import PartitionSpec as P

eps_norm = 1e-05


def shifted_2(shard, axis, by):
    count = lax.axis_size(axis)
    return lax.ppermute(shard, axis, [(i, (i + by) % count) for i in range(count)])


def swapped(shard, axis, bit):
    return lax.ppermute(shard, axis, [(i, i ^ bit) for i in range(lax.axis_size(axis))])


def add_columns(operand, portion):
    return jnp.dot(operand, portion, preferred_element_type=jnp.float32)


def routing(tile_map, tile_count, decode_owner, tile_slots, head_groups):
    most_tiles = tile_map.shape[1]
    owner_tile = decode_owner // head_groups
    owner_turn = decode_owner % head_groups
    usable = jnp.arange(most_tiles)[None, :] < tile_count[:, None]
    matched = (tile_map[:, :, None] == jnp.arange(tile_slots)[None, None, :]) & usable[:, :, None]
    return owner_tile, owner_turn, matched


def gather_plan(
    features, proj_weight, proj_bias, kv_weight, key_gain, tile_map, tile_count, decode_owner
):
    tile_slots, shard_len, feature_width = features.shape
    token_rows = tile_slots * shard_len
    feature_rows = features.reshape(token_rows, feature_width)
    weight_cols = lax.all_gather(proj_weight, "tile", axis=0, tiled=True)
    projected = jnp.dot(feature_rows, weight_cols, preferred_element_type=jnp.float32)
    projected_local = (projected + proj_bias.astype(jnp.float32)).astype(jnp.bfloat16)
    kv_width = kv_weight.shape[1]
    projected_all = lax.all_gather(projected_local, "head", axis=1, tiled=True)
    key_value = add_columns(projected_all, lax.all_gather(kv_weight, "tile", axis=0, tiled=True))
    layers, head_dim = key_gain.shape
    blocks = key_value.reshape(token_rows, -1, layers, 2, head_dim)
    keys_raw = blocks[:, :, :, 0]
    inv_rms = lax.rsqrt(jnp.mean(keys_raw * keys_raw, axis=-1, keepdims=True) + eps_norm)
    keys_normed = keys_raw * inv_rms * key_gain[None, None]
    stacked = jnp.stack([keys_normed, blocks[:, :, :, 1]], axis=3).astype(jnp.bfloat16)
    per_tile = stacked.reshape(tile_slots, shard_len * kv_width)
    tile_ranks = lax.axis_size("tile")
    head_groups = lax.axis_size("head")
    most_tiles = tile_map.shape[1]
    owner_tile, owner_turn, matched = routing(
        tile_map, tile_count, decode_owner, tile_slots, head_groups
    )
    owned_by = (owner_tile[:, None] == jnp.arange(tile_ranks)[None, :]).astype(jnp.float32)
    selector = jnp.einsum("rd,rjs->jds", owned_by, matched.astype(jnp.float32))
    selector = selector.astype(jnp.bfloat16).reshape(most_tiles * tile_ranks, tile_slots)
    outgoing = add_columns(selector, per_tile).astype(jnp.bfloat16)
    outgoing = outgoing.reshape(most_tiles, tile_ranks, shard_len, kv_width)
    arrived = lax.all_to_all(outgoing, "tile", split_axis=1, concat_axis=1, tiled=True)
    gathered_rows = arrived.reshape(
        most_tiles * tile_ranks * shard_len, kv_width // head_dim, head_dim
    )
    my_turn = jnp.sum(jnp.where(owner_tile == lax.axis_index("tile"), owner_turn, 0))
    stride = 1
    while stride < head_groups:
        shifted = shifted_2(gathered_rows, "head", stride)
        gathered_rows = jnp.where(my_turn // stride % 2 == 1, shifted, gathered_rows)
        stride = stride * 2
    return gathered_rows[None, None]


def terms_body(choice, weight, near, far, own, second, mirror, first, *kept_rest):
    near_product = add_columns(weight[...], near[...])
    far_product = add_columns(weight[...], far[...])
    near_kept = choice[0] == 1
    kept = jnp.where(near_kept, near_product, far_product)
    sent = jnp.where(near_kept, far_product, near_product)
    tall, width = weight.shape[0], own.shape[1]
    i = pl.program_id(0)
    rows = pl.ds(pl.multiple_of(i * tall, tall), tall)
    first[rows, :] = sent[:, :width].astype(first.dtype)

    def write_direct():
        own[rows, :] = kept[:, :width]
        second[rows, :] = sent[:, width:].astype(second.dtype)
        mirror[rows, :] = kept[:, width:].astype(mirror.dtype)

    if len(kept_rest) == 0:
        write_direct()
    else:
        pl.when(i < 2)(write_direct)

        @pl.when(i == 2)
        def _():
            kept_rest[0][...] = kept
            first[3 * tall :, :] = sent[:, width:].astype(first.dtype)


def term_shapes(depth, width, all_direct):
    direct, wide, narrow = depth if all_direct else depth // 3 * 2, jnp.float32, jnp.bfloat16
    shapes = [((direct, width), t) for t in (wide, narrow, narrow)]
    shapes = shapes + [((2 * depth - direct, width), narrow)]
    if not all_direct:
        shapes = shapes + [((depth // 3, 2 * width), wide)]
    return [jax.ShapeDtypeStruct(*shape) for shape in shapes]


def product_terms(choice, weight, near, far, all_direct):
    depth, rows = weight.shape
    columns = near.shape[1]
    tall = depth // 3
    shapes = term_shapes(depth, columns // 2, all_direct)
    whole = [pl.BlockSpec(array.shape, lambda i, choice: (0, 0)) for array in (near, *shapes)]
    return pl.pallas_call(
        terms_body,
        out_shape=shapes,
        grid_spec=pltpu.PrefetchScalarGridSpec(
            num_scalar_prefetch=1,
            grid=(3,),
            in_specs=[pl.BlockSpec((tall, rows), lambda i, choice: (i, 0)), whole[0], whole[0]],
            out_specs=whole[1:],
        ),
        compiler_params=pltpu.CompilerParams(vmem_limit_bytes=32 * 1024 * 1024),
        cost_estimate=pl.CostEstimate(
            flops=4 * depth * rows * columns,
            bytes_accessed=2 * depth * rows + 4 * rows * columns + 5 * depth * columns,
            transcendentals=0,
        ),
    )(choice, weight, near, far)


def blank_arrays(shapes):
    return pl.pallas_call(
        lambda *refs: None,
        out_shape=shapes,
        out_specs=[pl.BlockSpec(memory_space=pl.ANY)] * len(shapes),
    )()


def product_plan(
    features, proj_weight, proj_bias, kv_weight, key_gain, tile_map, tile_count, decode_owner
):
    tile_slots, shard_len, feature_width = features.shape
    token_rows = tile_slots * shard_len
    depth = proj_weight.shape[0]
    layers, head_dim = key_gain.shape
    width = layers * head_dim
    most_tiles = tile_map.shape[1]
    group, tile, head = (lax.axis_index(name) for name in ("groups", "tile", "head"))
    first_core, first_chip = tile % 2 == 0, tile < 2
    at_end = (head == 0) | (head == 3)
    feature_rows = features.reshape(token_rows, feature_width)
    step = lax.optimization_barrier

    def moved(shard, target):
        pairs = []
        for t in range(4):
            for h in range(4):
                to_tile, to_head = target(t, h)
                pairs.append((t * 4 + h, to_tile * 4 + to_head))
        return lax.ppermute(shard, ("tile", "head"), pairs)

    def outer_core(h):
        return (h ^ h // 2) % 2

    feature_parts = [
        lax.dynamic_slice_in_dim(feature_rows, (tile ^ r) * depth, depth, axis=1) for r in range(4)
    ]

    def put_first(condition, one, other, axis):
        return jnp.concatenate(
            [jnp.where(condition, one, other), jnp.where(condition, other, one)], axis=axis
        )

    def both_heads(ours, theirs):
        return put_first(group == 0, ours, theirs, 1)

    choice = (at_end == first_core).astype(jnp.int32).reshape(1)

    def products(near, far, all_direct):
        return tuple(product_terms(choice, proj_weight, near, far, all_direct))

    rest = depth // 3

    def to_neighbour(block):
        return swapped(block, "head", 1)

    def over_middle(block):
        return swapped(block, "head", 3)

    def plus(block, *arrived):
        for other in arrived:
            block = block + other.astype(jnp.float32)
        return block

    def in_loop(chain, given, empty):
        return lax.fori_loop(0, once, lambda _, carry: chain(carry[0]), (given, empty))[1]

    def times_features(rows, parts):
        return sum(add_columns(parts[r], rows[r]) for r in range(4))

    def finish(total, part):
        finished = []
        for k in range(2):
            entries = total[:, k * width : (k + 1) * width].reshape(token_rows, layers, head_dim)
            entries = entries + bias_part[k, :, part][None]
            if part == 0:
                squares = jnp.mean(entries * entries, axis=-1, keepdims=True)
                entries = entries * lax.rsqrt(squares + eps_norm) * key_gain[None]
            finished.append(entries.reshape(token_rows, width).astype(jnp.bfloat16))
        return jnp.concatenate(finished, axis=1).reshape(tile_slots, shard_len, 2 * width)

    owner_tile, owner_turn, matched = routing(tile_map, tile_count, decode_owner, tile_slots, 4)
    turn_of = jnp.sum(jnp.where(matched, owner_turn[:, None, None], 0), axis=(0, 1))
    owned_by = (owner_tile[:, None] == (tile ^ jnp.arange(4))[None, :]).astype(jnp.float32)
    selector = jnp.einsum("rd,rjs->djs", owned_by, matched.astype(jnp.float32))
    selector = selector.astype(jnp.bfloat16).reshape(4 * most_tiles, tile_slots)

    turned = [turn_of // stride % 2 == 1 for stride in (1, 2)]

    def rolled(rows, shifted, stride):
        return jnp.where(turned[stride - 1][:, None, None], shifted, rows)

    def outgoing(rows):
        picked = add_columns(selector, rows.reshape(tile_slots, -1)).astype(jnp.bfloat16)
        picked = picked.reshape(4, most_tiles, shard_len, 2, layers, head_dim)
        return [picked[r] for r in range(4)]

    def to_owners(picked):
        return [picked[0]] + [swapped(picked[r], "tile", r) for r in (1, 2, 3)]

    def in_order(arrived):
        even = [jnp.where(first_core, arrived[r], arrived[r ^ 1]) for r in range(4)]
        ranked = [jnp.where(first_chip, even[r], even[r ^ 2]) for r in range(4)]
        return jnp.stack(ranked, axis=1)

    column, half = group * 2 * head_dim, kv_weight.shape[0] // 2

    def halves(weight, part):
        mine = lax.dynamic_slice_in_dim(weight, column + part * head_dim, head_dim, axis=1)
        ours = lax.dynamic_slice_in_dim(mine, tile // 2 * half, half, axis=0)
        return ours, lax.dynamic_slice_in_dim(mine, half - tile // 2 * half, half, axis=0)

    def to_planes(stays, comes):
        pieces = []
        for j in range(2):
            piece = jnp.where(tile // 2 == (head // 2) ^ j, stays, comes)
            pieces.append(
                moved(piece, lambda t, h: (t // 2 * 2 + outer_core(h), t % 2 + 2 * ((h // 2) ^ j)))
            )
        return pieces

    key_stays, key_leaves, rows_later = step((*halves(kv_weight, 0), kv_weight))
    bias_rows = moved(proj_bias, lambda t, h: (h, t))
    value_stays, value_leaves = halves(rows_later, 1)
    key_stays, key_comes, bias_rows, counts_later, value_stays, value_leaves = step(
        (
            key_stays,
            swapped(key_leaves, "tile", 2),
            bias_rows,
            tile_count,
            value_stays,
            value_leaves,
        )
    )

    once = jnp.minimum(jnp.max(counts_later), 1)

    tokens = jax.ShapeDtypeStruct((tile_slots, shard_len, 2 * width), jnp.bfloat16)
    shapes = term_shapes(depth, width, True) + [tokens, tokens]
    *no_terms, no_keys, no_values = blank_arrays(shapes)
    bias_part = add_columns(bias_rows[None], rows_later)
    key_pieces, value_stays, value_comes, bias_part, once = step(
        (
            to_planes(key_stays, key_comes),
            value_stays,
            swapped(value_leaves, "tile", 2),
            bias_part,
            once,
        )
    )

    key_half = jnp.concatenate(key_pieces, axis=1)
    value_pieces = to_planes(value_stays, value_comes)
    key_half, key_other, feature_parts = step(
        (key_half, swapped(key_half, "tile", 2), feature_parts)
    )

    key_near = step(put_first(first_chip, key_half, key_other, 0))
    terms = products(key_near, swapped(key_near, "tile", 1), False)
    bias_part = bias_part + swapped(bias_part, "tile", 1)
    terms, value_pieces, bias_part = step((terms, value_pieces, bias_part))
    value_half = jnp.concatenate(value_pieces, axis=1)

    def values_terms(given):
        value_half, bias_part = given
        other, bias_other = step((swapped(value_half, "tile", 2), swapped(bias_part, "tile", 2)))
        near = step(put_first(first_chip, value_half, other, 0))
        terms = products(near, swapped(near, "tile", 1), True)
        return (other, bias_other), (terms, bias_part + bias_other)

    empty = tuple(no_terms), bias_part
    own, second, mirror, first, kept_rest = terms
    second, mirror, first, (value_terms, bias_part) = step(
        (
            swapped(second, "head", 2),
            over_middle(mirror),
            to_neighbour(first),
            in_loop(values_terms, (value_half, bias_part), empty),
        )
    )
    bias_part = bias_part.reshape(2, layers, 2, head_dim)

    direct = 2 * rest
    arrived = jnp.concatenate([first[direct : 3 * rest], first[3 * rest :]], axis=1)
    pair = plus(kept_rest, arrived)
    pair = step(pair)
    mirrored = over_middle(pair[:, width:].astype(jnp.bfloat16))
    pair, mirrored, value_terms = step((pair, mirrored, value_terms))
    blocks = [plus(own, second, mirror, first[:direct]), plus(pair[:, :width], mirrored)]
    own = jnp.concatenate([block.astype(jnp.bfloat16) for block in blocks], axis=0)

    def rest_of_plane(given, part):
        own, across_x, across_y = given
        rows_0 = step(both_heads(own, across_y))
        middle = depth // 2
        upper, lower, rows_1 = step(
            (
                swapped(across_x[:middle], "groups", 1),
                swapped(across_y[middle:], "tile", 2),
                swapped(rows_0, "tile", 1),
            )
        )
        rows_2 = step(both_heads(across_x, jnp.concatenate([upper, lower], axis=0)))
        rows = [rows_0, rows_1, rows_2, swapped(rows_2, "tile", 1)]
        return finish(times_features(rows, feature_parts), part)

    def keys_product(own):
        across_x, across_y = step((swapped(own, "tile", 2), swapped(own, "groups", 1)))
        rows_0 = step(both_heads(own, across_y))
        diagonal, rows_1 = step((swapped(across_y, "tile", 2), swapped(rows_0, "tile", 1)))
        rows_2 = step(both_heads(across_x, diagonal))
        rows = [rows_0, rows_1, rows_2, swapped(rows_2, "tile", 1)]
        return across_x, finish(times_features(rows, feature_parts), 0)

    value_own, second, mirror, first = value_terms
    second, mirror, first, keys = step(
        (
            swapped(second, "head", 2),
            over_middle(mirror),
            to_neighbour(first),
            in_loop(keys_product, own, no_keys),
        )
    )
    own = plus(value_own, second, mirror, first).astype(jnp.bfloat16)

    shifted, across_x, across_y = step(
        (shifted_2(keys, "head", 1), swapped(own, "tile", 2), swapped(own, "groups", 1))
    )

    def values_product(given):
        own, across_x, across_y = given
        return (across_y, own, across_x), rest_of_plane(given, 1)

    keys = step(rolled(keys, shifted, 1))
    values = in_loop(values_product, (own, across_x, across_y), no_values)
    shifted, values = step((shifted_2(keys, "head", 2), values))

    picked = outgoing(rolled(keys, shifted, 2))
    values, shifted = step((values, shifted_2(values, "head", 1)))

    values = step(rolled(values, shifted, 1))
    arrived, shifted = step((to_owners(picked), shifted_2(values, "head", 2)))

    value_cache = in_order(to_owners(outgoing(rolled(values, shifted, 2))))
    cache = jnp.stack([in_order(arrived), value_cache], axis=-2)
    return cache.reshape(1, 1, most_tiles * 4 * shard_len, 4 * layers, head_dim)


def solution(mesh):
    placed = (
        P("groups", "tile", None),
        P("tile", "head"),
        P("head"),
        P("tile", "head"),
        P(),
        P("groups", None),
        P("groups"),
        P("groups"),
    )
    sizes = tuple(mesh.shape[name] for name in ("groups", "tile", "head"))
    return jax.shard_map(
        product_plan if sizes == (2, 4, 4) else gather_plan,
        mesh=mesh,
        in_specs=placed,
        out_specs=P(("groups", "tile"), "head", None, None, None),
        check_vma=False,
    )
```

```python
import jax
import jax.numpy as jnp
from jax import lax
from jax.experimental import pallas as pl
from jax.experimental.pallas import tpu as pltpu
from jax.sharding import PartitionSpec as P

eps_norm = 1e-05


def shifted_2(shard, axis, by):
    count = lax.axis_size(axis)
    return lax.ppermute(shard, axis, [(i, (i + by) % count) for i in range(count)])


def swapped(shard, axis, bit):
    return lax.ppermute(shard, axis, [(i, i ^ bit) for i in range(lax.axis_size(axis))])


def add_columns(operand, portion):
    return jnp.dot(operand, portion, preferred_element_type=jnp.float32)


def routing(tile_map, tile_count, decode_owner, tile_slots, head_groups):
    most_tiles = tile_map.shape[1]
    owner_tile = decode_owner // head_groups
    owner_turn = decode_owner % head_groups
    usable = jnp.arange(most_tiles)[None, :] < tile_count[:, None]
    matched = (tile_map[:, :, None] == jnp.arange(tile_slots)[None, None, :]) & usable[:, :, None]
    return owner_tile, owner_turn, matched


def gather_plan(
    features, proj_weight, proj_bias, kv_weight, key_gain, tile_map, tile_count, decode_owner
):
    tile_slots, shard_len, feature_width = features.shape
    token_rows = tile_slots * shard_len
    feature_rows = features.reshape(token_rows, feature_width)
    weight_cols = lax.all_gather(proj_weight, "tile", axis=0, tiled=True)
    projected = jnp.dot(feature_rows, weight_cols, preferred_element_type=jnp.float32)
    projected_local = (projected + proj_bias.astype(jnp.float32)).astype(jnp.bfloat16)
    kv_width = kv_weight.shape[1]
    projected_all = lax.all_gather(projected_local, "head", axis=1, tiled=True)
    key_value = add_columns(projected_all, lax.all_gather(kv_weight, "tile", axis=0, tiled=True))
    layers, head_dim = key_gain.shape
    blocks = key_value.reshape(token_rows, -1, layers, 2, head_dim)
    keys_raw = blocks[:, :, :, 0]
    inv_rms = lax.rsqrt(jnp.mean(keys_raw * keys_raw, axis=-1, keepdims=True) + eps_norm)
    keys_normed = keys_raw * inv_rms * key_gain[None, None]
    stacked = jnp.stack([keys_normed, blocks[:, :, :, 1]], axis=3).astype(jnp.bfloat16)
    per_tile = stacked.reshape(tile_slots, shard_len * kv_width)
    tile_ranks = lax.axis_size("tile")
    head_groups = lax.axis_size("head")
    most_tiles = tile_map.shape[1]
    owner_tile, owner_turn, matched = routing(
        tile_map, tile_count, decode_owner, tile_slots, head_groups
    )
    owned_by = (owner_tile[:, None] == jnp.arange(tile_ranks)[None, :]).astype(jnp.float32)
    selector = jnp.einsum("rd,rjs->jds", owned_by, matched.astype(jnp.float32))
    selector = selector.astype(jnp.bfloat16).reshape(most_tiles * tile_ranks, tile_slots)
    outgoing = add_columns(selector, per_tile).astype(jnp.bfloat16)
    outgoing = outgoing.reshape(most_tiles, tile_ranks, shard_len, kv_width)
    arrived = lax.all_to_all(outgoing, "tile", split_axis=1, concat_axis=1, tiled=True)
    gathered_rows = arrived.reshape(
        most_tiles * tile_ranks * shard_len, kv_width // head_dim, head_dim
    )
    my_turn = jnp.sum(jnp.where(owner_tile == lax.axis_index("tile"), owner_turn, 0))
    stride = 1
    while stride < head_groups:
        shifted = shifted_2(gathered_rows, "head", stride)
        gathered_rows = jnp.where(my_turn // stride % 2 == 1, shifted, gathered_rows)
        stride = stride * 2
    return gathered_rows[None, None]


def terms_body(choice, weight, near, far, own, second, mirror, first, *kept_rest):
    near_product = add_columns(weight[...], near[...])
    far_product = add_columns(weight[...], far[...])
    near_kept = choice[0] == 1
    kept = jnp.where(near_kept, near_product, far_product)
    sent = jnp.where(near_kept, far_product, near_product)
    tall, width = weight.shape[0], own.shape[1]
    i = pl.program_id(0)
    rows = pl.ds(pl.multiple_of(i * tall, tall), tall)
    first[rows, :] = sent[:, :width].astype(first.dtype)

    def write_direct():
        own[rows, :] = kept[:, :width]
        second[rows, :] = sent[:, width:].astype(second.dtype)
        mirror[rows, :] = kept[:, width:].astype(mirror.dtype)

    if len(kept_rest) == 0:
        write_direct()
    else:
        pl.when(i < 2)(write_direct)

        @pl.when(i == 2)
        def _():
            kept_rest[0][...] = kept
            first[3 * tall :, :] = sent[:, width:].astype(first.dtype)


def term_shapes(depth, width, all_direct):
    direct, wide, narrow = depth if all_direct else depth // 3 * 2, jnp.float32, jnp.bfloat16
    shapes = [((direct, width), t) for t in (wide, narrow, narrow)]
    shapes = shapes + [((2 * depth - direct, width), narrow)]
    if not all_direct:
        shapes = shapes + [((depth // 3, 2 * width), wide)]
    return [jax.ShapeDtypeStruct(*shape) for shape in shapes]


def product_terms(choice, weight, near, far, all_direct):
    depth, rows = weight.shape
    columns = near.shape[1]
    tall = depth // 3
    shapes = term_shapes(depth, columns // 2, all_direct)
    whole = [pl.BlockSpec(array.shape, lambda i, choice: (0, 0)) for array in (near, *shapes)]
    return pl.pallas_call(
        terms_body,
        out_shape=shapes,
        grid_spec=pltpu.PrefetchScalarGridSpec(
            num_scalar_prefetch=1,
            grid=(3,),
            in_specs=[pl.BlockSpec((tall, rows), lambda i, choice: (i, 0)), whole[0], whole[0]],
            out_specs=whole[1:],
        ),
        compiler_params=pltpu.CompilerParams(vmem_limit_bytes=32 * 1024 * 1024),
        cost_estimate=pl.CostEstimate(
            flops=4 * depth * rows * columns,
            bytes_accessed=2 * depth * rows + 4 * rows * columns + 5 * depth * columns,
            transcendentals=0,
        ),
    )(choice, weight, near, far)


def blank_arrays(shapes):
    return pl.pallas_call(
        lambda *refs: None,
        out_shape=shapes,
        out_specs=[pl.BlockSpec(memory_space=pl.ANY)] * len(shapes),
    )()


def product_plan(
    features, proj_weight, proj_bias, kv_weight, key_gain, tile_map, tile_count, decode_owner
):
    tile_slots, shard_len, feature_width = features.shape
    token_rows = tile_slots * shard_len
    depth = proj_weight.shape[0]
    layers, head_dim = key_gain.shape
    width = layers * head_dim
    most_tiles = tile_map.shape[1]
    group, tile, head = (lax.axis_index(name) for name in ("groups", "tile", "head"))
    first_core, first_chip = tile % 2 == 0, tile < 2
    at_end = (head == 0) | (head == 3)
    feature_rows = features.reshape(token_rows, feature_width)
    step = lax.optimization_barrier

    def moved(shard, target):
        pairs = []
        for t in range(4):
            for h in range(4):
                to_tile, to_head = target(t, h)
                pairs.append((t * 4 + h, to_tile * 4 + to_head))
        return lax.ppermute(shard, ("tile", "head"), pairs)

    def outer_core(h):
        return (h ^ h // 2) % 2

    feature_parts = [
        lax.dynamic_slice_in_dim(feature_rows, (tile ^ r) * depth, depth, axis=1) for r in range(4)
    ]

    def put_first(condition, one, other, axis):
        return jnp.concatenate(
            [jnp.where(condition, one, other), jnp.where(condition, other, one)], axis=axis
        )

    def both_heads(ours, theirs):
        return put_first(group == 0, ours, theirs, 1)

    choice = (at_end == first_core).astype(jnp.int32).reshape(1)

    def products(near, far, all_direct):
        return tuple(product_terms(choice, proj_weight, near, far, all_direct))

    rest = depth // 3

    def to_neighbour(block):
        return swapped(block, "head", 1)

    def over_middle(block):
        return swapped(block, "head", 3)

    def plus(block, *arrived):
        for other in arrived:
            block = block + other.astype(jnp.float32)
        return block

    def in_loop(chain, given, empty):
        return lax.fori_loop(0, once, lambda _, carry: chain(carry[0]), (given, empty))[1]

    def times_features(rows, parts):
        return sum(add_columns(parts[r], rows[r]) for r in range(4))

    def finish(total, part):
        finished = []
        for k in range(2):
            entries = total[:, k * width : (k + 1) * width].reshape(token_rows, layers, head_dim)
            entries = entries + bias_part[k, :, part][None]
            if part == 0:
                squares = jnp.mean(entries * entries, axis=-1, keepdims=True)
                entries = entries * lax.rsqrt(squares + eps_norm) * key_gain[None]
            finished.append(entries.reshape(token_rows, width).astype(jnp.bfloat16))
        return jnp.concatenate(finished, axis=1).reshape(tile_slots, shard_len, 2 * width)

    owner_tile, owner_turn, matched = routing(tile_map, tile_count, decode_owner, tile_slots, 4)
    turn_of = jnp.sum(jnp.where(matched, owner_turn[:, None, None], 0), axis=(0, 1))
    owned_by = (owner_tile[:, None] == (tile ^ jnp.arange(4))[None, :]).astype(jnp.float32)
    selector = jnp.einsum("rd,rjs->djs", owned_by, matched.astype(jnp.float32))
    selector = selector.astype(jnp.bfloat16).reshape(4 * most_tiles, tile_slots)

    turned = [turn_of // stride % 2 == 1 for stride in (1, 2)]

    def rolled(rows, shifted, stride):
        return jnp.where(turned[stride - 1][:, None, None], shifted, rows)

    def outgoing(rows):
        picked = add_columns(selector, rows.reshape(tile_slots, -1)).astype(jnp.bfloat16)
        picked = picked.reshape(4, most_tiles, shard_len, 2, layers, head_dim)
        return [picked[r] for r in range(4)]

    def to_owners(picked):
        return [picked[0]] + [swapped(picked[r], "tile", r) for r in (1, 2, 3)]

    def in_order(arrived):
        even = [jnp.where(first_core, arrived[r], arrived[r ^ 1]) for r in range(4)]
        ranked = [jnp.where(first_chip, even[r], even[r ^ 2]) for r in range(4)]
        return jnp.stack(ranked, axis=1)

    column, half = group * 2 * head_dim, kv_weight.shape[0] // 2

    def halves(weight, part):
        mine = lax.dynamic_slice_in_dim(weight, column + part * head_dim, head_dim, axis=1)
        ours = lax.dynamic_slice_in_dim(mine, tile // 2 * half, half, axis=0)
        return ours, lax.dynamic_slice_in_dim(mine, half - tile // 2 * half, half, axis=0)

    def to_planes(stays, comes):
        pieces = []
        for j in range(2):
            piece = jnp.where(tile // 2 == (head // 2) ^ j, stays, comes)
            pieces.append(
                moved(piece, lambda t, h: (t // 2 * 2 + outer_core(h), t % 2 + 2 * ((h // 2) ^ j)))
            )
        return pieces

    key_stays, key_leaves, rows_later = step((*halves(kv_weight, 0), kv_weight))
    bias_rows = moved(proj_bias, lambda t, h: (h, t))
    value_stays, value_leaves = halves(rows_later, 1)
    key_stays, key_comes, bias_rows, counts_later, value_stays, value_leaves = step(
        (
            key_stays,
            swapped(key_leaves, "tile", 2),
            bias_rows,
            tile_count,
            value_stays,
            value_leaves,
        )
    )

    once = jnp.minimum(jnp.max(counts_later), 1)

    tokens = jax.ShapeDtypeStruct((tile_slots, shard_len, 2 * width), jnp.bfloat16)
    shapes = term_shapes(depth, width, True) + [tokens, tokens]
    *no_terms, no_keys, no_values = blank_arrays(shapes)
    bias_part = add_columns(bias_rows[None], rows_later)
    key_pieces, value_stays, value_comes, bias_part, once = step(
        (
            to_planes(key_stays, key_comes),
            value_stays,
            swapped(value_leaves, "tile", 2),
            bias_part,
            once,
        )
    )

    key_half = jnp.concatenate(key_pieces, axis=1)
    value_pieces = to_planes(value_stays, value_comes)
    key_half, key_other, feature_parts = step(
        (key_half, swapped(key_half, "tile", 2), feature_parts)
    )

    key_near = step(put_first(first_chip, key_half, key_other, 0))
    terms = products(key_near, swapped(key_near, "tile", 1), False)
    bias_part = bias_part + swapped(bias_part, "tile", 1)
    terms, value_pieces, bias_part = step((terms, value_pieces, bias_part))
    value_half = jnp.concatenate(value_pieces, axis=1)

    def values_terms(given):
        value_half, bias_part = given
        other, bias_other = step((swapped(value_half, "tile", 2), swapped(bias_part, "tile", 2)))
        near = step(put_first(first_chip, value_half, other, 0))
        terms = products(near, swapped(near, "tile", 1), True)
        return (other, bias_other), (terms, bias_part + bias_other)

    empty = tuple(no_terms), bias_part
    own, second, mirror, first, kept_rest = terms
    second, mirror, first, (value_terms, bias_part) = step(
        (
            swapped(second, "head", 2),
            over_middle(mirror),
            to_neighbour(first),
            in_loop(values_terms, (value_half, bias_part), empty),
        )
    )
    bias_part = bias_part.reshape(2, layers, 2, head_dim)

    direct = 2 * rest
    arrived = jnp.concatenate([first[direct : 3 * rest], first[3 * rest :]], axis=1)
    pair = plus(kept_rest, arrived)
    pair = step(pair)
    mirrored = over_middle(pair[:, width:].astype(jnp.bfloat16))
    pair, mirrored, value_terms = step((pair, mirrored, value_terms))
    blocks = [plus(own, second, mirror, first[:direct]), plus(pair[:, :width], mirrored)]
    own = jnp.concatenate([block.astype(jnp.bfloat16) for block in blocks], axis=0)

    def rest_of_plane(given, part):
        own, across_x, across_y = given
        rows_0 = step(both_heads(own, across_y))
        middle = depth // 2
        upper, lower, rows_1 = step(
            (
                swapped(across_x[:middle], "groups", 1),
                swapped(across_y[middle:], "tile", 2),
                swapped(rows_0, "tile", 1),
            )
        )
        rows_2 = step(both_heads(across_x, jnp.concatenate([upper, lower], axis=0)))
        rows = [rows_0, rows_1, rows_2, swapped(rows_2, "tile", 1)]
        return finish(times_features(rows, feature_parts), part)

    def keys_product(own):
        across_x, across_y = step((swapped(own, "tile", 2), swapped(own, "groups", 1)))
        rows_0 = step(both_heads(own, across_y))
        diagonal, rows_1 = step((swapped(across_y, "tile", 2), swapped(rows_0, "tile", 1)))
        rows_2 = step(both_heads(across_x, diagonal))
        rows = [rows_0, rows_1, rows_2, swapped(rows_2, "tile", 1)]
        return across_x, finish(times_features(rows, feature_parts), 0)

    value_own, second, mirror, first = value_terms
    second, mirror, first, keys = step(
        (
            swapped(second, "head", 2),
            over_middle(mirror),
            to_neighbour(first),
            in_loop(keys_product, own, no_keys),
        )
    )
    own = plus(value_own, second, mirror, first).astype(jnp.bfloat16)

    shifted, across_x, across_y = step(
        (shifted_2(keys, "head", 1), swapped(own, "tile", 2), swapped(own, "groups", 1))
    )

    def values_product(given):
        own, across_x, across_y = given
        return (across_y, own, across_x), rest_of_plane(given, 1)

    keys = step(rolled(keys, shifted, 1))
    values = in_loop(values_product, (own, across_x, across_y), no_values)
    shifted, values = step((shifted_2(keys, "head", 2), values))

    picked = outgoing(rolled(keys, shifted, 2))
    values, shifted = step((values, shifted_2(values, "head", 1)))

    values = step(rolled(values, shifted, 1))
    arrived, shifted = step((to_owners(picked), shifted_2(values, "head", 2)))

    pieces = to_owners(outgoing(rolled(values, shifted, 2)))
    key_cache, pieces = step((in_order(arrived), pieces))
    cache = jnp.stack([key_cache, in_order(pieces)], axis=-2)
    return cache.reshape(1, 1, most_tiles * 4 * shard_len, 4 * layers, head_dim)


def solution(mesh):
    placed = (
        P("groups", "tile", None),
        P("tile", "head"),
        P("head"),
        P("tile", "head"),
        P(),
        P("groups", None),
        P("groups"),
        P("groups"),
    )
    sizes = tuple(mesh.shape[name] for name in ("groups", "tile", "head"))
    return jax.shard_map(
        product_plan if sizes == (2, 4, 4) else gather_plan,
        mesh=mesh,
        in_specs=placed,
        out_specs=P(("groups", "tile"), "head", None, None, None),
        check_vma=False,
    )
```

```python
import jax
import jax.numpy as jnp
from jax import lax
from jax.experimental import pallas as pl
from jax.experimental.pallas import tpu as pltpu
from jax.sharding import PartitionSpec as P

eps_norm = 1e-05


def shifted_2(shard, axis, by):
    count = lax.axis_size(axis)
    return lax.ppermute(shard, axis, [(i, (i + by) % count) for i in range(count)])


def swapped(shard, axis, bit):
    return lax.ppermute(shard, axis, [(i, i ^ bit) for i in range(lax.axis_size(axis))])


def add_columns(operand, portion):
    return jnp.dot(operand, portion, preferred_element_type=jnp.float32)


def routing(tile_map, tile_count, decode_owner, tile_slots, head_groups):
    most_tiles = tile_map.shape[1]
    owner_tile = decode_owner // head_groups
    owner_turn = decode_owner % head_groups
    usable = jnp.arange(most_tiles)[None, :] < tile_count[:, None]
    matched = (tile_map[:, :, None] == jnp.arange(tile_slots)[None, None, :]) & usable[:, :, None]
    return owner_tile, owner_turn, matched


def gather_plan(
    features, proj_weight, proj_bias, kv_weight, key_gain, tile_map, tile_count, decode_owner
):
    tile_slots, shard_len, feature_width = features.shape
    token_rows = tile_slots * shard_len
    feature_rows = features.reshape(token_rows, feature_width)
    weight_cols = lax.all_gather(proj_weight, "tile", axis=0, tiled=True)
    projected = jnp.dot(feature_rows, weight_cols, preferred_element_type=jnp.float32)
    projected_local = (projected + proj_bias.astype(jnp.float32)).astype(jnp.bfloat16)
    kv_width = kv_weight.shape[1]
    projected_all = lax.all_gather(projected_local, "head", axis=1, tiled=True)
    key_value = add_columns(projected_all, lax.all_gather(kv_weight, "tile", axis=0, tiled=True))
    layers, head_dim = key_gain.shape
    blocks = key_value.reshape(token_rows, -1, layers, 2, head_dim)
    keys_raw = blocks[:, :, :, 0]
    inv_rms = lax.rsqrt(jnp.mean(keys_raw * keys_raw, axis=-1, keepdims=True) + eps_norm)
    keys_normed = keys_raw * inv_rms * key_gain[None, None]
    stacked = jnp.stack([keys_normed, blocks[:, :, :, 1]], axis=3).astype(jnp.bfloat16)
    per_tile = stacked.reshape(tile_slots, shard_len * kv_width)
    tile_ranks = lax.axis_size("tile")
    head_groups = lax.axis_size("head")
    most_tiles = tile_map.shape[1]
    owner_tile, owner_turn, matched = routing(
        tile_map, tile_count, decode_owner, tile_slots, head_groups
    )
    owned_by = (owner_tile[:, None] == jnp.arange(tile_ranks)[None, :]).astype(jnp.float32)
    selector = jnp.einsum("rd,rjs->jds", owned_by, matched.astype(jnp.float32))
    selector = selector.astype(jnp.bfloat16).reshape(most_tiles * tile_ranks, tile_slots)
    outgoing = add_columns(selector, per_tile).astype(jnp.bfloat16)
    outgoing = outgoing.reshape(most_tiles, tile_ranks, shard_len, kv_width)
    arrived = lax.all_to_all(outgoing, "tile", split_axis=1, concat_axis=1, tiled=True)
    gathered_rows = arrived.reshape(
        most_tiles * tile_ranks * shard_len, kv_width // head_dim, head_dim
    )
    my_turn = jnp.sum(jnp.where(owner_tile == lax.axis_index("tile"), owner_turn, 0))
    stride = 1
    while stride < head_groups:
        shifted = shifted_2(gathered_rows, "head", stride)
        gathered_rows = jnp.where(my_turn // stride % 2 == 1, shifted, gathered_rows)
        stride = stride * 2
    return gathered_rows[None, None]


def terms_body(choice, weight, near, far, own, second, mirror, first, *kept_rest):
    near_product = add_columns(weight[...], near[...])
    far_product = add_columns(weight[...], far[...])
    near_kept = choice[0] == 1
    kept = jnp.where(near_kept, near_product, far_product)
    sent = jnp.where(near_kept, far_product, near_product)
    tall, width = weight.shape[0], own.shape[1]
    i = pl.program_id(0)
    rows = pl.ds(pl.multiple_of(i * tall, tall), tall)
    first[rows, :] = sent[:, :width].astype(first.dtype)

    def write_direct():
        own[rows, :] = kept[:, :width]
        second[rows, :] = sent[:, width:].astype(second.dtype)
        mirror[rows, :] = kept[:, width:].astype(mirror.dtype)

    if len(kept_rest) == 0:
        write_direct()
    else:
        pl.when(i < 2)(write_direct)

        @pl.when(i == 2)
        def _():
            kept_rest[0][...] = kept
            first[3 * tall :, :] = sent[:, width:].astype(first.dtype)


def term_shapes(depth, width, all_direct):
    direct, wide, narrow = depth if all_direct else depth // 3 * 2, jnp.float32, jnp.bfloat16
    shapes = [((direct, width), t) for t in (wide, narrow, narrow)]
    shapes = shapes + [((2 * depth - direct, width), narrow)]
    if not all_direct:
        shapes = shapes + [((depth // 3, 2 * width), wide)]
    return [jax.ShapeDtypeStruct(*shape) for shape in shapes]


def product_terms(choice, weight, near, far, all_direct):
    depth, rows = weight.shape
    columns = near.shape[1]
    tall = depth // 3
    shapes = term_shapes(depth, columns // 2, all_direct)
    whole = [pl.BlockSpec(array.shape, lambda i, choice: (0, 0)) for array in (near, *shapes)]
    return pl.pallas_call(
        terms_body,
        out_shape=shapes,
        grid_spec=pltpu.PrefetchScalarGridSpec(
            num_scalar_prefetch=1,
            grid=(3,),
            in_specs=[pl.BlockSpec((tall, rows), lambda i, choice: (i, 0)), whole[0], whole[0]],
            out_specs=whole[1:],
        ),
        compiler_params=pltpu.CompilerParams(vmem_limit_bytes=32 * 1024 * 1024),
        cost_estimate=pl.CostEstimate(
            flops=4 * depth * rows * columns,
            bytes_accessed=2 * depth * rows + 4 * rows * columns + 5 * depth * columns,
            transcendentals=0,
        ),
    )(choice, weight, near, far)


def blank_arrays(shapes):
    return pl.pallas_call(
        lambda *refs: None,
        out_shape=shapes,
        out_specs=[pl.BlockSpec(memory_space=pl.ANY)] * len(shapes),
    )()


def product_plan(
    features, proj_weight, proj_bias, kv_weight, key_gain, tile_map, tile_count, decode_owner
):
    tile_slots, shard_len, feature_width = features.shape
    token_rows = tile_slots * shard_len
    depth = proj_weight.shape[0]
    layers, head_dim = key_gain.shape
    width = layers * head_dim
    most_tiles = tile_map.shape[1]
    group, tile, head = (lax.axis_index(name) for name in ("groups", "tile", "head"))
    first_core, first_chip = tile % 2 == 0, tile < 2
    at_end = (head == 0) | (head == 3)
    feature_rows = features.reshape(token_rows, feature_width)
    step = lax.optimization_barrier

    def moved(shard, target):
        pairs = []
        for t in range(4):
            for h in range(4):
                to_tile, to_head = target(t, h)
                pairs.append((t * 4 + h, to_tile * 4 + to_head))
        return lax.ppermute(shard, ("tile", "head"), pairs)

    def outer_core(h):
        return (h ^ h // 2) % 2

    feature_parts = [
        lax.dynamic_slice_in_dim(feature_rows, (tile ^ r) * depth, depth, axis=1) for r in range(4)
    ]

    def put_first(condition, one, other, axis):
        return jnp.concatenate(
            [jnp.where(condition, one, other), jnp.where(condition, other, one)], axis=axis
        )

    def both_heads(ours, theirs):
        return put_first(group == 0, ours, theirs, 1)

    choice = (at_end == first_core).astype(jnp.int32).reshape(1)

    def products(near, far, all_direct):
        return tuple(product_terms(choice, proj_weight, near, far, all_direct))

    rest = depth // 3

    def to_neighbour(block):
        return swapped(block, "head", 1)

    def over_middle(block):
        return swapped(block, "head", 3)

    def plus(block, *arrived):
        for other in arrived:
            block = block + other.astype(jnp.float32)
        return block

    def in_loop(chain, given, empty):
        return lax.fori_loop(0, once, lambda _, carry: chain(carry[0]), (given, empty))[1]

    def times_features(rows, parts):
        return sum(add_columns(parts[r], rows[r]) for r in range(4))

    def finish(total, part):
        finished = []
        for k in range(2):
            entries = total[:, k * width : (k + 1) * width].reshape(token_rows, layers, head_dim)
            entries = entries + bias_part[k, :, part][None]
            if part == 0:
                squares = jnp.mean(entries * entries, axis=-1, keepdims=True)
                entries = entries * lax.rsqrt(squares + eps_norm) * key_gain[None]
            finished.append(entries.reshape(token_rows, width).astype(jnp.bfloat16))
        return jnp.concatenate(finished, axis=1).reshape(tile_slots, shard_len, 2 * width)

    owner_tile, owner_turn, matched = routing(tile_map, tile_count, decode_owner, tile_slots, 4)
    turn_of = jnp.sum(jnp.where(matched, owner_turn[:, None, None], 0), axis=(0, 1))
    owned_by = (owner_tile[:, None] == (tile ^ jnp.arange(4))[None, :]).astype(jnp.float32)
    selector = jnp.einsum("rd,rjs->djs", owned_by, matched.astype(jnp.float32))
    selector = selector.astype(jnp.bfloat16).reshape(4 * most_tiles, tile_slots)

    turned = [turn_of // stride % 2 == 1 for stride in (1, 2)]

    def rolled(rows, shifted, stride):
        return jnp.where(turned[stride - 1][:, None, None], shifted, rows)

    def outgoing(rows):
        picked = add_columns(selector, rows.reshape(tile_slots, -1)).astype(jnp.bfloat16)
        picked = picked.reshape(4, most_tiles, shard_len, 2, layers, head_dim)
        return [picked[r] for r in range(4)]

    def to_owners(picked):
        return [picked[0]] + [swapped(picked[r], "tile", r) for r in (1, 2, 3)]

    def in_order(arrived):
        even = [jnp.where(first_core, arrived[r], arrived[r ^ 1]) for r in range(4)]
        ranked = [jnp.where(first_chip, even[r], even[r ^ 2]) for r in range(4)]
        return jnp.stack(ranked, axis=1)

    column, half = group * 2 * head_dim, kv_weight.shape[0] // 2

    def halves(weight, part):
        mine = lax.dynamic_slice_in_dim(weight, column + part * head_dim, head_dim, axis=1)
        ours = lax.dynamic_slice_in_dim(mine, tile // 2 * half, half, axis=0)
        return ours, lax.dynamic_slice_in_dim(mine, half - tile // 2 * half, half, axis=0)

    def to_planes(stays, comes):
        pieces = []
        for j in (1, 0):
            piece = jnp.where(tile // 2 == (head // 2) ^ j, stays, comes)
            pieces.append(
                moved(piece, lambda t, h: (t // 2 * 2 + outer_core(h), t % 2 + 2 * ((h // 2) ^ j)))
            )
        return pieces[::-1]

    key_stays, key_leaves, rows_later = step((*halves(kv_weight, 0), kv_weight))
    bias_rows = moved(proj_bias, lambda t, h: (h, t))
    value_stays, value_leaves = halves(rows_later, 1)
    key_stays, key_comes, bias_rows, counts_later, value_stays, value_leaves = step(
        (
            key_stays,
            swapped(key_leaves, "tile", 2),
            bias_rows,
            tile_count,
            value_stays,
            value_leaves,
        )
    )

    once = jnp.minimum(jnp.max(counts_later), 1)

    tokens = jax.ShapeDtypeStruct((tile_slots, shard_len, 2 * width), jnp.bfloat16)
    shapes = term_shapes(depth, width, True) + [tokens, tokens]
    *no_terms, no_keys, no_values = blank_arrays(shapes)
    bias_part = add_columns(bias_rows[None], rows_later)
    key_pieces, value_stays, value_comes, bias_part, once = step(
        (
            to_planes(key_stays, key_comes),
            value_stays,
            swapped(value_leaves, "tile", 2),
            bias_part,
            once,
        )
    )

    key_half = jnp.concatenate(key_pieces, axis=1)
    value_pieces = to_planes(value_stays, value_comes)
    key_half, key_other, feature_parts = step(
        (key_half, swapped(key_half, "tile", 2), feature_parts)
    )

    key_near = step(put_first(first_chip, key_half, key_other, 0))
    terms = products(key_near, swapped(key_near, "tile", 1), False)
    bias_part = bias_part + swapped(bias_part, "tile", 1)
    terms, value_pieces, bias_part = step((terms, value_pieces, bias_part))
    value_half = jnp.concatenate(value_pieces, axis=1)

    def values_terms(given):
        value_half, bias_part = given
        other, bias_other = step((swapped(value_half, "tile", 2), swapped(bias_part, "tile", 2)))
        near = step(put_first(first_chip, value_half, other, 0))
        terms = products(near, swapped(near, "tile", 1), True)
        return (other, bias_other), (terms, bias_part + bias_other)

    empty = tuple(no_terms), bias_part
    own, second, mirror, first, kept_rest = terms
    second, mirror, first, (value_terms, bias_part) = step(
        (
            swapped(second, "head", 2),
            over_middle(mirror),
            to_neighbour(first),
            in_loop(values_terms, (value_half, bias_part), empty),
        )
    )
    bias_part = bias_part.reshape(2, layers, 2, head_dim)

    direct = 2 * rest
    arrived = jnp.concatenate([first[direct : 3 * rest], first[3 * rest :]], axis=1)
    pair = plus(kept_rest, arrived)
    pair = step(pair)
    mirrored = over_middle(pair[:, width:].astype(jnp.bfloat16))
    pair, mirrored, value_terms = step((pair, mirrored, value_terms))
    blocks = [plus(own, second, mirror, first[:direct]), plus(pair[:, :width], mirrored)]
    own = jnp.concatenate([block.astype(jnp.bfloat16) for block in blocks], axis=0)

    def rest_of_plane(given, part):
        own, across_x, across_y = given
        rows_0 = step(both_heads(own, across_y))
        middle = depth // 2
        upper, lower, rows_1 = step(
            (
                swapped(across_x[:middle], "groups", 1),
                swapped(across_y[middle:], "tile", 2),
                swapped(rows_0, "tile", 1),
            )
        )
        rows_2 = step(both_heads(across_x, jnp.concatenate([upper, lower], axis=0)))
        rows = [rows_0, rows_1, rows_2, swapped(rows_2, "tile", 1)]
        return finish(times_features(rows, feature_parts), part)

    def keys_product(own):
        across_x, across_y = step((swapped(own, "tile", 2), swapped(own, "groups", 1)))
        rows_0 = step(both_heads(own, across_y))
        diagonal, rows_1 = step((swapped(across_y, "tile", 2), swapped(rows_0, "tile", 1)))
        rows_2 = step(both_heads(across_x, diagonal))
        rows = [rows_0, rows_1, rows_2, swapped(rows_2, "tile", 1)]
        return across_x, finish(times_features(rows, feature_parts), 0)

    value_own, second, mirror, first = value_terms
    second, mirror, first, keys = step(
        (
            swapped(second, "head", 2),
            over_middle(mirror),
            to_neighbour(first),
            in_loop(keys_product, own, no_keys),
        )
    )
    own = plus(value_own, second, mirror, first).astype(jnp.bfloat16)

    shifted, across_x, across_y = step(
        (shifted_2(keys, "head", 1), swapped(own, "tile", 2), swapped(own, "groups", 1))
    )

    def values_product(given):
        own, across_x, across_y = given
        return (across_y, own, across_x), rest_of_plane(given, 1)

    keys = step(rolled(keys, shifted, 1))
    values = in_loop(values_product, (own, across_x, across_y), no_values)
    shifted, values = step((shifted_2(keys, "head", 2), values))

    picked = outgoing(rolled(keys, shifted, 2))
    values, shifted = step((values, shifted_2(values, "head", 1)))

    values = step(rolled(values, shifted, 1))
    arrived, shifted = step((to_owners(picked), shifted_2(values, "head", 2)))

    pieces = to_owners(outgoing(rolled(values, shifted, 2)))
    key_cache, pieces = step((in_order(arrived), pieces))
    cache = jnp.stack([key_cache, in_order(pieces)], axis=-2)
    return cache.reshape(1, 1, most_tiles * 4 * shard_len, 4 * layers, head_dim)


def solution(mesh):
    placed = (
        P("groups", "tile", None),
        P("tile", "head"),
        P("head"),
        P("tile", "head"),
        P(),
        P("groups", None),
        P("groups"),
        P("groups"),
    )
    sizes = tuple(mesh.shape[name] for name in ("groups", "tile", "head"))
    return jax.shard_map(
        product_plan if sizes == (2, 4, 4) else gather_plan,
        mesh=mesh,
        in_specs=placed,
        out_specs=P(("groups", "tile"), "head", None, None, None),
        check_vma=False,
    )
```
